32 devices in a mesh: wide: 16 (over z, y, x), narrow: 2 (over core).
Axes of the slice: x: 2, y: 2, z: 4, core: 2. Of those that a mesh axis runs over, the one named last changes fastest.
Arguments:
- tokens: bfloat16 [65536, 768], P(('wide', 'narrow')), may hold values from -6 to 6
- cotangent: bfloat16 [65536, 768], P(('wide', 'narrow')), may hold values from -6 to 6
- size_tags: int32 [16], P('wide'), may hold values from 1024 to 4096, as said below
- timesteps: int32 [64], P(('wide', 'narrow')), may hold values from 0 to 999, as said below
- labels: int32 [64], P(('wide', 'narrow')), may hold values from 0 to 999, as said below
- modulator: bfloat16 [768, 4608], replicated, may hold values from -0.21875 to 0.21875
- class_table: bfloat16 [768, 1000], replicated, may hold values from -6 to 6
- mix_kernel: bfloat16 [768, 9], replicated, may hold values from -2 to 2
- heads_in: bfloat16 [768, 2304], P(None, 'narrow'), may hold values from -0.21875 to 0.21875
- heads_out: bfloat16 [768, 768], P('narrow'), may hold values from -1.25 to 1.25
- up_weight: bfloat16 [768, 3072], P(None, 'narrow'), may hold values from -0.21875 to 0.21875
- hidden_kernel: bfloat16 [3072, 9], P('narrow'), may hold values from -2 to 2
- down_weight: bfloat16 [3072, 768], P('narrow'), may hold values from -0.109375 to 0.109375
- modulator_master: float32 [768, 4608], P(('wide', 'narrow')), may hold values from -0.21875 to 0.21875
- modulator_first: float32 [768, 4608], P(('wide', 'narrow')), may hold values from -6 to 6
- modulator_second: float32 [768, 4608], P(('wide', 'narrow')), may hold values from 1 to 4
- class_table_master: float32 [768, 1000], P(('wide', 'narrow')), may hold values from -6 to 6
- class_table_first: float32 [768, 1000], P(('wide', 'narrow')), may hold values from -0.625 to 0.625
- class_table_second: float32 [768, 1000], P(('wide', 'narrow')), may hold values from 0.05 to 0.2
- mix_kernel_master: float32 [768, 9], P(('wide', 'narrow')), may hold values from -2 to 2
- mix_kernel_first: float32 [768, 9], P(('wide', 'narrow')), may hold values from -6 to 6
- mix_kernel_second: float32 [768, 9], P(('wide', 'narrow')), may hold values from 1 to 4
- heads_in_master: float32 [768, 2304], P('wide', 'narrow'), may hold values from -0.21875 to 0.21875
- heads_in_first: float32 [768, 2304], P('wide', 'narrow'), may hold values from -6 to 6
- heads_in_second: float32 [768, 2304], P('wide', 'narrow'), may hold values from 1 to 4
- heads_out_master: float32 [768, 768], P(('narrow', 'wide')), may hold values from -1.25 to 1.25
- heads_out_first: float32 [768, 768], P(('narrow', 'wide')), may hold values from -6 to 6
- heads_out_second: float32 [768, 768], P(('narrow', 'wide')), may hold values from 1 to 4
- up_weight_master: float32 [768, 3072], P('wide', 'narrow'), may hold values from -0.21875 to 0.21875
- up_weight_first: float32 [768, 3072], P('wide', 'narrow'), may hold values from -6 to 6
- up_weight_second: float32 [768, 3072], P('wide', 'narrow'), may hold values from 0.1 to 0.4
- hidden_kernel_master: float32 [3072, 9], P(('narrow', 'wide')), may hold values from -2 to 2
- hidden_kernel_first: float32 [3072, 9], P(('narrow', 'wide')), may hold values from -6 to 6
- hidden_kernel_second: float32 [3072, 9], P(('narrow', 'wide')), may hold values from 0.05 to 0.2
- down_weight_master: float32 [3072, 768], P(('narrow', 'wide')), may hold values from -0.109375 to 0.109375
- down_weight_first: float32 [3072, 768], P(('narrow', 'wide')), may hold values from -6 to 6
- down_weight_second: float32 [3072, 768], P(('narrow', 'wide')), may hold values from 1 to 4
Outputs:
- output: bfloat16 [65536, 768], P(('wide', 'narrow'))
- input_grad: bfloat16 [65536, 768], P(('wide', 'narrow'))
- grad_norm: float32 [], replicated
- modulator_first_new: float32 [768, 4608], P(('wide', 'narrow'))
- modulator_second_new: float32 [768, 4608], P(('wide', 'narrow'))
- modulator_master_new: float32 [768, 4608], P(('wide', 'narrow'))
- modulator_copy: bfloat16 [768, 4608], P(('wide', 'narrow'))
- class_table_first_new: float32 [768, 1000], P(('wide', 'narrow'))
- class_table_second_new: float32 [768, 1000], P(('wide', 'narrow'))
- class_table_master_new: float32 [768, 1000], P(('wide', 'narrow'))
- class_table_copy: bfloat16 [768, 1000], P(('wide', 'narrow'))
- mix_kernel_first_new: float32 [768, 9], P(('wide', 'narrow'))
- mix_kernel_second_new: float32 [768, 9], P(('wide', 'narrow'))
- mix_kernel_master_new: float32 [768, 9], P(('wide', 'narrow'))
- mix_kernel_copy: bfloat16 [768, 9], P(('wide', 'narrow'))
- heads_in_first_new: float32 [768, 2304], P('wide', 'narrow')
- heads_in_second_new: float32 [768, 2304], P('wide', 'narrow')
- heads_in_master_new: float32 [768, 2304], P('wide', 'narrow')
- heads_in_copy: bfloat16 [768, 2304], P('wide', 'narrow')
- heads_out_first_new: float32 [768, 768], P(('narrow', 'wide'))
- heads_out_second_new: float32 [768, 768], P(('narrow', 'wide'))
- heads_out_master_new: float32 [768, 768], P(('narrow', 'wide'))
- heads_out_copy: bfloat16 [768, 768], P(('narrow', 'wide'))
- up_weight_first_new: float32 [768, 3072], P('wide', 'narrow')
- up_weight_second_new: float32 [768, 3072], P('wide', 'narrow')
- up_weight_master_new: float32 [768, 3072], P('wide', 'narrow')
- up_weight_copy: bfloat16 [768, 3072], P('wide', 'narrow')
- hidden_kernel_first_new: float32 [3072, 9], P(('narrow', 'wide'))
- hidden_kernel_second_new: float32 [3072, 9], P(('narrow', 'wide'))
- hidden_kernel_master_new: float32 [3072, 9], P(('narrow', 'wide'))
- hidden_kernel_copy: bfloat16 [3072, 9], P(('narrow', 'wide'))
- down_weight_first_new: float32 [3072, 768], P(('narrow', 'wide'))
- down_weight_second_new: float32 [3072, 768], P(('narrow', 'wide'))
- down_weight_master_new: float32 [3072, 768], P(('narrow', 'wide'))
- down_weight_copy: bfloat16 [3072, 768], P(('narrow', 'wide'))
- modulation_two_grad: float32 [64, 1536], P(('wide', 'narrow'))
The draws below stay inside these ranges and needn't reach their ends.
Inputs may be any that keep to these rules, and one draw needn't show every extreme that they name: `size_tags`: each tag is 1024 or 4096; both occur in every draw. `timesteps`: the four frames of a quad tagged 4 * 32 * 32 carry the same timestep. `labels`: the four frames of a quad tagged 4 * 32 * 32 carry the same label.
All inputs are finite; a program needn't handle non-finite values.
Results may differ from the reference program's by a relative error of at most 0.03.
Values may be sent and summed in bfloat16 or wider, within the bound.
A program may use at most 576 MiB of HBM per device.

```python
import math
import jax
import jax.numpy as jnp
from jax import lax

D = 768
HS = 64
FF = 3072
NCLS = 1000
SIDE = 32
STEP = 10
QUADS = 16
FRAMES = 64
TOKENS = 65536
PARAMS = 11419392


def long_quads(key):
    base_key = jax.random.fold_in(key, 11)
    coin_flags = jax.random.randint(base_key, (QUADS,), 0, 5) < 3
    shuffled = jax.random.permutation(jax.random.fold_in(base_key, 1), QUADS)
    return coin_flags.at[shuffled[0]].set(True).at[shuffled[1]].set(False)


def draw_size_tags(key, part):
    return jnp.where(long_quads(key), 4 * SIDE * SIDE, SIDE * SIDE).astype(jnp.int32)


def frame_values(key, salt_value, upper_bound):
    drawn_values = jax.random.randint(jax.random.fold_in(key, salt_value), (QUADS, 4), 0, upper_bound)
    shared = jnp.where(long_quads(key)[:, None], drawn_values[:, :1], drawn_values)
    return shared.reshape(FRAMES).astype(jnp.int32)


def draw_timesteps(key, part):
    return frame_values(key, 23, 1000)


def draw_labels(key, part):
    return frame_values(key, 29, NCLS)


def levels(key, dims, cuts, smallest, largest):
    def one(axis_at, shards_of):
        heights = jax.random.uniform(jax.random.fold_in(jax.random.fold_in(key, 6), axis_at), (shards_of,), jnp.float32, smallest / len(cuts), largest / len(cuts))
        return jnp.repeat(jnp.exp(heights), dims[axis_at] // shards_of).reshape((-1,) + (1,) * (len(dims) - axis_at - 1))

    loudness = one(*cuts[0])
    for cut in cuts[1:]:
        loudness = loudness * one(*cut)
    return loudness


def centred(rng, extent, deviation, most, shards=(), held_as=jnp.bfloat16):
    drawn = jax.random.normal(rng, extent, jnp.float32) * deviation
    if len(shards) > 0:
        drawn = levels(rng, extent, shards, -0.22, 0.18) * drawn
    return jnp.clip(drawn, min=-most, max=most).astype(held_as)


def setup_inputs(seed: int = 0) -> dict:
    streams_of = jax.random.split(jax.random.key(seed), 38)
    return {
        "tokens": centred(streams_of[0], (TOKENS, D), 1.0, 6.0, ((0, 32),)),
        "cotangent": centred(streams_of[1], (TOKENS, D), 1.0, 6.0, ((0, 32),)),
        "size_tags": draw_size_tags(jax.random.fold_in(streams_of[37], 71), 0),
        "timesteps": draw_timesteps(jax.random.fold_in(streams_of[37], 71), 0),
        "labels": draw_labels(jax.random.fold_in(streams_of[37], 71), 0),
        "modulator": centred(streams_of[5], (D, 6 * D), D ** -0.5, 0.21875),
        "class_table": centred(streams_of[6], (D, NCLS), 1.0, 6.0),
        "mix_kernel": centred(streams_of[7], (D, 9), 9 ** -0.5, 2.0),
        "heads_in": centred(streams_of[8], (D, 3 * D), D ** -0.5, 0.21875, ((1, 2),)),
        "heads_out": centred(streams_of[9], (D, D), (D // 32) ** -0.5, 1.25, ((0, 2),)),
        "up_weight": centred(streams_of[10], (D, FF), D ** -0.5, 0.21875, ((1, 2),)),
        "hidden_kernel": centred(streams_of[11], (FF, 9), 9 ** -0.5, 2.0, ((0, 2),)),
        "down_weight": centred(streams_of[12], (FF, D), FF ** -0.5, 0.109375, ((0, 2),)),
        "modulator_master": centred(streams_of[13], (D, 6 * D), D ** -0.5, 0.21875, ((0, 32),), jnp.float32),
        "modulator_first": centred(streams_of[14], (D, 6 * D), 1.0, 6.0, ((0, 32),), jnp.float32),
        "modulator_second": jnp.clip(jnp.exp(math.log(4.0) - 1.3862944 * jax.random.uniform(streams_of[15], (D, 6 * D), jnp.float32) ** levels(streams_of[15], (D, 6 * D), ((0, 32),), -0.2, 0.2)), 1.0, 4.0),
        "class_table_master": centred(streams_of[16], (D, NCLS), 1.0, 6.0, ((0, 32),), jnp.float32),
        "class_table_first": centred(streams_of[17], (D, NCLS), 0.1, 0.625, ((0, 32),), jnp.float32),
        "class_table_second": jnp.clip(jnp.exp(math.log(0.2) - 1.3862944 * jax.random.uniform(streams_of[18], (D, NCLS), jnp.float32) ** levels(streams_of[18], (D, NCLS), ((0, 32),), -0.2, 0.2)), 0.05, 0.2),
        "mix_kernel_master": centred(streams_of[19], (D, 9), 9 ** -0.5, 2.0, ((0, 32),), jnp.float32),
        "mix_kernel_first": centred(streams_of[20], (D, 9), 1.0, 6.0, ((0, 32),), jnp.float32),
        "mix_kernel_second": jnp.clip(jnp.exp(math.log(4.0) - 1.3862944 * jax.random.uniform(streams_of[21], (D, 9), jnp.float32) ** levels(streams_of[21], (D, 9), ((0, 32),), -0.2, 0.2)), 1.0, 4.0),
        "heads_in_master": centred(streams_of[22], (D, 3 * D), D ** -0.5, 0.21875, ((0, 16), (1, 2)), jnp.float32),
        "heads_in_first": centred(streams_of[23], (D, 3 * D), 1.0, 6.0, ((0, 16), (1, 2)), jnp.float32),
        "heads_in_second": jnp.clip(jnp.exp(math.log(4.0) - 1.3862944 * jax.random.uniform(streams_of[24], (D, 3 * D), jnp.float32) ** levels(streams_of[24], (D, 3 * D), ((0, 16), (1, 2)), -0.2, 0.2)), 1.0, 4.0),
        "heads_out_master": centred(streams_of[25], (D, D), (D // 32) ** -0.5, 1.25, ((0, 32),), jnp.float32),
        "heads_out_first": centred(streams_of[26], (D, D), 1.0, 6.0, ((0, 32),), jnp.float32),
        "heads_out_second": jnp.clip(jnp.exp(math.log(4.0) - 1.3862944 * jax.random.uniform(streams_of[27], (D, D), jnp.float32) ** levels(streams_of[27], (D, D), ((0, 32),), -0.2, 0.2)), 1.0, 4.0),
        "up_weight_master": centred(streams_of[28], (D, FF), D ** -0.5, 0.21875, ((0, 16), (1, 2)), jnp.float32),
        "up_weight_first": centred(streams_of[29], (D, FF), 1.0, 6.0, ((0, 16), (1, 2)), jnp.float32),
        "up_weight_second": jnp.clip(jnp.exp(math.log(0.4) - 1.3862944 * jax.random.uniform(streams_of[30], (D, FF), jnp.float32) ** levels(streams_of[30], (D, FF), ((0, 16), (1, 2)), -0.2, 0.2)), 0.1, 0.4),
        "hidden_kernel_master": centred(streams_of[31], (FF, 9), 9 ** -0.5, 2.0, ((0, 32),), jnp.float32),
        "hidden_kernel_first": centred(streams_of[32], (FF, 9), 1.0, 6.0, ((0, 32),), jnp.float32),
        "hidden_kernel_second": jnp.clip(jnp.exp(math.log(0.2) - 1.3862944 * jax.random.uniform(streams_of[33], (FF, 9), jnp.float32) ** levels(streams_of[33], (FF, 9), ((0, 32),), -0.2, 0.2)), 0.05, 0.2),
        "down_weight_master": centred(streams_of[34], (FF, D), FF ** -0.5, 0.109375, ((0, 32),), jnp.float32),
        "down_weight_first": centred(streams_of[35], (FF, D), 1.0, 6.0, ((0, 32),), jnp.float32),
        "down_weight_second": jnp.clip(jnp.exp(math.log(4.0) - 1.3862944 * jax.random.uniform(streams_of[36], (FF, D), jnp.float32) ** levels(streams_of[36], (FF, D), ((0, 32),), -0.2, 0.2)), 1.0, 4.0),
    }


@jax.custom_vjp
def low(v):
    return lax.optimization_barrier(v.astype(jnp.bfloat16)).astype(jnp.float32)

@jax.custom_vjp
def low_back(v):
    return v

def low_keep(v):
    return (low(v), None)

def low_pass(kept, grad):
    return (grad,)

def back_keep(v):
    return (v, None)

def back_low(kept, grad):
    return (low(grad),)
low.defvjp(low_keep, low_pass)
low_back.defvjp(back_keep, back_low)
NORM_EPS = 1e-06
BETA_ONE = 0.5
BETA_TWO = 0.5
ADAM_EPS = 1e-08
WEIGHT_DECAY = 0.01
HIGHEST_PRECISION = lax.Precision.HIGHEST

def matmul(left, right):
    return jnp.dot(left, right, precision=HIGHEST_PRECISION, preferred_element_type=jnp.float32)

def timestep_code(stamps):
    half_dim = D // 2
    scales = jnp.exp(-jnp.log(10000.0) * jnp.arange(half_dim, dtype=jnp.float32) / half_dim)
    angles = stamps.astype(jnp.float32)[:, None] * scales[None, :]
    return jnp.concatenate([jnp.cos(angles), jnp.sin(angles)], axis=1)

def layer_norm(fields):
    center = fields - lax.optimization_barrier(jnp.mean(fields, -1, keepdims=True))
    return center * lax.rsqrt(lax.optimization_barrier(jnp.mean(center * center, -1, keepdims=True)) + NORM_EPS)

def conv_image(images, kernel):
    padded = jnp.pad(images, ((0, 0), (1, 1), (1, 1), (0, 0)))
    row_count, col_count = (images.shape[1], images.shape[2])
    result = jnp.zeros_like(images)
    for offset in range(9):
        result = result + padded[:, offset // 3:offset // 3 + row_count, offset % 3:offset % 3 + col_count, :] * kernel[:, offset]
    return result

def quad_conv(fields, kernel, is_big):
    channels = fields.shape[-1]

    def large_case(inputs):
        return conv_image(inputs.reshape(1, 2 * SIDE, 2 * SIDE, channels), kernel).reshape(inputs.shape)

    def small_case(inputs):
        return conv_image(inputs.reshape(4, SIDE, SIDE, channels), kernel).reshape(inputs.shape)
    return lax.cond(is_big, large_case, small_case, fields)

def to_groups(fields, is_big):
    channels = fields.shape[-1]
    half_side = SIDE // 2

    def large_case(inputs):
        return inputs.reshape(SIDE, 2, SIDE, 2, channels).transpose(1, 3, 0, 2, 4).reshape(4, SIDE * SIDE, channels)

    def small_case(inputs):
        return inputs.reshape(4, half_side, 2, half_side, 2, channels).transpose(2, 4, 0, 1, 3, 5).reshape(4, SIDE * SIDE, channels)
    return lax.cond(is_big, large_case, small_case, fields)

def from_groups(blocks, is_big):
    channels = blocks.shape[-1]
    half_side = SIDE // 2

    def large_case(inputs):
        return inputs.reshape(2, 2, SIDE, SIDE, channels).transpose(2, 0, 3, 1, 4).reshape(-1, channels)

    def small_case(inputs):
        return inputs.reshape(2, 2, 4, half_side, half_side, channels).transpose(2, 3, 0, 4, 1, 5).reshape(-1, channels)
    return lax.cond(is_big, large_case, small_case, blocks)

def attend(queries, key_rows, values):
    scores = low_back(jnp.einsum('blhe,bmhe->bhlm', queries, key_rows, precision=HIGHEST_PRECISION) * HS ** (-0.5))
    highest = lax.optimization_barrier(jnp.max(scores, -1, keepdims=True))
    weights = jnp.exp(scores - highest)
    shares = low(weights / lax.optimization_barrier(jnp.sum(weights, -1, keepdims=True)))
    return jnp.einsum('bhlm,bmhe->blhe', shares, values, precision=HIGHEST_PRECISION)

def group_step(operands):
    group_rows, is_big = operands
    row_count = group_rows.shape[0]
    divided = group_rows.reshape(row_count, -1, 3, HS)
    head_count = divided.shape[1]

    def branch(pieces):

        def run_branch(members):
            shaped = [member.reshape(pieces, row_count // pieces, head_count, HS) for member in members]
            return attend(shaped[0], shaped[1], shaped[2]).reshape(row_count, head_count * HS)
        return run_branch
    return lax.cond(is_big, branch(1), branch(4), (divided[:, :, 0], divided[:, :, 1], divided[:, :, 2]))

def quad_forward(fields, offsets, is_big, stamps, classes, params):
    modulator, class_table, mix_kernel, heads_in, heads_out, up_weight, hidden_kernel, down_weight = params
    embedded = timestep_code(stamps) + class_table[:, classes].T
    cond_low = low(jax.nn.silu(embedded))
    modulation = low_back(matmul(cond_low, modulator)).reshape(4, 6, 1, D) + offsets[:, :, None, :]
    frames = fields.reshape(4, SIDE * SIDE, D)
    norm_one = low((layer_norm(frames) * (1.0 + modulation[:, 1]) + modulation[:, 0]).reshape(-1, D))
    mixture = low(quad_conv(norm_one, mix_kernel, is_big))
    triples = low_back(low(matmul(mixture, heads_in)))
    grouped = to_groups(triples, is_big)
    attended = lax.map(jax.checkpoint(group_step), (grouped, jnp.broadcast_to(is_big, (4,))))
    attended = low_back(low(from_groups(attended, is_big)))
    attn_out = low_back(matmul(attended, heads_out)).reshape(4, -1, D)
    residual = frames + modulation[:, 2] * attn_out
    norm_two = low((layer_norm(residual) * (1.0 + modulation[:, 4]) + modulation[:, 3]).reshape(-1, D))
    hidden = low_back(matmul(norm_two, up_weight))
    activated = low(jax.nn.gelu(quad_conv(hidden, hidden_kernel, is_big)))
    ffn_out = low_back(matmul(activated, down_weight)).reshape(4, -1, D)
    return (residual + modulation[:, 5] * ffn_out).reshape(-1, D)

def adamw_update(gradient, master, first_old, second, step_rate, factor):
    scaled = gradient * factor
    first_new = BETA_ONE * first_old + (1.0 - BETA_ONE) * scaled
    second_new = BETA_TWO * second + (1.0 - BETA_TWO) * scaled * scaled
    step_ratio = first_new / (1.0 - BETA_ONE ** STEP) / (jnp.sqrt(second_new / (1.0 - BETA_TWO ** STEP)) + ADAM_EPS)
    master_new = master - step_rate * (step_ratio + WEIGHT_DECAY * master)
    return (first_new, second_new, master_new, master_new.astype(jnp.bfloat16))

def reference(tokens, cotangent, size_tags, timesteps, labels, modulator, class_table, mix_kernel, heads_in, heads_out, up_weight, hidden_kernel, down_weight, modulator_master, modulator_first, modulator_second, class_table_master, class_table_first, class_table_second, mix_kernel_master, mix_kernel_first, mix_kernel_second, heads_in_master, heads_in_first, heads_in_second, heads_out_master, heads_out_first, heads_out_second, up_weight_master, up_weight_first, up_weight_second, hidden_kernel_master, hidden_kernel_first, hidden_kernel_second, down_weight_master, down_weight_first, down_weight_second):
    params = tuple((weight_in.astype(jnp.float32) for weight_in in (modulator, class_table, mix_kernel, heads_in, heads_out, up_weight, hidden_kernel, down_weight)))
    quad_len = 4 * SIDE * SIDE
    sequence = (tokens.reshape(QUADS, quad_len, D), cotangent.reshape(QUADS, quad_len, D), size_tags, timesteps.reshape(QUADS, 4), labels.reshape(QUADS, 4))

    def visit_quad(totals, entries):
        fields, grads_out, size_tag, stamps, classes = entries
        is_big = size_tag > SIDE * SIDE

        def forward(inputs, offsets, weights):
            return quad_forward(inputs, offsets, is_big, stamps, classes, weights)
        zero_offsets = jnp.zeros((4, 6, D), jnp.float32)
        result, pullback = jax.vjp(forward, fields.astype(jnp.float32), zero_offsets, params)
        grad_in, grad_offsets, grad_params = pullback(grads_out.astype(jnp.float32))
        second_mod = grad_offsets[:, 3:5].reshape(4, 2 * D)
        return (jax.tree.map(jnp.add, totals, grad_params), (result.astype(jnp.bfloat16), grad_in.astype(jnp.bfloat16), second_mod))
    zero_grads = tuple((jnp.zeros_like(weight_in) for weight_in in params))
    grads_all, (outputs, input_grads, second_mods) = lax.scan(visit_quad, zero_grads, sequence)
    total_square = jnp.float32(0.0)
    for gradient in grads_all:
        total_square = total_square + jnp.sum(gradient * gradient)
    grad_norm = jnp.sqrt(total_square)
    clip_limit = PARAMS ** 0.5
    factor = clip_limit / jnp.maximum(grad_norm, clip_limit)
    step_rates = (D ** (-0.5), 1.0, 1.0 / 3.0, D ** (-0.5), (D // 32) ** (-0.5), D ** (-0.5), 1.0 / 3.0, FF ** (-0.5))
    states = ((modulator_master, modulator_first, modulator_second), (class_table_master, class_table_first, class_table_second), (mix_kernel_master, mix_kernel_first, mix_kernel_second), (heads_in_master, heads_in_first, heads_in_second), (heads_out_master, heads_out_first, heads_out_second), (up_weight_master, up_weight_first, up_weight_second), (hidden_kernel_master, hidden_kernel_first, hidden_kernel_second), (down_weight_master, down_weight_first, down_weight_second))
    updated = [adamw_update(gradient, state_set[0], state_set[1], state_set[2], step_rate, factor) for gradient, state_set, step_rate in zip(grads_all, states, step_rates)]
    return (outputs.reshape(TOKENS, D), input_grads.reshape(TOKENS, D), grad_norm, updated[0][0], updated[0][1], updated[0][2], updated[0][3], updated[1][0], updated[1][1], updated[1][2], updated[1][3], updated[2][0], updated[2][1], updated[2][2], updated[2][3], updated[3][0], updated[3][1], updated[3][2], updated[3][3], updated[4][0], updated[4][1], updated[4][2], updated[4][3], updated[5][0], updated[5][1], updated[5][2], updated[5][3], updated[6][0], updated[6][1], updated[6][2], updated[6][3], updated[7][0], updated[7][1], updated[7][2], updated[7][3], second_mods.reshape(FRAMES, 2 * D))
```

```python
import functools

import jax
import jax.numpy as jnp
from jax import lax
from jax.experimental import pallas as pl
from jax.experimental.pallas import tpu as pltpu
from jax.sharding import PartitionSpec as P

D = 768
HS = 64
FF = 3072
SIDE = 32
STEP = 10
PARAMS = 11419392

NORM_EPS = 1e-06
BETA_ONE = 0.5
BETA_TWO = 0.5
ADAM_EPS = 1e-08
WEIGHT_DECAY = 0.01

F32 = jnp.float32
BF16 = jnp.bfloat16

BODY = 512
HALF = 256
EDGE = 32
PLANE = 592
CHUNK = 256
VMEM_BYTES = 60 * 1024 * 1024


def params(*semantics):
    return pltpu.CompilerParams(
        dimension_semantics=semantics or None, vmem_limit_bytes=VMEM_BYTES
    )


def nn(left, right):
    return lax.dot_general(left, right, (((1,), (0,)), ((), ())), preferred_element_type=F32)


def nt(left, right):
    return lax.dot_general(left, right, (((1,), (1,)), ((), ())), preferred_element_type=F32)


def tn(left, right):
    return lax.dot_general(left, right, (((0,), (0,)), ((), ())), preferred_element_type=F32)


def whole(shape):
    return pl.BlockSpec(shape, lambda *_: (0,) * len(shape), pipeline_mode=pl.Buffered(1))


def scalars():
    return pl.BlockSpec(memory_space=pltpu.SMEM)


def geometry(scal_ref):
    return scal_ref[0], scal_ref[1], scal_ref[2] == 1, scal_ref[3]


def body_offset(half, gap):
    return pl.multiple_of(EDGE + half * (HALF + gap), 16)


def edge_offset(place):
    return pl.multiple_of(jnp.where(place == 0, EDGE + BODY, 0), 16)


def normalize(fields):
    center = fields - jnp.mean(fields, -1, keepdims=True)
    inverse = lax.rsqrt(jnp.mean(center * center, -1, keepdims=True) + NORM_EPS)
    return center * inverse, inverse


def norm_back(grad_hat, normed, inverse):
    return inverse * (
        grad_hat
        - jnp.mean(grad_hat, -1, keepdims=True)
        - normed * jnp.mean(grad_hat * normed, -1, keepdims=True)
    )


def variants(base, shifted, offset, width, rows, lanes):
    up = pl.multiple_of(offset - width, 16)
    down = pl.multiple_of(offset + width, 16)
    found = {}
    for part, shift, where in ((0, 0, offset), (0, 1, down), (1, 0, offset), (1, -1, up)):
        for column in (0, 1):
            at = (2 * part + column, pl.ds(where, rows), lanes)
            found[part, shift, column, 0] = base[at]
            found[part, shift, column, 1] = shifted[at]
    return found


def tap(found, p, q, a, b):
    part, shift = ((1, -1), (0, 0), (1, 0))[a + 1] if p == 0 else ((0, 0), (1, 0), (0, 1))[a + 1]
    column, moved = ((1, 1), (0, 0), (1, 0))[b + 1] if q == 0 else ((0, 0), (1, 0), (0, 1))[b + 1]
    return found[part, shift, column, moved]


def conv_at(found, kernel, p, q, flip=False):
    total = None
    for a in (-1, 0, 1):
        for b in (-1, 0, 1):
            index = 3 * (a + 1) + (b + 1)
            term = tap(found, p, q, a, b) * kernel[8 - index if flip else index]
            total = term if total is None else total + term
    return total


def kernel_rows(kernel_ref, lanes, rows):
    return [
        jnp.broadcast_to(kernel_ref[index : index + 1, lanes], (rows, lanes.size)) for index in range(9)
    ]


def clear_borders(plane, wide_gap=True):
    zeros = jnp.zeros((4, EDGE, plane.shape[2]), plane.dtype)
    plane[:, 0:EDGE, :] = zeros
    plane[:, EDGE + HALF : EDGE + HALF + EDGE, :] = zeros
    plane[:, EDGE + BODY : EDGE + BODY + EDGE, :] = zeros
    plane[:, PLANE - EDGE : PLANE, :] = zeros


def shift_planes(base, shifted, shift_ref, gap, long_latent, place, lanes=slice(None)):
    for column in (0, 1):

        @pl.loop(0, 4)
        def _(step, column=column):
            group = 2 * (step // 2) + column
            at = (group, pl.ds(body_offset(step % 2, gap), HALF), lanes)
            shifted[at] = nn(shift_ref[column], base[at]).astype(BF16)

        @pl.when(long_latent)
        def _(column=column):
            for part in (0, 1):
                at = (2 * part + column, pl.ds(edge_offset(place), EDGE), lanes)
                shifted[at] = nn(shift_ref[column, 0:EDGE, 0:EDGE], base[at]).astype(BF16)


def front_kernel(
    scal_ref, x_ref, edge_ref, perm_ref, edge_perm_ref, shift_ref, mod_ref, taps_ref, weight_ref,
    x_out, mixed_out, base_out, shifted_out, q_out, kv_out,
):
    width, gap, long_latent, place = geometry(scal_ref)
    step = pl.program_id(0)

    @pl.when(step == 0)
    def _():
        clear_borders(base_out)
        clear_borders(shifted_out)

        @pl.loop(0, 8)
        def _(block):
            half = block // 4
            rows = x_ref[pl.ds(pl.multiple_of(block * 256, 256), 256), :]
            shift = mod_ref[half, 0:1, :]
            scale = mod_ref[half, 1:2, :]
            place_in = pl.ds(pl.multiple_of(block * 64, 64), 64)
            place_out = pl.ds(pl.multiple_of(body_offset(half, gap) + (block % 4) * 64, 16), 64)
            for group in range(4):
                picked = nn(perm_ref[64 * group : 64 * group + 64, :], rows)
                x_out[group, place_in, :] = picked.astype(BF16)
                normed = normalize(picked)[0]
                base_out[group, place_out, :] = (normed * (1.0 + scale) + shift).astype(BF16)

        @pl.when(long_latent)
        def _():
            for group in range(4):
                picked = nn(edge_perm_ref[32 * group : 32 * group + 32, :], edge_ref[...])
                normed = normalize(picked)[0]
                value = normed * (1.0 + mod_ref[0, 1:2, :]) + mod_ref[0, 0:1, :]
                base_out[group, pl.ds(edge_offset(place), EDGE), :] = value.astype(BF16)

        shift_planes(base_out, shifted_out, shift_ref, gap, long_latent, place)

        for lane in range(D // 128):
            lanes = pl.ds(lane * 128, 128)
            kernel = kernel_rows(taps_ref, lanes, 16)

            @pl.loop(0, 32)
            def _(tile, lanes=lanes, kernel=kernel):
                offset = body_offset(tile // 16, gap) + (tile % 16) * 16
                found = variants(base_out, shifted_out, pl.multiple_of(offset, 16), width, 16, lanes)
                for p in (0, 1):
                    for q in (0, 1):
                        at = (2 * p + q, pl.ds(pl.multiple_of(tile * 16, 16), 16), lanes)
                        mixed_out[at] = conv_at(found, kernel, p, q)

    for group in range(4):
        triple = nn(mixed_out[group], weight_ref[0])
        q_out[0, group] = (triple[:, 0:128] * (HS**-0.5)).astype(BF16)
        kv_out[0, 0, group] = triple[:, 128:256].astype(BF16)
        kv_out[0, 1, group] = triple[:, 256:384].astype(BF16)


def front(scal, x, edge, perm, edge_perm, shifts, mod, taps, weight):
    pairs = weight.shape[0]
    plane = jax.ShapeDtypeStruct((4, PLANE, D), BF16)
    body = jax.ShapeDtypeStruct((4, BODY, D), BF16)
    return pl.pallas_call(
        front_kernel,
        grid=(pairs,),
        out_shape=(
            body, body, plane, plane,
            jax.ShapeDtypeStruct((pairs, 4, BODY, 128), BF16),
            jax.ShapeDtypeStruct((pairs, 2, 4, BODY, 128), BF16),
        ),
        in_specs=[
            scalars(), whole(x.shape), whole(edge.shape), whole(perm.shape), whole(edge_perm.shape),
            whole(shifts.shape), whole(mod.shape), whole(taps.shape),
            pl.BlockSpec((1, D, 384), lambda i: (i, 0, 0)),
        ],
        out_specs=(
            whole(body.shape), whole(body.shape), whole(plane.shape), whole(plane.shape),
            pl.BlockSpec((1, 4, BODY, 128), lambda i: (i, 0, 0, 0)),
            pl.BlockSpec((1, 2, 4, BODY, 128), lambda i: (i, 0, 0, 0, 0)),
        ),
        compiler_params=params("arbitrary"),
        name="front",
    )(scal, x, edge, perm, edge_perm, shifts, mod, taps, weight)


def head_mask(rows, head):
    lane = lax.broadcasted_iota(jnp.int32, (rows, 128), 1)
    return (lane < HS) if head == 0 else (lane >= HS)


def pieces(first, second, rows):
    lane = lax.broadcasted_iota(jnp.int32, (rows, 128), 1)
    value = jnp.where(lane < HS, first, second)
    one = value.astype(BF16).astype(F32)
    two = (value - one).astype(BF16).astype(F32)
    three = value - one - two
    turn = lane % HS
    picked = jnp.where(turn == 0, one, jnp.where(turn == 1, two, jnp.where(turn == 2, three, 0.0)))
    return picked.astype(BF16)


def unit_pieces(rows):
    lane = lax.broadcasted_iota(jnp.int32, (rows, 128), 1)
    return jnp.where(lane % HS < 3, 1.0, 0.0).astype(BF16)


def attend_kernel(scal_ref, q_ref, own_ref, other_ref, out_ref, log_ref):
    long_latent = scal_ref[2] == 1

    def attend(query, keys, values, rows):
        mixes, logs = [], []
        for head in (0, 1):
            masked = jnp.where(head_mask(rows, head), query, jnp.zeros_like(query))
            scores = [nt(masked, key) for key in keys]
            highest = jnp.max(scores[0], -1, keepdims=True)
            for other in scores[1:]:
                highest = jnp.maximum(highest, jnp.max(other, -1, keepdims=True))
            mix = None
            for score, value in zip(scores, values):
                share = jnp.exp(score - highest).astype(BF16)
                part = nn(share, value)
                mix = part if mix is None else mix + part
            total = mix[:, 128:256]
            mixes.append(mix[:, 0:128] / total)
            logs.append(highest + jnp.log(total))
        mix = jnp.where(head_mask(rows, 0), mixes[0], mixes[1])
        return mix.astype(BF16), pieces(-logs[0], -logs[1], rows)

    def with_ones(value):
        return jnp.concatenate([value, jnp.ones_like(value)], axis=1)

    @pl.when(long_latent)
    def _():
        for tile in range(2):
            at = pl.ds(tile * 256, 256)
            out_ref[0, at, :], log_ref[0, 0, at, :] = attend(
                q_ref[0, 0, at, :],
                [own_ref[0, 0, 0], other_ref[0, 0, 0]],
                [with_ones(own_ref[0, 1, 0]), with_ones(other_ref[0, 1, 0])],
                256,
            )

    @pl.when(jnp.logical_not(long_latent))
    def _():
        for tile in range(2):
            at = pl.ds(tile * 256, 256)
            out_ref[0, at, :], log_ref[0, 0, at, :] = attend(
                q_ref[0, 0, at, :],
                [own_ref[0, 0, 0, at, :]],
                [with_ones(own_ref[0, 1, 0, at, :])],
                256,
            )


def attention(scal, q, own, other):
    pairs = q.shape[0]
    pair_spec = pl.BlockSpec((1, 1, BODY, 128), lambda p, g: (p, g, 0, 0))
    kv_spec = pl.BlockSpec((1, 2, 1, BODY, 128), lambda p, g: (p, 0, g, 0, 0))
    other_spec = pl.BlockSpec((1, 2, 1, BODY, 128), lambda p, g: ((p + pairs // 2) % pairs, 0, g, 0, 0))
    return pl.pallas_call(
        attend_kernel,
        grid=(pairs, 4),
        out_shape=(
            jax.ShapeDtypeStruct((4, BODY, 128 * pairs), BF16),
            jax.ShapeDtypeStruct((pairs, 4, BODY, 128), BF16),
        ),
        in_specs=[scalars(), pair_spec, kv_spec, other_spec],
        out_specs=(pl.BlockSpec((1, BODY, 128), lambda p, g: (g, 0, p)), pair_spec),
        compiler_params=params("arbitrary", "arbitrary"),
        name="attention",
    )(scal, q, own, other)


def attend_back_kernel(
    scal_ref, q_ref, own_ref, other_ref, mix_ref, grad_ref, log_ref, gq_ref, gown_ref, gother_ref
):
    long_latent = scal_ref[2] == 1

    def side(query, mix, grad, log):
        rows = query.shape[0]
        product = mix.astype(F32) * grad.astype(F32)
        deltas = [
            jnp.sum(jnp.where(head_mask(rows, head), product, 0.0), -1, keepdims=True) for head in (0, 1)
        ]
        delta = pieces(-deltas[0], -deltas[1], rows)
        result = []
        for head in (0, 1):
            mask = head_mask(rows, head)
            zero = jnp.zeros_like(query)
            q_head = jnp.where(mask, query, zero)
            g_head = jnp.where(mask, grad, zero)
            q_more = jnp.concatenate([q_head, jnp.where(mask, log, zero)], axis=1)
            g_more = jnp.concatenate([g_head, jnp.where(mask, delta, zero)], axis=1)
            result.append((q_head, g_head, q_more, g_more))
        return result

    def keys_part(heads, key, value):
        rows = key.shape[0]
        ones = unit_pieces(rows)
        key_more = jnp.concatenate([key, ones], axis=1)
        value_more = jnp.concatenate([value, ones], axis=1)
        key_turned = key.astype(F32).T.astype(BF16)
        gk = gv = None
        turned = []
        for q_head, g_head, q_more, g_more in heads:
            share = jnp.exp(nt(key_more, q_more))
            slope = (share * nt(value_more, g_more)).astype(BF16)
            share = share.astype(BF16)
            gv_part = nn(share, g_head)
            gk_part = nn(slope, q_head)
            gv = gv_part if gv is None else gv + gv_part
            gk = gk_part if gk is None else gk + gk_part
            turned.append(nn(key_turned, slope))
        return gk, gv, turned

    def query_grad(turned):
        row = lax.broadcasted_iota(jnp.int32, turned[0].shape, 0)
        both = jnp.where(row < HS, turned[0], turned[1]) * (HS**-0.5)
        return both.T.astype(BF16)

    @pl.when(long_latent)
    def _():
        heads = side(q_ref[0, 0], mix_ref[0], grad_ref[0], log_ref[0, 0])
        totals = None
        for source, target in ((own_ref, gown_ref), (other_ref, gother_ref)):
            for tile in range(2):
                at = pl.ds(tile * 256, 256)
                gk, gv, turned = keys_part(heads, source[0, 0, 0, at, :], source[0, 1, 0, at, :])
                target[0, 0, 0, at, :] = gk.astype(BF16)
                target[0, 1, 0, at, :] = gv.astype(BF16)
                totals = turned if totals is None else [a + b for a, b in zip(totals, turned)]
        gq_ref[0, 0] = query_grad(totals)

    @pl.when(jnp.logical_not(long_latent))
    def _():
        for tile in range(2):
            at = pl.ds(tile * 256, 256)
            heads = side(q_ref[0, 0, at, :], mix_ref[0, at, :], grad_ref[0, at, :], log_ref[0, 0, at, :])
            gk, gv, turned = keys_part(heads, own_ref[0, 0, 0, at, :], own_ref[0, 1, 0, at, :])
            gown_ref[0, 0, 0, at, :] = gk.astype(BF16)
            gown_ref[0, 1, 0, at, :] = gv.astype(BF16)
            gq_ref[0, 0, at, :] = query_grad(turned)
        gother_ref[...] = jnp.zeros_like(gother_ref)


def attention_back(scal, q, own, other, mix, grad, log):
    pairs = q.shape[0]
    pair_spec = pl.BlockSpec((1, 1, BODY, 128), lambda p, g: (p, g, 0, 0))
    kv_spec = pl.BlockSpec((1, 2, 1, BODY, 128), lambda p, g: (p, 0, g, 0, 0))
    other_spec = pl.BlockSpec((1, 2, 1, BODY, 128), lambda p, g: ((p + pairs // 2) % pairs, 0, g, 0, 0))
    lane_spec = pl.BlockSpec((1, BODY, 128), lambda p, g: (g, 0, p))
    return pl.pallas_call(
        attend_back_kernel,
        grid=(pairs, 4),
        out_shape=(
            jax.ShapeDtypeStruct(q.shape, BF16),
            jax.ShapeDtypeStruct(own.shape, BF16),
            jax.ShapeDtypeStruct(own.shape, BF16),
        ),
        in_specs=[scalars(), pair_spec, kv_spec, other_spec, lane_spec, lane_spec, pair_spec],
        out_specs=(pair_spec, kv_spec, other_spec),
        compiler_params=params("arbitrary", "arbitrary"),
        name="attention_back",
    )(scal, q, own, other, mix, grad, log)


def middle_kernel(
    x_ref, mix_ref, cot_ref, perm_ref, mod_ref, weight_ref, attn_out, norm_out, cot_out, grad_out
):
    gate_one = mod_ref[0, 2:3, :]
    shift = mod_ref[0, 3:4, :]
    scale = mod_ref[0, 4:5, :]
    gate_two = mod_ref[0, 5:6, :]
    for group in range(4):
        attn = nn(mix_ref[group], weight_ref[...])
        attn_low = attn.astype(BF16)
        attn_out[group] = attn_low
        residual = x_ref[group].astype(F32) + gate_one * attn_low.astype(F32)
        norm_out[group] = (normalize(residual)[0] * (1.0 + scale) + shift).astype(BF16)
        cot = nn(perm_ref[64 * group : 64 * group + 64, :], cot_ref[...])
        cot_out[group] = cot.astype(BF16)
        grad_out[group] = (cot * gate_two).astype(BF16)


def middle(x, mix, cot, perm, mod, weight):
    block = pl.BlockSpec((4, 64, D), lambda i: (0, i, 0))
    body = jax.ShapeDtypeStruct((4, BODY, D), BF16)
    return pl.pallas_call(
        middle_kernel,
        grid=(8,),
        out_shape=(body,) * 4,
        in_specs=[
            block, block, pl.BlockSpec((256, D), lambda i: (i, 0)), whole(perm.shape),
            pl.BlockSpec((1, 8, D), lambda i: (i // 4, 0, 0)), whole(weight.shape),
        ],
        out_specs=(block,) * 4,
        compiler_params=params("arbitrary"),
        name="middle",
    )(x, mix, cot, perm, mod, weight)


def gelu_both(value):
    root = 0.7978845608028654
    square = value * value
    angle = value * (root + (root * 0.044715) * square)
    bent = jnp.tanh(angle)
    half = 0.5 + 0.5 * bent
    inner = (0.5 * root) + (1.5 * root * 0.044715) * square
    return value * half, half + value * (1.0 - bent * bent) * inner


def ffn_kernel(
    scal_ref, taps_own, taps_other, norm_ref, norm_edge, grad_ref, grad_edge, shift_ref,
    up_own, up_other, down_own, down_other,
    ffn_out, back_out, up_grad, down_grad, taps_grad,
    hid, hid_moved, gc, gc_moved, act, gh, da, da_edge, ffn_sum, back_sum, up, down, taps, norm_turned, grad_turned,
):
    width, gap, long_latent, place = geometry(scal_ref)
    step = pl.program_id(0)
    steps = pl.num_programs(0)

    @pl.when(step < steps // 2)
    def _():
        up[...] = up_own[...]
        down[...] = down_own[...]
        taps[...] = taps_own[...]

    @pl.when(step >= steps // 2)
    def _():
        up[...] = up_other[...]
        down[...] = down_other[...]
        taps[...] = taps_other[...]

    @pl.when(step == 0)
    def _():
        for plane in (hid, hid_moved, gc, gc_moved):
            clear_borders(plane)

        @pl.loop(0, 8)
        def _(tile):
            rows = pl.ds(pl.multiple_of((tile % 2) * HALF, HALF), HALF)
            cols = pl.ds(pl.multiple_of(tile * HALF, HALF), HALF)
            norm_turned[:, cols] = norm_ref[tile // 2, rows, :].T
            grad_turned[:, cols] = grad_ref[tile // 2, rows, :].T
            ffn_sum[tile // 2, rows, :] = jnp.zeros((HALF, D), F32)
            back_sum[tile // 2, rows, :] = jnp.zeros((HALF, D), F32)

    turn = lax.broadcasted_iota(jnp.int32, (BODY, CHUNK), 0) & (width - 1)
    keep = (turn != width - 1, turn != 0)
    for group in range(4):
        value = nn(norm_ref[group], up[...])
        moved = jnp.where(keep[group % 2], pltpu.roll(value, BODY - 1 if group % 2 == 0 else 1, 0), 0.0)
        for half in (0, 1):
            at = (group, pl.ds(body_offset(half, gap), HALF), slice(None))
            hid[at] = value[half * HALF : (half + 1) * HALF].astype(BF16)
            hid_moved[at] = moved[half * HALF : (half + 1) * HALF].astype(BF16)
        da[group] = nt(grad_ref[group], down[...]).astype(BF16)

    @pl.when(long_latent)
    def _():
        for group in range(4):
            at = (group, pl.ds(edge_offset(place), EDGE), slice(None))
            value = nn(norm_edge[group], up[...]).astype(BF16)
            hid[at] = value
            hid_moved[at] = nn(shift_ref[group % 2, 0:EDGE, 0:EDGE], value).astype(BF16)
            da_edge[group] = nt(grad_edge[group], down[...]).astype(BF16)

    for lane in range(CHUNK // 128):
        lanes = pl.ds(lane * 128, 128)
        kernel = kernel_rows(taps, lanes, 16)

        @pl.loop(0, 32, unroll=4)
        def _(tile, lanes=lanes, kernel=kernel):
            offset = pl.multiple_of(body_offset(tile // 16, gap) + (tile % 16) * 16, 16)
            found = variants(hid, hid_moved, offset, width, 16, lanes)
            rows = pl.ds(pl.multiple_of(tile * 16, 16), 16)
            for p in (0, 1):
                for q in (0, 1):
                    group = 2 * p + q
                    value, slope = gelu_both(conv_at(found, kernel, p, q).astype(F32))
                    act[group, rows, lanes] = value.astype(BF16)
                    gc[group, pl.ds(offset, 16), lanes] = (slope * da[group, rows, lanes].astype(F32)).astype(BF16)

        for side in (0, 1):

            @pl.when(jnp.logical_and(long_latent, place == side))
            def _(lanes=lanes, kernel=kernel, side=side):
                for tile in (0, 1):
                    offset = (EDGE + BODY if side == 0 else 0) + 16 * tile
                    low = max(offset - EDGE, 0)
                    found = {}
                    for part, shift, where in ((0, 0, offset), (0, 1, offset + EDGE), (1, 0, offset), (1, -1, low)):
                        if where + 16 > PLANE:
                            continue
                        for column in (0, 1):
                            at = (2 * part + column, slice(where, where + 16), lanes)
                            found[part, shift, column, 0] = hid[at]
                            found[part, shift, column, 1] = hid_moved[at]
                    for q in (0, 1):
                        group = 2 * side + q
                        slope = gelu_both(conv_at(found, kernel, side, q).astype(F32))[1]
                        grad = da_edge[group, 16 * tile : 16 * tile + 16, lanes].astype(F32)
                        gc[group, offset : offset + 16, lanes] = (slope * grad).astype(BF16)

    for group in range(4):
        for half in (0, 1):
            at = (group, pl.ds(body_offset(half, gap), HALF), slice(None))
            value = gc[at].astype(F32)
            moved = pltpu.roll(value, HALF - 1 if group % 2 == 0 else 1, 0)
            gc_moved[at] = jnp.where(keep[group % 2][:HALF], moved, 0.0).astype(BF16)
        @pl.when(long_latent)
        def _(group=group):
            at = (group, pl.ds(edge_offset(place), EDGE), slice(None))
            gc_moved[at] = nn(shift_ref[group % 2, 0:EDGE, 0:EDGE], gc[at]).astype(BF16)

    for lane in range(CHUNK // 128):
        lanes = pl.ds(lane * 128, 128)
        kernel = kernel_rows(taps, lanes, 16)

        def back_tile(tile, sums, lanes=lanes, kernel=kernel):
            offset = pl.multiple_of(body_offset(tile // 16, gap) + (tile % 16) * 16, 16)
            rows = pl.ds(pl.multiple_of(tile * 16, 16), 16)
            found = variants(gc, gc_moved, offset, width, 16, lanes)
            for p in (0, 1):
                for q in (0, 1):
                    gh[2 * p + q, rows, lanes] = conv_at(found, kernel, p, q, flip=True)
            return taps_at(found, variants(hid, hid_moved, offset, width, 16, lanes), sums)

        sums = lax.fori_loop(0, 32, back_tile, (jnp.zeros((16, 128), F32),) * 9,unroll=4)
        for index in range(9):
            taps_grad[0, index : index + 1, lanes] = jnp.sum(sums[index], 0, keepdims=True)

    for group in range(4):
        ffn_sum[group] += nn(act[group], down[...])
        back_sum[group] += nt(gh[group], up[...])

    flat_gh = gh[...].reshape(4 * BODY, CHUNK)
    flat_act = act[...].reshape(4 * BODY, CHUNK)
    up_grad[0] = nn(norm_turned[...], flat_gh).astype(BF16)
    down_grad[...] = nn(grad_turned[...], flat_act).T.astype(BF16)

    @pl.when(step == steps - 1)
    def _():
        ffn_out[...] = ffn_sum[...].astype(BF16)
        back_out[...] = back_sum[...].astype(BF16)


def taps_at(grads, fields, sums):
    sums = list(sums)
    for a in (-1, 0, 1):
        for b in (-1, 0, 1):
            index = 3 * (a + 1) + (b + 1)
            total = None
            for p in (0, 1):
                for q in (0, 1):
                    term = grads[p, 0, q, 0] * tap(fields, p, q, a, b)
                    total = term if total is None else total + term
            sums[index] = sums[index] + total.astype(F32)
    return tuple(sums)


def feed_forward(scal, taps_own, taps_other, norm, norm_edge, grad, grad_edge, shifts, up_own, up_other, down_own, down_other):
    half = up_own.shape[1] // CHUNK
    steps = 2 * half
    body = jax.ShapeDtypeStruct((4, BODY, D), BF16)

    def own(i):
        return jnp.minimum(i, half - 1)

    def other(i):
        return jnp.maximum(i - half, 0)

    per = D // CHUNK
    plane = pltpu.VMEM((4, PLANE, CHUNK), BF16)
    small = pltpu.VMEM((4, BODY, CHUNK), BF16)
    return pl.pallas_call(
        ffn_kernel,
        grid=(steps,),
        out_shape=(
            body, body,
            jax.ShapeDtypeStruct((steps // per, D, D), BF16),
            jax.ShapeDtypeStruct((steps * CHUNK, D), BF16),
            jax.ShapeDtypeStruct((steps, 16, CHUNK), F32),
        ),
        in_specs=[
            scalars(),
            pl.BlockSpec((16, CHUNK), lambda i: (0, own(i))),
            pl.BlockSpec((16, CHUNK), lambda i: (0, other(i))),
            whole(norm.shape), whole(norm_edge.shape), whole(grad.shape), whole(grad_edge.shape), whole(shifts.shape),
            pl.BlockSpec((D, CHUNK), lambda i: (0, own(i))),
            pl.BlockSpec((D, CHUNK), lambda i: (0, other(i))),
            pl.BlockSpec((CHUNK, D), lambda i: (own(i), 0)),
            pl.BlockSpec((CHUNK, D), lambda i: (other(i), 0)),
        ],
        out_specs=(
            whole(body.shape), whole(body.shape),
            pl.BlockSpec((1, D, CHUNK), lambda i: (i // per, 0, i % per)),
            pl.BlockSpec((CHUNK, D), lambda i: (i, 0)),
            pl.BlockSpec((1, 16, CHUNK), lambda i: (i, 0, 0)),
        ),
        scratch_shapes=[
            plane, plane, plane, plane, small, small, small, pltpu.VMEM((4, EDGE, CHUNK), BF16),
            pltpu.VMEM((4, BODY, D), F32), pltpu.VMEM((4, BODY, D), F32),
            pltpu.VMEM((D, CHUNK), BF16), pltpu.VMEM((CHUNK, D), BF16), pltpu.VMEM((16, CHUNK), BF16),
            pltpu.VMEM((D, 4 * BODY), BF16), pltpu.VMEM((D, 4 * BODY), BF16),
        ],
        compiler_params=params("arbitrary"),
        name="feed_forward",
    )(scal, taps_own, taps_other, norm, norm_edge, grad, grad_edge, shifts, up_own, up_other, down_own, down_other)


def turn_kernel(
    x_ref, attn_ref, ffn_ref, cot_ref, back_ref, mix_ref, perm_ref, mod_ref, weight_ref,
    out_ref, grad_ref, gmix_ref, sums_ref, wgrad_ref,
    wsum,
):
    step = pl.program_id(0)
    gate_one = mod_ref[0, 2:3, :]
    scale = mod_ref[0, 4:5, :]
    gate_two = mod_ref[0, 5:6, :]

    @pl.when(step % 4 == 0)
    def _():
        sums_ref[...] = jnp.zeros_like(sums_ref)

    @pl.when(step == 0)
    def _():
        wsum[...] = jnp.zeros_like(wsum)

    result = None
    for group in range(4):
        attn = attn_ref[group].astype(F32)
        ffn = ffn_ref[group].astype(F32)
        cot = cot_ref[group].astype(F32)
        back = back_ref[group].astype(F32)
        residual = x_ref[group].astype(F32) + gate_one * attn
        low = (residual + gate_two * ffn).astype(BF16)
        part = nn(perm_ref[:, 64 * group : 64 * group + 64], low)
        result = part if result is None else result + part
        normed, inverse = normalize(residual)
        grad = cot + norm_back(back * (1.0 + scale), normed, inverse)
        grad_ref[group] = grad.astype(BF16)
        for row, value in ((0, grad * attn), (1, back), (2, back * normed), (3, cot * ffn)):
            sums_ref[0, row : row + 1, :] += jnp.sum(value, 0, keepdims=True)
        gattn = (grad * gate_one).astype(BF16)
        gmix_ref[group] = nt(gattn, weight_ref[...]).astype(BF16)
        wsum[...] += tn(mix_ref[group], gattn)
    out_ref[...] = result.astype(BF16)

    @pl.when(step == 7)
    def _():
        wgrad_ref[...] = wsum[...].astype(BF16)


def turn(x, attn, ffn, cot, back, mix, perm, mod, weight):
    block = pl.BlockSpec((4, 64, D), lambda i: (0, i, 0))
    body = jax.ShapeDtypeStruct((4, BODY, D), BF16)
    return pl.pallas_call(
        turn_kernel,
        grid=(8,),
        out_shape=(
            jax.ShapeDtypeStruct((2048, D), BF16), body, body,
            jax.ShapeDtypeStruct((2, 8, D), F32), jax.ShapeDtypeStruct((D, D), BF16),
        ),
        in_specs=[block] * 6 + [
            whole(perm.shape), pl.BlockSpec((1, 8, D), lambda i: (i // 4, 0, 0)), whole(weight.shape),
        ],
        out_specs=(
            pl.BlockSpec((256, D), lambda i: (i, 0)), block, block,
            pl.BlockSpec((1, 8, D), lambda i: (i // 4, 0, 0)), whole((D, D)),
        ),
        scratch_shapes=[pltpu.VMEM((D, D), F32)],
        compiler_params=params("arbitrary"),
        name="turn",
    )(x, attn, ffn, cot, back, mix, perm, mod, weight)


def project_back_kernel(gq_ref, gown_ref, gother_ref, mixed_ref, weight_ref, gmixed_ref, wgrad_ref, gsum, turned):
    step = pl.program_id(0)

    @pl.when(step == 0)
    def _():
        gsum[...] = jnp.zeros_like(gsum)

        @pl.loop(0, 8)
        def _(tile):
            rows = pl.ds(pl.multiple_of((tile % 2) * HALF, HALF), HALF)
            cols = pl.ds(pl.multiple_of(tile * HALF, HALF), HALF)
            turned[:, cols] = mixed_ref[tile // 2, rows, :].T

    wsum = None
    for group in range(4):
        gk = (gown_ref[0, 0, group].astype(F32) + gother_ref[0, 0, group].astype(F32)).astype(BF16)
        gv = (gown_ref[0, 1, group].astype(F32) + gother_ref[0, 1, group].astype(F32)).astype(BF16)
        triple = jnp.concatenate([gq_ref[0, group], gk, gv], axis=1)
        gsum[group] += nt(triple, weight_ref[0])
        part = nn(turned[:, BODY * group : BODY * (group + 1)], triple)
        wsum = part if wsum is None else wsum + part
    wgrad_ref[0] = wsum.astype(BF16)

    @pl.when(step == pl.num_programs(0) - 1)
    def _():
        gmixed_ref[...] = gsum[...].astype(BF16)


def project_back(gq, gown, gother, mixed, weight):
    pairs = gq.shape[0]
    kv_spec = pl.BlockSpec((1, 2, 4, BODY, 128), lambda i: (i, 0, 0, 0, 0))
    return pl.pallas_call(
        project_back_kernel,
        grid=(pairs,),
        out_shape=(jax.ShapeDtypeStruct((4, BODY, D), BF16), jax.ShapeDtypeStruct((pairs, D, 384), BF16)),
        in_specs=[
            pl.BlockSpec((1, 4, BODY, 128), lambda i: (i, 0, 0, 0)), kv_spec, kv_spec,
            whole(mixed.shape), pl.BlockSpec((1, D, 384), lambda i: (i, 0, 0)),
        ],
        out_specs=(whole((4, BODY, D)), pl.BlockSpec((1, D, 384), lambda i: (i, 0, 0))),
        scratch_shapes=[pltpu.VMEM((4, BODY, D), F32), pltpu.VMEM((D, 4 * BODY), BF16)],
        compiler_params=params("arbitrary"),
        name="project_back",
    )(gq, gown, gother, mixed, weight)


def back_kernel(
    scal_ref, x_ref, gmixed_ref, gedge_ref, base_ref, shifted_ref, gres_ref, perm_ref, shift_ref, mod_ref, taps_ref,
    out_ref, sums_ref, taps_grad,
    gm, gm_moved, gnorm,
):
    width, gap, long_latent, place = geometry(scal_ref)
    clear_borders(gm)
    clear_borders(gm_moved)
    for group in range(4):
        for half in (0, 1):
            gm[group, pl.ds(body_offset(half, gap), HALF), :] = gmixed_ref[group, half * HALF : (half + 1) * HALF, :]

    @pl.when(long_latent)
    def _():
        for group in range(4):
            gm[group, pl.ds(edge_offset(place), EDGE), :] = gedge_ref[group]

    shift_planes(gm, gm_moved, shift_ref, gap, long_latent, place)

    for lane in range(D // 128):
        lanes = pl.ds(lane * 128, 128)
        kernel = kernel_rows(taps_ref, lanes, 16)

        def back_tile(tile, sums, lanes=lanes, kernel=kernel):
            offset = pl.multiple_of(body_offset(tile // 16, gap) + (tile % 16) * 16, 16)
            rows = pl.ds(pl.multiple_of(tile * 16, 16), 16)
            found = variants(gm, gm_moved, offset, width, 16, lanes)
            for p in (0, 1):
                for q in (0, 1):
                    gnorm[2 * p + q, rows, lanes] = conv_at(found, kernel, p, q, flip=True)
            return taps_at(found, variants(base_ref, shifted_ref, offset, width, 16, lanes), sums)

        sums = lax.fori_loop(0, 32, back_tile, (jnp.zeros((16, 128), F32),) * 9)
        for index in range(9):
            taps_grad[index : index + 1, lanes] = jnp.sum(sums[index], 0, keepdims=True)

    sums_ref[...] = jnp.zeros_like(sums_ref)

    @pl.loop(0, 8)
    def _(block):
        half = block // 4
        scale = mod_ref[half, 1:2, :]
        rows = pl.ds(pl.multiple_of(block * 64, 64), 64)
        result = None
        for group in range(4):
            normed, inverse = normalize(x_ref[group, rows, :].astype(F32))
            back = gnorm[group, rows, :].astype(F32)
            grad = gres_ref[group, rows, :].astype(F32) + norm_back(back * (1.0 + scale), normed, inverse)
            sums_ref[half, 0:1, :] += jnp.sum(back, 0, keepdims=True)
            sums_ref[half, 1:2, :] += jnp.sum(back * normed, 0, keepdims=True)
            part = nn(perm_ref[:, 64 * group : 64 * group + 64], grad.astype(BF16))
            result = part if result is None else result + part
        out_ref[pl.ds(pl.multiple_of(block * 256, 256), 256), :] = result.astype(BF16)


def back(scal, x, gmixed, gedge, base, shifted, gres, perm, shifts, mod, taps):
    arrays = (x, gmixed, gedge, base, shifted, gres, perm, shifts, mod, taps)
    plane = pltpu.VMEM((4, PLANE, D), BF16)
    return pl.pallas_call(
        back_kernel,
        out_shape=(
            jax.ShapeDtypeStruct((2048, D), BF16),
            jax.ShapeDtypeStruct((2, 8, D), F32),
            jax.ShapeDtypeStruct((16, D), F32),
        ),
        in_specs=[scalars()] + [pl.BlockSpec(memory_space=pltpu.VMEM)] * len(arrays),
        out_specs=(pl.BlockSpec(memory_space=pltpu.VMEM),) * 3,
        scratch_shapes=[plane, plane, pltpu.VMEM((4, BODY, D), BF16)],
        compiler_params=params(),
        name="back",
    )(scal, *arrays)


MESH = pl.DeviceIdType.MESH


def chip_grid(count):
    return {16: (4, 2, 2), 64: (4, 4, 4)}.get(count, (count, 1, 1))


def reduce_gather_kernel(grid, parts_ref, sent_ref, sum_ref, all_ref, *scratch):
    (first, work, r1a, r1b, w1a, w1b, r2a, r2b, w2, r3, gz, gx, gy) = scratch[:13]
    sends, recvs = scratch[13:]
    deep, tall, broad = grid
    low = deep // 2
    wide = lax.axis_index("wide")
    place = lax.axis_index("narrow")
    z, y, x = wide // (tall * broad), (wide // broad) % tall, wide % broad

    def chip(zz, yy, xx):
        return {"wide": (zz * tall + yy) * broad + xx, "narrow": place}

    def along_x(step):
        return chip(z, y, (x + step) % broad)

    def along_y(step):
        return chip(z, (y + step) % tall, x)

    def along_z(step):
        return chip((z + step) % deep, y, x)

    sibling = {"wide": wide, "narrow": 1 - place}
    partners = (
        [sibling]
        + [along_x(step) for step in range(1, broad)]
        + [along_y(step) for step in range(1, tall)]
        + [along_z(step) for step in range(1, deep)]
    )
    barrier = pltpu.get_barrier_semaphore()
    for partner in partners:
        pl.semaphore_signal(barrier, inc=1, device_id=partner, device_id_type=MESH)
    pl.semaphore_wait(barrier, len(partners))

    count = [0]

    def send(source, target, partner):
        copy = pltpu.make_async_remote_copy(
            src_ref=source, dst_ref=target, send_sem=sends.at[count[0]], recv_sem=recvs.at[count[0]],
            device_id=partner, device_id_type=MESH,
        )
        count[0] += 1
        copy.start()
        return copy

    def wait(copies):
        for copy in copies:
            copy.wait()

    def add(target, *sources):
        total = sources[0].astype(F32)
        for source in sources[1:]:
            total = total + source.astype(F32)
        return total.astype(target.dtype)

    gz[z] = sent_ref[...]
    halves = ((0, low), (low, deep))
    swaps = [send(parts_ref.at[1, start:stop], first.at[start:stop], sibling) for start, stop in halves]
    gathers = [send(sent_ref, gz.at[z], along_z(step)) for step in range(1, deep)]

    def add_first(start, stop):
        for zz in range(start, stop):

            @pl.loop(0, tall * broad)
            def _(at, zz=zz):
                yy, xx = at // broad, at % broad
                work[zz, yy, xx] = add(work, parts_ref[0, zz, yy, xx], first[zz, yy, xx])

    swaps[0].wait()
    add_first(0, low)
    one_a = [send(work.at[0:low, :, (x + s) % broad], r1a.at[s - 1], along_x(s)) for s in range(1, broad)]
    swaps[1].wait()
    add_first(low, deep)
    one_b = [send(work.at[low:deep, (y + s) % tall], r1b.at[s - 1], along_y(s)) for s in range(1, tall)]
    wait(gathers)
    gx[x] = gz[...]
    gathers = [send(gz, gx.at[x], along_x(step)) for step in range(1, broad)]

    wait(one_a)
    for zz in range(low):
        for yy in range(tall):
            w1a[zz, yy] = add(w1a, work[zz, yy, x], *[r1a[s, zz, yy] for s in range(broad - 1)])
    two_a = [send(w1a.at[:, (y + s) % tall], r2a.at[s - 1], along_y(s)) for s in range(1, tall)]
    wait(one_b)
    for zz in range(deep - low):
        for xx in range(broad):
            w1b[zz, xx] = add(w1b, work[low + zz, y, xx], *[r1b[s, zz, xx] for s in range(tall - 1)])
    two_b = [send(w1b.at[:, (x + s) % broad], r2b.at[s - 1], along_x(s)) for s in range(1, broad)]
    wait(gathers)
    gy[y] = gx[...]
    gathers = [send(gx, gy.at[y], along_y(step)) for step in range(1, tall)]

    wait(two_a)
    for zz in range(low):
        w2[zz] = add(w2, w1a[zz, y], *[r2a[s, zz] for s in range(tall - 1)])
    wait(two_b)
    for zz in range(deep - low):
        w2[low + zz] = add(w2, w1b[zz, x], *[r2b[s, zz] for s in range(broad - 1)])
    three = [send(w2.at[(z + s) % deep], r3.at[s - 1], along_z(s)) for s in range(1, deep)]
    wait(gathers)
    all_ref[place] = gy[...]
    gathers = [send(gy, all_ref.at[place], sibling)]
    wait(three)
    sum_ref[...] = add(sum_ref, w2[z], *[r3[s] for s in range(deep - 1)])
    wait(gathers)


def reduce_gather(parts, sent):
    wide_count, rows, lanes = parts.shape[1:]
    deep, tall, broad = grid = chip_grid(wide_count)
    low = deep // 2
    unit = (rows, lanes)
    copies = 2 + 2 * (broad - 1 + tall - 1) + (deep - 1) + (deep - 1) + (broad - 1) + (tall - 1) + 1

    def slots(count, *shape):
        return pltpu.VMEM((max(count, 1), *shape, *unit), BF16)

    row = sent.shape
    result = pl.pallas_call(
        functools.partial(reduce_gather_kernel, grid),
        out_shape=(
            jax.ShapeDtypeStruct(unit, F32),
            jax.ShapeDtypeStruct((2, tall, broad, deep, *row), BF16),
        ),
        in_specs=[pl.BlockSpec(memory_space=pltpu.VMEM)] * 2,
        out_specs=(pl.BlockSpec(memory_space=pltpu.VMEM),) * 2,
        scratch_shapes=[
            pltpu.VMEM((*grid, *unit), BF16), pltpu.VMEM((*grid, *unit), BF16),
            slots(broad - 1, low, tall), slots(tall - 1, deep - low, broad),
            pltpu.VMEM((low, tall, *unit), BF16), pltpu.VMEM((deep - low, broad, *unit), BF16),
            slots(tall - 1, low), slots(broad - 1, deep - low),
            pltpu.VMEM((deep, *unit), BF16), slots(deep - 1),
            pltpu.VMEM((deep, *row), BF16), pltpu.VMEM((broad, deep, *row), BF16),
            pltpu.VMEM((tall, broad, deep, *row), BF16),
            pltpu.SemaphoreType.DMA((copies,)), pltpu.SemaphoreType.DMA((copies,)),
        ],
        compiler_params=pltpu.CompilerParams(
            collective_id=1, has_side_effects=True, vmem_limit_bytes=VMEM_BYTES
        ),
        name="reduce_gather",
    )(parts.reshape(2, *grid, *unit), sent)
    return result[0], result[1].reshape(-1, *row)


def square_sum_kernel(grid, *refs):
    count = len(refs) - 6
    grads = refs[:count]
    out_ref, mine, near, far, sends, recvs = refs[count:]
    deep, tall, broad = grid
    wide = lax.axis_index("wide")
    place = lax.axis_index("narrow")
    z, across = wide // (tall * broad), wide % (tall * broad)
    line = z * 2 + place

    def near_device(step):
        other = (line + step) % (2 * deep)
        return {"wide": (other // 2) * (tall * broad) + across, "narrow": other % 2}

    def far_device(step):
        return {"wide": z * (tall * broad) + (across + step) % (tall * broad), "narrow": place}

    nears = [near_device(step) for step in range(1, 2 * deep)]
    fars = [far_device(step) for step in range(1, tall * broad)]
    barrier = pltpu.get_barrier_semaphore()
    for partner in nears + fars:
        pl.semaphore_signal(barrier, inc=1, device_id=partner, device_id_type=MESH)

    total = jnp.zeros((), F32)
    for grad in grads:
        total = total + jnp.sum(grad[...] * grad[...])
    mine[...] = jnp.full((8, 128), total, F32)
    pl.semaphore_wait(barrier, len(nears + fars))

    def exchange(slots, partners, first):
        copies = []
        for step, partner in enumerate(partners):
            copy = pltpu.make_async_remote_copy(
                src_ref=mine, dst_ref=slots.at[step], send_sem=sends.at[first + step],
                recv_sem=recvs.at[first + step], device_id=partner, device_id_type=MESH,
            )
            copy.start()
            copies.append(copy)
        for copy in copies:
            copy.wait()
        value = mine[...]
        for step in range(len(partners)):
            value = value + slots[step]
        return value

    mine[...] = exchange(near, nears, 0)
    out_ref[...] = exchange(far, fars, len(nears))


def square_sum(wide_count, grads):
    deep, tall, broad = grid = chip_grid(wide_count)
    near, far = 2 * deep - 1, tall * broad - 1
    return pl.pallas_call(
        functools.partial(square_sum_kernel, grid),
        out_shape=jax.ShapeDtypeStruct((8, 128), F32),
        in_specs=[pl.BlockSpec(memory_space=pltpu.VMEM)] * len(grads),
        out_specs=pl.BlockSpec(memory_space=pltpu.VMEM),
        scratch_shapes=[
            pltpu.VMEM((8, 128), F32), pltpu.VMEM((near, 8, 128), F32), pltpu.VMEM((max(far, 1), 8, 128), F32),
            pltpu.SemaphoreType.DMA((near + far,)), pltpu.SemaphoreType.DMA((near + far,)),
        ],
        compiler_params=pltpu.CompilerParams(
            collective_id=2, has_side_effects=True, vmem_limit_bytes=VMEM_BYTES
        ),
        name="square_sum",
    )(*grads)


def adamw_kernel(rates, square_ref, *refs):
    clip_limit = PARAMS**0.5
    norm = jnp.sqrt(square_ref[0:1, 0:1])
    factor = clip_limit / jnp.maximum(norm, clip_limit)
    count = len(rates)
    ins, outs = refs[: 4 * count], refs[4 * count :]
    for index, rate in enumerate(rates):
        grad, master, first, second = ins[4 * index : 4 * index + 4]
        scaled = grad[...] * factor
        first_new = BETA_ONE * first[...] + (1.0 - BETA_ONE) * scaled
        second_new = BETA_TWO * second[...] + (1.0 - BETA_TWO) * scaled * scaled
        ratio = (first_new * (1.0 / (1.0 - BETA_ONE**STEP))) / (
            jnp.sqrt(second_new * (1.0 / (1.0 - BETA_TWO**STEP))) + ADAM_EPS
        )
        master_new = master[...] - rate * (ratio + WEIGHT_DECAY * master[...])
        first_out, second_out, master_out, copy_out = outs[4 * index : 4 * index + 4]
        first_out[...] = first_new
        second_out[...] = second_new
        master_out[...] = master_new
        copy_out[...] = master_new.astype(BF16)


def adamw(square, grads, states, rates):
    arrays = [array for grad, state in zip(grads, states) for array in (grad, *state)]
    shapes = [
        jax.ShapeDtypeStruct(grad.shape, dtype) for grad in grads for dtype in (F32, F32, F32, BF16)
    ]
    space = pl.BlockSpec(memory_space=pltpu.VMEM)
    return pl.pallas_call(
        functools.partial(adamw_kernel, rates),
        out_shape=shapes,
        in_specs=[space] * (1 + len(arrays)),
        out_specs=[space] * len(shapes),
        compiler_params=params(),
        name="adamw",
    )(square, *arrays)


def timestep_code(stamps, channels):
    half_dim = channels // 2
    scales = jnp.exp(-jnp.log(10000.0) * jnp.arange(half_dim, dtype=F32) / half_dim)
    angles = stamps.astype(F32)[:, None] * scales[None, :]
    return jnp.concatenate([jnp.cos(angles), jnp.sin(angles)], axis=1)


def one_hot_rows(source, columns, valid=None):
    hit = source[:, None] == jnp.arange(columns, dtype=jnp.int32)[None, :]
    if valid is not None:
        hit = jnp.logical_and(hit, valid[:, None])
    return hit.astype(BF16)


def permutation(long_latent):
    row = jnp.arange(256, dtype=jnp.int32)
    p, q, s = row // 128, (row // 64) % 2, row % 64
    big = (2 * (s // 32) + p) * 64 + 2 * (s % 32) + q
    small = (2 * (s // 16) + p) * 32 + 2 * (s % 16) + q
    return one_hot_rows(jnp.where(long_latent, big, small), 256)


def edge_permutation():
    row = jnp.arange(128, dtype=jnp.int32)
    return one_hot_rows((row // 64) * 64 + 2 * (row % 32) + (row // 32) % 2, 128)


def shift_matrices(width):
    row = jnp.arange(256, dtype=jnp.int32)
    column = row % width
    return jnp.stack([one_hot_rows(row + 1, 256, column != width - 1), one_hot_rows(row - 1, 256, column != 0)])


def pair_columns(weight):
    split = weight.reshape(weight.shape[0], -1, 2, 3, HS)
    return split.transpose(1, 0, 3, 2, 4).reshape(-1, weight.shape[0], 6 * HS)


def head_columns(paired):
    split = paired.reshape(paired.shape[0], paired.shape[1], 3, 2, HS)
    return split.transpose(1, 0, 3, 2, 4).reshape(paired.shape[1], -1)


def tap_rows(kernel):
    return jnp.pad(kernel.T, ((0, 7), (0, 0)))


def per_device(tokens, cotangent, size_tags, timesteps, labels, *weights_and_states):
    modulator, class_table, mix_kernel, heads_in, heads_out, up_weight, hidden_kernel, down_weight = weights_and_states[:8]
    states = [weights_and_states[8 + 3 * i : 11 + 3 * i] for i in range(8)]
    wide_count = lax.axis_size("wide")
    wide = lax.axis_index("wide")
    place = lax.axis_index("narrow")
    cell = wide * 2 + place
    cells = wide_count * 2

    def swap(value):
        return lax.ppermute(value, "narrow", [(0, 1), (1, 0)])

    def boundary(body):
        return jnp.where(place == 0, body[:, BODY - EDGE :], body[:, :EDGE])

    edge = swap(jnp.where(place == 0, tokens[-4 * EDGE :], tokens[: 4 * EDGE]))
    hin_own = pair_columns(heads_in)
    hin = jnp.concatenate([hin_own, swap(hin_own)], axis=0)
    hout = jnp.concatenate([heads_out, swap(heads_out)], axis=0)
    up_other = swap(up_weight)
    down_other = swap(down_weight)
    taps_own = tap_rows(hidden_kernel)
    taps_other = swap(taps_own)
    mix_taps = tap_rows(mix_kernel)

    long_latent = size_tags[0] > SIDE * SIDE
    width = jnp.where(long_latent, SIDE, SIDE // 2)
    gap = jnp.where(long_latent, 0, 16)
    scal = jnp.stack([width, gap, long_latent.astype(jnp.int32), place]).astype(jnp.int32)
    perm = permutation(long_latent)
    perm_back = perm.T
    shifts = shift_matrices(width)
    embedded = timestep_code(timesteps, D) + class_table[:, labels].astype(F32).T
    cond_low = jax.nn.silu(embedded).astype(BF16)
    modulation = jnp.dot(cond_low, modulator, preferred_element_type=F32).reshape(-1, 6, D)
    mod = jnp.pad(modulation, ((0, 0), (0, 2), (0, 0)))

    x, mixed, base, shifted, q, kv = front(
        scal, tokens, edge, perm, edge_permutation(), shifts, mod, mix_taps, hin
    )
    kv_other = swap(kv)
    attended, logs = attention(scal, q, kv, kv_other)
    attn, norm, cot, grad_ffn = middle(x, attended, cotangent, perm, mod, hout)
    norm_edge, grad_edge = swap((boundary(norm), boundary(grad_ffn)))
    ffn, back_norm, up_grad, down_grad, taps_grad = feed_forward(
        scal, taps_own, taps_other, norm, norm_edge, grad_ffn, grad_edge, shifts, up_weight, up_other, down_weight, down_other
    )

    output, grad_residual, grad_attended, sums_two, hout_grad = turn(
        x, attn, ffn, cot, back_norm, attended, perm_back, mod, hout
    )
    rows = D // wide_count
    half = FF // 2
    up_sum = up_grad[:2].astype(F32) + swap(up_grad[2:]).astype(F32)
    down_sum = down_grad[:half].astype(F32) + swap(down_grad[half:]).astype(F32)
    hout_sum = hout_grad[: D // 2].astype(F32) + swap(hout_grad[D // 2 :]).astype(F32)
    tap_half = taps_grad.shape[0] // 2
    taps_sum = taps_grad[:tap_half, :9] + swap(taps_grad[tap_half:, :9])
    tap_part = taps_sum.transpose(0, 2, 1).reshape(wide_count, -1)
    tap_part = jnp.pad(tap_part, ((0, 0), (0, -tap_part.shape[1] % D)))
    grads = jnp.concatenate(
        [
            up_sum.reshape(2, wide_count, rows, D).transpose(1, 0, 2, 3).reshape(wide_count, 2 * rows, D),
            down_sum.reshape(wide_count, -1, D),
            hout_sum.reshape(wide_count, -1, D),
            tap_part.reshape(wide_count, -1, D),
        ],
        axis=1,
    )
    pad = -grads.shape[1] % 16
    grads = jnp.pad(grads, ((0, 0), (0, pad), (0, 0))).astype(BF16)
    grads, grad_attended = lax.optimization_barrier((grads, grad_attended))
    mine = lax.psum_scatter(grads, "wide", scatter_dimension=0, tiled=False)

    gq, gkv, gkv_other = attention_back(scal, q, kv, kv_other, attended, grad_attended, logs)
    gmixed, hin_grad = project_back(gq, gkv, swap(gkv_other), mixed, hin)
    gmixed_edge = swap(boundary(gmixed))
    input_grad, sums_one, mix_grad = back(
        scal, x, gmixed, gmixed_edge, base, shifted, grad_residual, perm_back, shifts, mod, mix_taps
    )

    modulation_two_grad = sums_two[:, 1:3].reshape(-1, 2 * D)
    own = D // cells
    hin_rows = 3 * rows
    hin_parts = hin_grad.reshape(2, -1, wide_count, rows, 6 * HS).transpose(0, 2, 1, 3, 4)
    hin_parts = hin_parts.reshape(2, wide_count, hin_rows, 6 * HS)
    hin_parts = jnp.pad(hin_parts, ((0, 0), (0, 0), (0, -hin_rows % 16), (0, 0)))
    mix_parts = mix_grad[:9].T.reshape(wide_count, 2, 1, own * 9).transpose(1, 0, 2, 3)
    mix_parts = jnp.where(place == 0, mix_parts, mix_parts[::-1]).astype(BF16)
    mix_parts = jnp.pad(mix_parts, ((0, 0), (0, 0), (0, 15), (0, 6 * HS - own * 9)))
    parts = jnp.concatenate([hin_parts, mix_parts], axis=2)
    slope = jax.vjp(jax.nn.silu, embedded)[1](jnp.ones_like(embedded))[0]
    blocks = jnp.concatenate([sums_one[:, 0:2], sums_two[:, 0:4]], axis=1).transpose(1, 0, 2).reshape(12, D)
    digits = jnp.stack([labels // 32, labels % 32], axis=1).astype(F32)
    digits = jnp.pad(digits, ((0, 14), (0, 126)))
    sent = jnp.concatenate([jnp.concatenate([blocks, cond_low.astype(F32), slope], axis=0), digits], axis=1)
    summed, everyone = reduce_gather(parts, sent.astype(BF16))
    everyone = everyone.transpose(1, 0, 2)
    all_modulation = everyone[:12, :, :D].reshape(6, 2, -1, D)
    mine_columns = lax.dynamic_slice_in_dim(everyone[12:, :, :D], cell * own, own, 2)
    all_cond = mine_columns[:2]
    all_slope = mine_columns[2:].astype(F32)
    all_digits = everyone[:2, :, D : D + 2].astype(jnp.int32)
    all_labels = (all_digits[..., 0] * 32 + all_digits[..., 1])[..., None]
    modulator_mine = jnp.einsum("fcd,kfcl->dkl", all_cond, all_modulation, preferred_element_type=F32).reshape(own, -1)
    modulator_rows = lax.dynamic_slice_in_dim(modulator, cell * own, own, 0).reshape(own, 6, D)
    all_embedded = all_slope * jnp.einsum(
        "kfcl,dkl->fcd", all_modulation, modulator_rows, preferred_element_type=F32
    )
    chosen = (all_labels == jnp.arange(class_table.shape[1], dtype=jnp.int32)).astype(F32)
    class_mine = jnp.einsum(
        "fcd,fck->dk", all_embedded, chosen, precision=lax.Precision.HIGHEST, preferred_element_type=F32
    )
    mix_mine = summed[-16, : own * 9].reshape(own, 9)
    hin_mine = summed[:hin_rows].reshape(-1, rows, 6 * HS)
    mine = mine.astype(F32)

    at = 2 * rows
    up_mine = jnp.concatenate([mine[:rows], mine[rows:at]], axis=1)
    down_mine = mine[at : at + half // wide_count]
    at += half // wide_count
    hout_mine = mine[at : at + D // 2 // wide_count]
    at += D // 2 // wide_count
    hidden = half // wide_count
    taps_mine = mine[at:].reshape(-1)[: hidden * 9].reshape(hidden, 9)
    shards = (
        modulator_mine, class_mine, mix_mine, head_columns(hin_mine),
        hout_mine, up_mine, taps_mine, down_mine,
    )
    square = square_sum(wide_count, shards)
    grad_norm = jnp.sqrt(square[0, 0])
    step_rates = (
        D ** (-0.5), 1.0, 1.0 / 3.0, D ** (-0.5), (D // 32) ** (-0.5), D ** (-0.5), 1.0 / 3.0, FF ** (-0.5),
    )
    flat = adamw(square, shards, states, step_rates)
    return (output, input_grad, grad_norm, *flat, modulation_two_grad)


def solution(mesh):
    both = P(("wide", "narrow"), None)
    turned = P(("narrow", "wide"), None)
    grid = P("wide", "narrow")
    places = (both, both, both, grid, turned, grid, turned, turned)
    in_specs = (
        both, both, P("wide"), P(("wide", "narrow")), P(("wide", "narrow")),
        P(), P(), P(), P(None, "narrow"), P("narrow", None), P(None, "narrow"), P("narrow", None), P("narrow", None),
        *[place for place in places for _ in range(3)],
    )
    out_specs = (both, both, P(), *[place for place in places for _ in range(4)], both)
    return jax.shard_map(per_device, mesh=mesh, in_specs=in_specs, out_specs=out_specs, check_vma=False)
```

```python
import functools

import jax
import jax.numpy as jnp
from jax import lax
from jax.experimental import pallas as pl
from jax.experimental.pallas import tpu as pltpu
from jax.sharding import PartitionSpec as P

D = 768
HS = 64
FF = 3072
SIDE = 32
STEP = 10
PARAMS = 11419392

NORM_EPS = 1e-06
BETA_ONE = 0.5
BETA_TWO = 0.5
ADAM_EPS = 1e-08
WEIGHT_DECAY = 0.01

F32 = jnp.float32
BF16 = jnp.bfloat16

BODY = 512
HALF = 256
EDGE = 32
PLANE = 592
CHUNK = 256
VMEM_BYTES = 60 * 1024 * 1024


def params(*semantics):
    return pltpu.CompilerParams(
        dimension_semantics=semantics or None, vmem_limit_bytes=VMEM_BYTES
    )


def nn(left, right):
    return lax.dot_general(left, right, (((1,), (0,)), ((), ())), preferred_element_type=F32)


def nt(left, right):
    return lax.dot_general(left, right, (((1,), (1,)), ((), ())), preferred_element_type=F32)


def tn(left, right):
    return lax.dot_general(left, right, (((0,), (0,)), ((), ())), preferred_element_type=F32)


def whole(shape):
    return pl.BlockSpec(shape, lambda *_: (0,) * len(shape), pipeline_mode=pl.Buffered(1))


def scalars():
    return pl.BlockSpec(memory_space=pltpu.SMEM)


def geometry(scal_ref):
    return scal_ref[0], scal_ref[1], scal_ref[2] == 1, scal_ref[3]


def body_offset(half, gap):
    return pl.multiple_of(EDGE + half * (HALF + gap), 16)


def edge_offset(place):
    return pl.multiple_of(jnp.where(place == 0, EDGE + BODY, 0), 16)


def normalize(fields):
    center = fields - jnp.mean(fields, -1, keepdims=True)
    inverse = lax.rsqrt(jnp.mean(center * center, -1, keepdims=True) + NORM_EPS)
    return center * inverse, inverse


def norm_back(grad_hat, normed, inverse):
    return inverse * (
        grad_hat
        - jnp.mean(grad_hat, -1, keepdims=True)
        - normed * jnp.mean(grad_hat * normed, -1, keepdims=True)
    )


def variants(base, shifted, offset, width, rows, lanes):
    up = pl.multiple_of(offset - width, 16)
    down = pl.multiple_of(offset + width, 16)
    found = {}
    for part, shift, where in ((0, 0, offset), (0, 1, down), (1, 0, offset), (1, -1, up)):
        for column in (0, 1):
            at = (2 * part + column, pl.ds(where, rows), lanes)
            found[part, shift, column, 0] = base[at].astype(F32)
            found[part, shift, column, 1] = shifted[at].astype(F32)
    return found


def tap(found, p, q, a, b):
    part, shift = ((1, -1), (0, 0), (1, 0))[a + 1] if p == 0 else ((0, 0), (1, 0), (0, 1))[a + 1]
    column, moved = ((1, 1), (0, 0), (1, 0))[b + 1] if q == 0 else ((0, 0), (1, 0), (0, 1))[b + 1]
    return found[part, shift, column, moved]


def conv_at(found, kernel, p, q, flip=False):
    total = None
    for a in (-1, 0, 1):
        for b in (-1, 0, 1):
            index = 3 * (a + 1) + (b + 1)
            term = tap(found, p, q, a, b) * kernel[8 - index if flip else index]
            total = term if total is None else total + term
    return total


def kernel_rows(kernel_ref, lanes, rows):
    return [
        jnp.broadcast_to(kernel_ref[index : index + 1, lanes].astype(F32), (rows, lanes.size)) for index in range(9)
    ]


def clear_borders(plane, wide_gap=True):
    zeros = jnp.zeros((4, EDGE, plane.shape[2]), plane.dtype)
    plane[:, 0:EDGE, :] = zeros
    plane[:, EDGE + HALF : EDGE + HALF + EDGE, :] = zeros
    plane[:, EDGE + BODY : EDGE + BODY + EDGE, :] = zeros
    plane[:, PLANE - EDGE : PLANE, :] = zeros


def column_masks(rows, width):
    column = lax.broadcasted_iota(jnp.int32, (rows, 128), 0) & (width - 1)
    return column != width - 1, column != 0


def moved_rows(value, column, masks):
    rows, lanes = value.shape
    moved = pltpu.roll(value, rows - 1 if column == 0 else 1, 0)
    parts = [jnp.where(masks[column], moved[:, at : at + 128], 0.0) for at in range(0, lanes, 128)]
    return parts[0] if len(parts) == 1 else jnp.concatenate(parts, axis=1)


def own_half(half):
    return lambda i: jnp.minimum(i, half - 1)


def other_half(half):
    return lambda i: jnp.maximum(i - half, 0)


def front_kernel(
    scal_ref, x_ref, edge_ref, perm_ref, edge_perm_ref, mod_ref, taps_ref, order_ref, weight_ref,
    x_out, mixed_out, base_out, shifted_out, q_out, kv_out,
):
    width, gap, long_latent, place = geometry(scal_ref)
    @pl.when(pl.program_id(0) == 0)
    def _():
        clear_borders(base_out)
        clear_borders(shifted_out)
        masks = column_masks(64, width)
        edge_masks = column_masks(EDGE, width)

        @pl.loop(0, 8, unroll=2)
        def _(block):
            half = block // 4
            rows = x_ref[pl.ds(pl.multiple_of(block * 256, 256), 256), :]
            shift = mod_ref[half, 0:1, :]
            scale = mod_ref[half, 1:2, :]
            place_in = pl.ds(pl.multiple_of(block * 64, 64), 64)
            place_out = pl.ds(pl.multiple_of(body_offset(half, gap) + (block % 4) * 64, 16), 64)
            for group in range(4):
                picked = nn(perm_ref[64 * group : 64 * group + 64, :], rows)
                x_out[group, place_in, :] = picked.astype(BF16)
                normed = normalize(picked)[0]
                value = normed * (1.0 + scale) + shift
                base_out[group, place_out, :] = value.astype(BF16)
                shifted_out[group, place_out, :] = moved_rows(value, group % 2, masks).astype(BF16)

        @pl.when(long_latent)
        def _():
            at = pl.ds(edge_offset(place), EDGE)
            for group in range(4):
                picked = nn(edge_perm_ref[32 * group : 32 * group + 32, :], edge_ref[...])
                normed = normalize(picked)[0]
                value = normed * (1.0 + mod_ref[0, 1:2, :]) + mod_ref[0, 0:1, :]
                base_out[group, at, :] = value.astype(BF16)
                shifted_out[group, at, :] = moved_rows(value, group % 2, edge_masks).astype(BF16)

        for lane in range(D // 128):
            lanes = pl.ds(lane * 128, 128)
            kernel = kernel_rows(taps_ref, lanes, 16)

            @pl.loop(0, 32, unroll=4)
            def _(tile, lanes=lanes, kernel=kernel):
                offset = body_offset(tile // 16, gap) + (tile % 16) * 16
                found = variants(base_out, shifted_out, pl.multiple_of(offset, 16), width, 16, lanes)
                for p in (0, 1):
                    for q in (0, 1):
                        at = (2 * p + q, pl.ds(pl.multiple_of(tile * 16, 16), 16), lanes)
                        mixed_out[at] = conv_at(found, kernel, p, q).astype(BF16)

    project_kernel(mixed_out, order_ref, weight_ref, q_out, kv_out)


def project_kernel(mixed_ref, order_ref, weight_ref, q_out, kv_out):
    weight = nn(weight_ref[...], order_ref[...]).astype(BF16)
    for group in range(4):
        triple = nn(mixed_ref[group], weight)
        q_out[0, group] = (triple[:, 0:128] * (HS**-0.5)).astype(BF16)
        kv_out[0, 0, group] = triple[:, 128:256].astype(BF16)
        kv_out[0, 1, group] = triple[:, 256:384].astype(BF16)


def project_specs(pairs):
    shapes = (
        jax.ShapeDtypeStruct((pairs, 4, BODY, 128), BF16),
        jax.ShapeDtypeStruct((pairs, 2, 4, BODY, 128), BF16),
    )
    blocks = (
        pl.BlockSpec((1, 4, BODY, 128), lambda i: (i, 0, 0, 0)),
        pl.BlockSpec((1, 2, 4, BODY, 128), lambda i: (i, 0, 0, 0, 0)),
    )
    return shapes, blocks, pl.BlockSpec((D, 384), lambda i: (0, i))


def front(scal, x, edge, perm, edge_perm, mod, taps, order, weight):
    pairs = weight.shape[1] // 384
    shapes, blocks, weight_block = project_specs(pairs)
    plane = jax.ShapeDtypeStruct((4, PLANE, D), BF16)
    body = jax.ShapeDtypeStruct((4, BODY, D), BF16)
    return pl.pallas_call(
        front_kernel,
        grid=(pairs,),
        out_shape=(body, body, plane, plane, *shapes),
        in_specs=[
            scalars(), whole(x.shape), whole(edge.shape), whole(perm.shape), whole(edge_perm.shape),
            whole(mod.shape), whole(taps.shape), whole(order.shape), weight_block,
        ],
        out_specs=(whole(body.shape), whole(body.shape), whole(plane.shape), whole(plane.shape), *blocks),
        compiler_params=params("arbitrary"),
        name="front",
    )(scal, x, edge, perm, edge_perm, mod, taps, order, weight)


def project(mixed, order, weight):
    pairs = weight.shape[1] // 384
    shapes, blocks, weight_block = project_specs(pairs)
    return pl.pallas_call(
        project_kernel,
        grid=(pairs,),
        out_shape=shapes,
        in_specs=[whole(mixed.shape), whole(order.shape), weight_block],
        out_specs=blocks,
        compiler_params=params("arbitrary"),
        name="project",
    )(mixed, order, weight)


def head_mask(rows, head):
    lane = lax.broadcasted_iota(jnp.int32, (rows, 128), 1)
    return (lane < HS) if head == 0 else (lane >= HS)


def pieces(first, second, rows):
    lane = lax.broadcasted_iota(jnp.int32, (rows, 128), 1)
    value = jnp.where(lane < HS, first, second)
    one = value.astype(BF16).astype(F32)
    two = (value - one).astype(BF16).astype(F32)
    three = value - one - two
    turn = lane % HS
    picked = jnp.where(turn == 0, one, jnp.where(turn == 1, two, jnp.where(turn == 2, three, 0.0)))
    return picked.astype(BF16)


def unit_pieces(rows):
    lane = lax.broadcasted_iota(jnp.int32, (rows, 128), 1)
    return jnp.where(lane % HS < 3, 1.0, 0.0).astype(BF16)


def attend_kernel(scal_ref, q_ref, own_ref, other_ref, out_ref, log_ref):
    long_latent = scal_ref[2] == 1

    def attend(query, keys, values, rows):
        mixes, logs = [], []
        for head in (0, 1):
            masked = jnp.where(head_mask(rows, head), query, jnp.zeros_like(query))
            scores = [nt(masked, key) for key in keys]
            highest = jnp.max(scores[0], -1, keepdims=True)
            for other in scores[1:]:
                highest = jnp.maximum(highest, jnp.max(other, -1, keepdims=True))
            mix = None
            for score, value in zip(scores, values):
                share = jnp.exp(score - highest).astype(BF16)
                part = nn(share, value)
                mix = part if mix is None else mix + part
            total = mix[:, 128:256]
            mixes.append(mix[:, 0:128] / total)
            logs.append(highest + jnp.log(total))
        mix = jnp.where(head_mask(rows, 0), mixes[0], mixes[1])
        return mix.astype(BF16), pieces(-logs[0], -logs[1], rows)

    def with_ones(value):
        return jnp.concatenate([value, jnp.ones_like(value)], axis=1)

    @pl.when(long_latent)
    def _():
        for tile in range(2):
            at = pl.ds(tile * 256, 256)
            out_ref[0, at, :], log_ref[0, 0, at, :] = attend(
                q_ref[0, 0, at, :],
                [own_ref[0, 0, 0], other_ref[0, 0, 0]],
                [with_ones(own_ref[0, 1, 0]), with_ones(other_ref[0, 1, 0])],
                256,
            )

    @pl.when(jnp.logical_not(long_latent))
    def _():
        for tile in range(2):
            at = pl.ds(tile * 256, 256)
            out_ref[0, at, :], log_ref[0, 0, at, :] = attend(
                q_ref[0, 0, at, :],
                [own_ref[0, 0, 0, at, :]],
                [with_ones(own_ref[0, 1, 0, at, :])],
                256,
            )


def attention(scal, q, own, other):
    pairs = q.shape[0]
    pair_spec = pl.BlockSpec((1, 1, BODY, 128), lambda p, g: (p, g, 0, 0))
    kv_spec = pl.BlockSpec((1, 2, 1, BODY, 128), lambda p, g: (p, 0, g, 0, 0))
    return pl.pallas_call(
        attend_kernel,
        grid=(pairs, 4),
        out_shape=(
            jax.ShapeDtypeStruct((4, BODY, 128 * pairs), BF16),
            jax.ShapeDtypeStruct((pairs, 4, BODY, 128), BF16),
        ),
        in_specs=[scalars(), pair_spec, kv_spec, kv_spec],
        out_specs=(pl.BlockSpec((1, BODY, 128), lambda p, g: (g, 0, p)), pair_spec),
        compiler_params=params("arbitrary", "arbitrary"),
        name="attention",
    )(scal, q, own, other)


def attend_back_kernel(
    scal_ref, q_ref, own_ref, other_ref, mix_ref, grad_ref, log_ref, gq_ref, gown_ref, gother_ref
):
    long_latent = scal_ref[2] == 1

    def side(query, mix, grad, log):
        rows = query.shape[0]
        product = mix.astype(F32) * grad.astype(F32)
        deltas = [
            jnp.sum(jnp.where(head_mask(rows, head), product, 0.0), -1, keepdims=True) for head in (0, 1)
        ]
        delta = pieces(-deltas[0], -deltas[1], rows)
        result = []
        for head in (0, 1):
            mask = head_mask(rows, head)
            zero = jnp.zeros_like(query)
            q_head = jnp.where(mask, query, zero)
            g_head = jnp.where(mask, grad, zero)
            q_more = jnp.concatenate([q_head, jnp.where(mask, log, zero)], axis=1)
            g_more = jnp.concatenate([g_head, jnp.where(mask, delta, zero)], axis=1)
            result.append((q_head, g_head, q_more, g_more))
        return result

    def keys_part(heads, key, value):
        rows = key.shape[0]
        ones = unit_pieces(rows)
        key_more = jnp.concatenate([key, ones], axis=1)
        value_more = jnp.concatenate([value, ones], axis=1)
        key_turned = key.astype(F32).T.astype(BF16)
        gk = gv = None
        turned = []
        for q_head, g_head, q_more, g_more in heads:
            share = jnp.exp(nt(key_more, q_more))
            slope = (share * nt(value_more, g_more)).astype(BF16)
            share = share.astype(BF16)
            gv_part = nn(share, g_head)
            gk_part = nn(slope, q_head)
            gv = gv_part if gv is None else gv + gv_part
            gk = gk_part if gk is None else gk + gk_part
            turned.append(nn(key_turned, slope))
        return gk, gv, turned

    def query_grad(turned):
        row = lax.broadcasted_iota(jnp.int32, turned[0].shape, 0)
        both = jnp.where(row < HS, turned[0], turned[1]) * (HS**-0.5)
        return both.T.astype(BF16)

    @pl.when(long_latent)
    def _():
        heads = side(q_ref[0, 0], mix_ref[0], grad_ref[0], log_ref[0, 0])
        totals = None
        for source, target in ((own_ref, gown_ref), (other_ref, gother_ref)):
            for tile in range(2):
                at = pl.ds(tile * 256, 256)
                gk, gv, turned = keys_part(heads, source[0, 0, 0, at, :], source[0, 1, 0, at, :])
                target[0, 0, 0, at, :] = gk.astype(BF16)
                target[0, 1, 0, at, :] = gv.astype(BF16)
                totals = turned if totals is None else [a + b for a, b in zip(totals, turned)]
        gq_ref[0, 0] = query_grad(totals)

    @pl.when(jnp.logical_not(long_latent))
    def _():
        for tile in range(2):
            at = pl.ds(tile * 256, 256)
            heads = side(q_ref[0, 0, at, :], mix_ref[0, at, :], grad_ref[0, at, :], log_ref[0, 0, at, :])
            gk, gv, turned = keys_part(heads, own_ref[0, 0, 0, at, :], own_ref[0, 1, 0, at, :])
            gown_ref[0, 0, 0, at, :] = gk.astype(BF16)
            gown_ref[0, 1, 0, at, :] = gv.astype(BF16)
            gq_ref[0, 0, at, :] = query_grad(turned)
        gother_ref[...] = jnp.zeros_like(gother_ref)


def attention_back(scal, q, own, other, mix, grad, log):
    pairs = q.shape[0]
    pair_spec = pl.BlockSpec((1, 1, BODY, 128), lambda p, g: (p, g, 0, 0))
    kv_spec = pl.BlockSpec((1, 2, 1, BODY, 128), lambda p, g: (p, 0, g, 0, 0))
    lane_spec = pl.BlockSpec((1, BODY, 128), lambda p, g: (g, 0, p))
    return pl.pallas_call(
        attend_back_kernel,
        grid=(pairs, 4),
        out_shape=(
            jax.ShapeDtypeStruct(q.shape, BF16),
            jax.ShapeDtypeStruct(own.shape, BF16),
            jax.ShapeDtypeStruct(own.shape, BF16),
        ),
        in_specs=[scalars(), pair_spec, kv_spec, kv_spec, lane_spec, lane_spec, pair_spec],
        out_specs=(pair_spec, kv_spec, kv_spec),
        compiler_params=params("arbitrary", "arbitrary"),
        name="attention_back",
    )(scal, q, own, other, mix, grad, log)


def middle_kernel(
    x_ref, mix_own, mix_other, cot_ref, perm_ref, mod_ref, own_ref, other_ref, attn_out, norm_out, cot_out, grad_out
):
    gate_one = mod_ref[0, 2:3, :]
    shift = mod_ref[0, 3:4, :]
    scale = mod_ref[0, 4:5, :]
    gate_two = mod_ref[0, 5:6, :]
    for group in range(4):
        attn = nn(mix_own[group], own_ref[...]) + nn(mix_other[group], other_ref[...])
        attn_low = attn.astype(BF16)
        attn_out[group] = attn_low
        residual = x_ref[group].astype(F32) + gate_one * attn_low.astype(F32)
        norm_out[group] = (normalize(residual)[0] * (1.0 + scale) + shift).astype(BF16)
        cot = nn(perm_ref[64 * group : 64 * group + 64, :], cot_ref[...])
        cot_out[group] = cot.astype(BF16)
        grad_out[group] = (cot * gate_two).astype(BF16)


def middle(x, mix, mix_other, cot, perm, mod, weight, weight_other):
    part = pl.BlockSpec((4, 64, D // 2), lambda i: (0, i, 0))
    block = pl.BlockSpec((4, 64, D), lambda i: (0, i, 0))
    body = jax.ShapeDtypeStruct((4, BODY, D), BF16)
    return pl.pallas_call(
        middle_kernel,
        grid=(8,),
        out_shape=(body,) * 4,
        in_specs=[
            block, part, part, pl.BlockSpec((256, D), lambda i: (i, 0)), whole(perm.shape),
            pl.BlockSpec((1, 8, D), lambda i: (i // 4, 0, 0)), whole(weight.shape), whole(weight.shape),
        ],
        out_specs=(block,) * 4,
        compiler_params=params("arbitrary"),
        name="middle",
    )(x, mix, mix_other, cot, perm, mod, weight, weight_other)


def gelu_both(value):
    root = 0.7978845608028654
    square = value * value
    angle = value * (root + (root * 0.044715) * square)
    bent = jnp.tanh(angle)
    half = 0.5 + 0.5 * bent
    inner = (0.5 * root) + (1.5 * root * 0.044715) * square
    return value * half, half + value * (1.0 - bent * bent) * inner


def ffn_kernel(
    scal_ref, taps_own, taps_other, norm_ref, norm_edge, grad_ref, grad_edge,
    up_own, up_other, down_own, down_other,
    ffn_out, back_out, up_grad_own, up_grad_other, down_grad_own, down_grad_other, taps_grad,
    hid, hid_moved, gc, gc_moved, act, gh, da, da_edge, ffn_sum, back_sum, up, down, taps, norm_turned, grad_turned, tap_sums,
):
    width, gap, long_latent, place = geometry(scal_ref)
    step = pl.program_id(0)
    steps = pl.num_programs(0)

    @pl.when(step < steps // 2)
    def _():
        up[...] = up_own[...]
        down[...] = down_own[...]
        taps[...] = taps_own[...].astype(F32)

    @pl.when(step >= steps // 2)
    def _():
        up[...] = up_other[...]
        down[...] = down_other[...]
        taps[...] = taps_other[...].astype(F32)

    @pl.when(step == 0)
    def _():
        for plane in (hid, hid_moved, gc, gc_moved):
            clear_borders(plane)

        @pl.loop(0, 8)
        def _(tile):
            rows = pl.ds(pl.multiple_of((tile % 2) * HALF, HALF), HALF)
            cols = pl.ds(pl.multiple_of(tile * HALF, HALF), HALF)
            norm_turned[:, cols] = norm_ref[tile // 2, rows, :].T
            grad_turned[:, cols] = grad_ref[tile // 2, rows, :].T
            ffn_sum[tile // 2, rows, :] = jnp.zeros((HALF, D), F32)
            back_sum[tile // 2, rows, :] = jnp.zeros((HALF, D), F32)

    masks = column_masks(BODY, width)
    edge_masks = column_masks(EDGE, width)

    for group in range(4):
        value = nn(norm_ref[group], up[...])
        moved = moved_rows(value, group % 2, masks)
        for half in (0, 1):
            at = (group, pl.ds(body_offset(half, gap), HALF), slice(None))
            hid[at] = value[half * HALF : (half + 1) * HALF]
            hid_moved[at] = moved[half * HALF : (half + 1) * HALF]
        da[group] = nt(grad_ref[group], down[...]).astype(BF16)

    @pl.when(long_latent)
    def _():
        for group in range(4):
            at = (group, pl.ds(edge_offset(place), EDGE), slice(None))
            value = nn(norm_edge[group], up[...])
            hid[at] = value
            hid_moved[at] = moved_rows(value, group % 2, edge_masks)
            da_edge[group] = nt(grad_edge[group], down[...]).astype(BF16)

    def plane_rows(block, row):
        return pl.multiple_of(body_offset(block // 4, gap) + (block % 4) * 64 + row, 16)

    def accumulate(total, left, right, block):
        rows = slice(64 * block, 64 * block + 64)
        part = nn(left[:, rows, :].reshape(256, CHUNK), right)
        total[:, rows, :] += part.reshape(4, 64, D)

    down_now = down[...]
    up_turned = up[...].T

    for block in range(8):
        for lane in range(CHUNK // 128):
            lanes = pl.ds(lane * 128, 128)
            kernel = kernel_rows(taps, lanes, 16)
            for tile in (0, 32):
                grads = [[] for _ in range(4)]
                for part in (0, 16):
                    offset = plane_rows(block, tile + part)
                    rows = pl.ds(block * 64 + tile + part, 16)
                    found = variants(hid, hid_moved, offset, width, 16, lanes)
                    for p in (0, 1):
                        for q in (0, 1):
                            group = 2 * p + q
                            value, slope = gelu_both(conv_at(found, kernel, p, q))
                            act[group, rows, lanes] = value.astype(BF16)
                            grads[group].append(slope * da[group, rows, lanes].astype(F32))
                at = pl.ds(plane_rows(block, tile), 32)
                for group in range(4):
                    grad = jnp.concatenate(grads[group], axis=0)
                    gc[group, at, lanes] = grad
                    gc_moved[group, at, lanes] = moved_rows(grad, group % 2, edge_masks)
        if block > 0:
            accumulate(ffn_sum, act, down_now, block - 1)
    accumulate(ffn_sum, act, down_now, 7)

    for side in (0, 1):

        @pl.when(jnp.logical_and(long_latent, place == side))
        def _(side=side):
            for lane in range(CHUNK // 128):
                lanes = pl.ds(lane * 128, 128)
                kernel = kernel_rows(taps, lanes, 32)
                offset = EDGE + BODY if side == 0 else 0
                found = {}
                for part, shift, where in ((0, 0, offset), (0, 1, offset + EDGE), (1, 0, offset), (1, -1, offset - EDGE)):
                    if where < 0 or where + 32 > PLANE:
                        continue
                    for column in (0, 1):
                        at = (2 * part + column, slice(where, where + 32), lanes)
                        found[part, shift, column, 0] = hid[at]
                        found[part, shift, column, 1] = hid_moved[at]
                for q in (0, 1):
                    group = 2 * side + q
                    slope = gelu_both(conv_at(found, kernel, side, q))[1]
                    grad = slope * da_edge[group, :, lanes].astype(F32)
                    gc[group, offset : offset + 32, lanes] = grad
                    gc_moved[group, offset : offset + 32, lanes] = moved_rows(grad, q, edge_masks)

    tap_sums[...] = jnp.zeros_like(tap_sums)
    for block in range(8):
        for lane in range(CHUNK // 128):
            lanes = pl.ds(lane * 128, 128)
            kernel = kernel_rows(taps, lanes, 16)
            totals = None
            for tile in range(0, 64, 16):
                offset = plane_rows(block, tile)
                rows = pl.ds(block * 64 + tile, 16)
                found = variants(gc, gc_moved, offset, width, 16, lanes)
                for p in (0, 1):
                    for q in (0, 1):
                        gh[2 * p + q, rows, lanes] = conv_at(found, kernel, p, q, flip=True).astype(BF16)
                parts = taps_at(found, variants(hid, hid_moved, offset, width, 16, lanes))
                totals = parts if totals is None else [total + more for total, more in zip(totals, parts)]
            for index, total in enumerate(totals):
                tap_sums[lane, index] += total
        if block > 0:
            accumulate(back_sum, gh, up_turned, block - 1)
    accumulate(back_sum, gh, up_turned, 7)
    for lane in range(CHUNK // 128):
        for index in range(9):
            taps_grad[0, index : index + 1, lane * 128 : (lane + 1) * 128] = jnp.sum(tap_sums[lane, index], 0, keepdims=True)

    def weight_grads(up_grad, down_grad):
        down_grad[...] = nn(grad_turned[...], act[...].reshape(4 * BODY, CHUNK)).T.astype(BF16)
        up_grad[0] = nn(norm_turned[...], gh[...].reshape(4 * BODY, CHUNK)).astype(BF16)

    @pl.when(step < steps // 2)
    def _():
        weight_grads(up_grad_own, down_grad_own)

    @pl.when(step >= steps // 2)
    def _():
        weight_grads(up_grad_other, down_grad_other)

    @pl.when(step == steps - 1)
    def _():
        ffn_out[...] = ffn_sum[...].astype(BF16)
        back_out[...] = back_sum[...].astype(BF16)


def taps_at(grads, fields):
    sums = []
    for a in (-1, 0, 1):
        for b in (-1, 0, 1):
            total = None
            for p in (0, 1):
                for q in (0, 1):
                    term = grads[p, 0, q, 0] * tap(fields, p, q, a, b)
                    total = term if total is None else total + term
            sums.append(sum(total[at : at + 8] for at in range(0, total.shape[0], 8)))
    return sums


def feed_forward(scal, taps_own, taps_other, norm, norm_edge, grad, grad_edge, up_own, up_other, down_own, down_other):
    half = up_own.shape[1] // CHUNK
    steps = 2 * half
    body = jax.ShapeDtypeStruct((4, BODY, D), BF16)

    own, other = own_half(half), other_half(half)
    per = D // CHUNK
    plane = pltpu.VMEM((4, PLANE, CHUNK), F32)
    small = pltpu.VMEM((4, BODY, CHUNK), BF16)
    return pl.pallas_call(
        ffn_kernel,
        grid=(steps,),
        out_shape=(
            body, body,
            *[jax.ShapeDtypeStruct((half // per, D, D), BF16)] * 2,
            *[jax.ShapeDtypeStruct((half * CHUNK, D), BF16)] * 2,
            jax.ShapeDtypeStruct((steps, 16, CHUNK), F32),
        ),
        in_specs=[
            scalars(),
            pl.BlockSpec((16, CHUNK), lambda i: (0, own(i))),
            pl.BlockSpec((16, CHUNK), lambda i: (0, other(i))),
            whole(norm.shape), whole(norm_edge.shape), whole(grad.shape), whole(grad_edge.shape),
            pl.BlockSpec((D, CHUNK), lambda i: (0, own(i))),
            pl.BlockSpec((D, CHUNK), lambda i: (0, other(i))),
            pl.BlockSpec((CHUNK, D), lambda i: (own(i), 0)),
            pl.BlockSpec((CHUNK, D), lambda i: (other(i), 0)),
        ],
        out_specs=(
            whole(body.shape), whole(body.shape),
            pl.BlockSpec((1, D, CHUNK), lambda i: (own(i) // per, 0, own(i) % per)),
            pl.BlockSpec((1, D, CHUNK), lambda i: (other(i) // per, 0, other(i) % per)),
            pl.BlockSpec((CHUNK, D), lambda i: (own(i), 0)),
            pl.BlockSpec((CHUNK, D), lambda i: (other(i), 0)),
            pl.BlockSpec((1, 16, CHUNK), lambda i: (i, 0, 0)),
        ),
        scratch_shapes=[
            plane, plane, plane, plane, small, small, small, pltpu.VMEM((4, EDGE, CHUNK), BF16),
            pltpu.VMEM((4, BODY, D), F32), pltpu.VMEM((4, BODY, D), F32),
            pltpu.VMEM((D, CHUNK), BF16), pltpu.VMEM((CHUNK, D), BF16), pltpu.VMEM((16, CHUNK), F32),
            pltpu.VMEM((D, 4 * BODY), BF16), pltpu.VMEM((D, 4 * BODY), BF16),
            pltpu.VMEM((CHUNK // 128, 9, 8, 128), F32),
        ],
        compiler_params=params("arbitrary"),
        name="feed_forward",
    )(scal, taps_own, taps_other, norm, norm_edge, grad, grad_edge, up_own, up_other, down_own, down_other)


def turn_kernel(
    x_ref, attn_ref, ffn_ref, cot_ref, back_ref, mix_own, mix_other, perm_ref, mod_ref, own_ref, other_ref,
    out_ref, grad_ref, gmix_own, gmix_other, sums_ref, wgrad_own, wgrad_other,
    wsum,
):
    step = pl.program_id(0)
    gate_one = mod_ref[0, 2:3, :]
    scale = mod_ref[0, 4:5, :]
    gate_two = mod_ref[0, 5:6, :]

    @pl.when(step % 4 == 0)
    def _():
        sums_ref[...] = jnp.zeros_like(sums_ref)

    @pl.when(step == 0)
    def _():
        wsum[...] = jnp.zeros_like(wsum)

    result = None
    gattns = []
    for group in range(4):
        attn = attn_ref[group].astype(F32)
        ffn = ffn_ref[group].astype(F32)
        cot = cot_ref[group].astype(F32)
        back = back_ref[group].astype(F32)
        residual = x_ref[group].astype(F32) + gate_one * attn
        low = (residual + gate_two * ffn).astype(BF16)
        part = nn(perm_ref[:, 64 * group : 64 * group + 64], low)
        result = part if result is None else result + part
        normed, inverse = normalize(residual)
        grad = cot + norm_back(back * (1.0 + scale), normed, inverse)
        grad_ref[group] = grad.astype(BF16)
        for row, value in ((0, grad * attn), (1, back), (2, back * normed), (3, cot * ffn)):
            sums_ref[0, row : row + 1, :] += jnp.sum(value, 0, keepdims=True)
        gattn = (grad * gate_one).astype(BF16)
        gattns.append(gattn)
    gattn = jnp.concatenate(gattns, axis=0)
    for index, (mix, weight, gmix) in enumerate(((mix_own, own_ref, gmix_own), (mix_other, other_ref, gmix_other))):
        gmix[...] = nt(gattn, weight[...]).astype(BF16).reshape(4, 64, D // 2)
        wsum[index] += tn(mix[...].reshape(256, D // 2), gattn)
    out_ref[...] = result.astype(BF16)

    @pl.when(step == 7)
    def _():
        wgrad_own[...] = wsum[0].astype(BF16)
        wgrad_other[...] = wsum[1].astype(BF16)


def turn(x, attn, ffn, cot, back, mix, mix_other, perm, mod, weight, weight_other):
    block = pl.BlockSpec((4, 64, D), lambda i: (0, i, 0))
    part = pl.BlockSpec((4, 64, D // 2), lambda i: (0, i, 0))
    body = jax.ShapeDtypeStruct((4, BODY, D), BF16)
    half_body = jax.ShapeDtypeStruct((4, BODY, D // 2), BF16)
    half_weight = jax.ShapeDtypeStruct((D // 2, D), BF16)
    return pl.pallas_call(
        turn_kernel,
        grid=(8,),
        out_shape=(
            jax.ShapeDtypeStruct((2048, D), BF16), body, half_body, half_body,
            jax.ShapeDtypeStruct((2, 8, D), F32), half_weight, half_weight,
        ),
        in_specs=[block] * 5 + [part] * 2 + [
            whole(perm.shape), pl.BlockSpec((1, 8, D), lambda i: (i // 4, 0, 0)), whole(weight.shape), whole(weight.shape),
        ],
        out_specs=(
            pl.BlockSpec((256, D), lambda i: (i, 0)), block, part, part,
            pl.BlockSpec((1, 8, D), lambda i: (i // 4, 0, 0)), whole(weight.shape), whole(weight.shape),
        ),
        scratch_shapes=[pltpu.VMEM((2, D // 2, D), F32)],
        compiler_params=params("arbitrary"),
        name="turn",
    )(x, attn, ffn, cot, back, mix, mix_other, perm, mod, weight, weight_other)


def project_back_kernel(
    gq_own, gkv_own, add_own, gq_other, gkv_other, add_other, mixed_ref, order_ref, own_ref, other_ref,
    gmixed_ref, wgrad_own, wgrad_other,
    gsum, turned, triples, weights,
):
    step = pl.program_id(0)
    half_steps = pl.num_programs(0) // 2

    @pl.when(step == 0)
    def _():
        for tile in range(8):
            rows = slice((tile % 2) * HALF, (tile % 2 + 1) * HALF)
            turned[:, tile * HALF : (tile + 1) * HALF] = mixed_ref[tile // 2, rows, :].T

    def gather(gq_ref, gkv_ref, add_ref, weight_ref, pair):
        at = 384 * pair
        weights[:, at : at + 384] = nn(weight_ref[...], order_ref[...]).astype(BF16)
        for group in range(4):
            triples[group, :, at : at + 128] = gq_ref[0, group]
            for part in (0, 1):
                total = gkv_ref[0, part, group].astype(F32) + add_ref[0, part, group].astype(F32)
                triples[group, :, at + 128 * (part + 1) : at + 128 * (part + 2)] = total.astype(BF16)

    def finish(wgrad_ref, last):
        width = weights.shape[1]
        for group in range(4):
            part = nt(triples[group], weights[...])
            if last:
                gmixed_ref[group] = (gsum[group] + part).astype(BF16)
            else:
                gsum[group] = part
        wgrad = nn(turned[...], triples[...].reshape(4 * BODY, width)).astype(BF16)
        for at in range(0, width, 384):
            wgrad_ref[:, at : at + 384] = nt(wgrad[:, at : at + 384], order_ref[...]).astype(BF16)

    for half, refs in enumerate(((gq_own, gkv_own, add_own, own_ref), (gq_other, gkv_other, add_other, other_ref))):
        for pair in range(weights.shape[1] // 384):

            @pl.when(step == half * half_steps + pair)
            def _(refs=refs, pair=pair):
                gather(*refs, pair)

    @pl.when(step == half_steps - 1)
    def _():
        finish(wgrad_own, False)

    @pl.when(step == 2 * half_steps - 1)
    def _():
        finish(wgrad_other, True)


def project_back(own_grads, other_grads, mixed, order, weight, weight_other):
    half = own_grads[0].shape[0]
    own, other = own_half(half), other_half(half)

    def specs(at):
        kv_spec = pl.BlockSpec((1, 2, 4, BODY, 128), lambda i: (at(i), 0, 0, 0, 0))
        return [pl.BlockSpec((1, 4, BODY, 128), lambda i: (at(i), 0, 0, 0)), kv_spec, kv_spec]

    weight_specs = [pl.BlockSpec((D, 384), lambda i: (0, own(i))), pl.BlockSpec((D, 384), lambda i: (0, other(i)))]
    weight_shape = jax.ShapeDtypeStruct(weight.shape, BF16)
    return pl.pallas_call(
        project_back_kernel,
        grid=(2 * half,),
        out_shape=(jax.ShapeDtypeStruct((4, BODY, D), BF16), weight_shape, weight_shape),
        in_specs=[*specs(own), *specs(other), whole(mixed.shape), whole(order.shape), *weight_specs],
        out_specs=(whole((4, BODY, D)), whole(weight.shape), whole(weight.shape)),
        scratch_shapes=[
            pltpu.VMEM((4, BODY, D), F32), pltpu.VMEM((D, 4 * BODY), BF16),
            pltpu.VMEM((4, BODY, weight.shape[1]), BF16), pltpu.VMEM(weight.shape, BF16),
        ],
        compiler_params=params("arbitrary"),
        name="project_back",
    )(*own_grads, *other_grads, mixed, order, weight, weight_other)


def back_kernel(
    scal_ref, x_ref, gmixed_ref, gedge_ref, base_ref, shifted_ref, gres_ref, perm_ref, mod_ref, taps_ref,
    out_ref, sums_ref, taps_grad,
    gm, gm_moved, gnorm,
):
    width, gap, long_latent, place = geometry(scal_ref)
    clear_borders(gm)
    clear_borders(gm_moved)
    masks = column_masks(64, width)
    edge_masks = column_masks(EDGE, width)

    @pl.loop(0, 8)
    def _(block):
        place_in = pl.ds(pl.multiple_of(block * 64, 64), 64)
        place_out = pl.ds(pl.multiple_of(body_offset(block // 4, gap) + (block % 4) * 64, 16), 64)
        for group in range(4):
            value = gmixed_ref[group, place_in, :].astype(F32)
            gm[group, place_out, :] = value
            gm_moved[group, place_out, :] = moved_rows(value, group % 2, masks)

    @pl.when(long_latent)
    def _():
        at = pl.ds(edge_offset(place), EDGE)
        for group in range(4):
            value = gedge_ref[group].astype(F32)
            gm[group, at, :] = value
            gm_moved[group, at, :] = moved_rows(value, group % 2, edge_masks)

    for lane in range(D // 128):
        lanes = pl.ds(lane * 128, 128)
        kernel = kernel_rows(taps_ref, lanes, 16)

        def back_tile(tile, sums, lanes=lanes, kernel=kernel):
            offset = pl.multiple_of(body_offset(tile // 16, gap) + (tile % 16) * 16, 16)
            rows = pl.ds(pl.multiple_of(tile * 16, 16), 16)
            found = variants(gm, gm_moved, offset, width, 16, lanes)
            for p in (0, 1):
                for q in (0, 1):
                    gnorm[2 * p + q, rows, lanes] = conv_at(found, kernel, p, q, flip=True).astype(BF16)
            totals = taps_at(found, variants(base_ref, shifted_ref, offset, width, 16, lanes))
            return tuple(total + more for total, more in zip(sums, totals))

        sums = lax.fori_loop(0, 32, back_tile, (jnp.zeros((8, 128), F32),) * 9, unroll=2)
        for index in range(9):
            taps_grad[index : index + 1, lanes] = jnp.sum(sums[index], 0, keepdims=True)

    sums_ref[...] = jnp.zeros_like(sums_ref)

    @pl.loop(0, 8, unroll=2)
    def _(block):
        half = block // 4
        scale = mod_ref[half, 1:2, :]
        rows = pl.ds(pl.multiple_of(block * 64, 64), 64)
        result = None
        for group in range(4):
            normed, inverse = normalize(x_ref[group, rows, :].astype(F32))
            back = gnorm[group, rows, :].astype(F32)
            grad = gres_ref[group, rows, :].astype(F32) + norm_back(back * (1.0 + scale), normed, inverse)
            sums_ref[half, 0:1, :] += jnp.sum(back, 0, keepdims=True)
            sums_ref[half, 1:2, :] += jnp.sum(back * normed, 0, keepdims=True)
            part = nn(perm_ref[:, 64 * group : 64 * group + 64], grad.astype(BF16))
            result = part if result is None else result + part
        out_ref[pl.ds(pl.multiple_of(block * 256, 256), 256), :] = result.astype(BF16)


def back(scal, x, gmixed, gedge, base, shifted, gres, perm, mod, taps):
    arrays = (x, gmixed, gedge, base, shifted, gres, perm, mod, taps)
    plane = pltpu.VMEM((4, PLANE, D), F32)
    return pl.pallas_call(
        back_kernel,
        out_shape=(
            jax.ShapeDtypeStruct((2048, D), BF16),
            jax.ShapeDtypeStruct((2, 8, D), F32),
            jax.ShapeDtypeStruct((16, D), F32),
        ),
        in_specs=[scalars()] + [pl.BlockSpec(memory_space=pltpu.VMEM)] * len(arrays),
        out_specs=(pl.BlockSpec(memory_space=pltpu.VMEM),) * 3,
        scratch_shapes=[plane, plane, pltpu.VMEM((4, BODY, D), BF16)],
        compiler_params=params(),
        name="back",
    )(scal, *arrays)


MESH = pl.DeviceIdType.MESH


def chip_grid(count):
    return {16: (4, 2, 2), 64: (4, 4, 4)}.get(count, (count, 1, 1))


def reduce_gather_kernel(grid, units, *refs):
    own_refs, other_refs, sent_ref = refs[:units], refs[units : 2 * units], refs[2 * units]
    sum_refs, all_ref = refs[2 * units + 1 : 3 * units + 1], refs[3 * units + 1]
    scratch = refs[3 * units + 2 :]
    buffers = [scratch[10 * unit : 10 * unit + 10] for unit in range(units)]
    gz, gx, gy, sends, recvs = scratch[10 * units :]
    deep, tall, broad = grid
    low = deep // 2
    wide = lax.axis_index("wide")
    place = lax.axis_index("narrow")
    z, y, x = wide // (tall * broad), (wide // broad) % tall, wide % broad

    def chip(zz, yy, xx):
        return {"wide": (zz * tall + yy) * broad + xx, "narrow": place}

    def along_x(step):
        return chip(z, y, (x + step) % broad)

    def along_y(step):
        return chip(z, (y + step) % tall, x)

    def along_z(step):
        return chip((z + step) % deep, y, x)

    sibling = {"wide": wide, "narrow": 1 - place}
    partners = (
        [sibling]
        + [along_x(step) for step in range(1, broad)]
        + [along_y(step) for step in range(1, tall)]
        + [along_z(step) for step in range(1, deep)]
    )
    barrier = pltpu.get_barrier_semaphore()
    for partner in partners:
        pl.semaphore_signal(barrier, inc=1, device_id=partner, device_id_type=MESH)
    pl.semaphore_wait(barrier, len(partners))

    count = [0]

    def send(source, target, partner):
        copy = pltpu.make_async_remote_copy(
            src_ref=source, dst_ref=target, send_sem=sends.at[count[0]], recv_sem=recvs.at[count[0]],
            device_id=partner, device_id_type=MESH,
        )
        count[0] += 1
        copy.start()
        return copy

    def wait(copies):
        for copy in copies:
            copy.wait()

    def add(target, *sources):
        total = sources[0].astype(F32)
        for source in sources[1:]:
            total = total + source.astype(F32)
        return total.astype(target.dtype)

    gz[z] = sent_ref[...]
    halves = ((0, low), (low, deep))
    swaps = [
        [send(other.at[start:stop], buffer[0].at[start:stop], sibling) for other, buffer in zip(other_refs, buffers)]
        for start, stop in halves
    ]
    gathers = [send(sent_ref, gz.at[z], along_z(step)) for step in range(1, deep)]

    def add_first(start, stop):
        for own, (first, work, *_) in zip(own_refs, buffers):
            for zz in range(start, stop):

                @pl.loop(0, tall * broad)
                def _(at, zz=zz, own=own, first=first, work=work):
                    yy, xx = at // broad, at % broad
                    work[zz, yy, xx] = add(work, own[zz, yy, xx], first[zz, yy, xx])

    wait(swaps[0])
    add_first(0, low)
    one_a = [
        send(work.at[0:low, :, (x + s) % broad], r1a.at[s - 1], along_x(s))
        for _, work, r1a, *_ in buffers
        for s in range(1, broad)
    ]
    wait(swaps[1])
    add_first(low, deep)
    one_b = [
        send(work.at[low:deep, (y + s) % tall], r1b.at[s - 1], along_y(s))
        for _, work, _, r1b, *_ in buffers
        for s in range(1, tall)
    ]
    wait(gathers)
    gx[x] = gz[...]
    gathers = [send(gz, gx.at[x], along_x(step)) for step in range(1, broad)]

    wait(one_a)
    two_a = []
    for _, work, r1a, _, w1a, _, r2a, *_ in buffers:
        for zz in range(low):
            for yy in range(tall):
                w1a[zz, yy] = add(w1a, work[zz, yy, x], *[r1a[s, zz, yy] for s in range(broad - 1)])
        two_a += [send(w1a.at[:, (y + s) % tall], r2a.at[s - 1], along_y(s)) for s in range(1, tall)]
    wait(one_b)
    two_b = []
    for _, work, _, r1b, _, w1b, _, r2b, *_ in buffers:
        for zz in range(deep - low):
            for xx in range(broad):
                w1b[zz, xx] = add(w1b, work[low + zz, y, xx], *[r1b[s, zz, xx] for s in range(tall - 1)])
        two_b += [send(w1b.at[:, (x + s) % broad], r2b.at[s - 1], along_x(s)) for s in range(1, broad)]
    wait(gathers)
    gy[y] = gx[...]
    gathers = [send(gx, gy.at[y], along_y(step)) for step in range(1, tall)]

    wait(two_a)
    for _, _, _, _, w1a, _, r2a, _, w2, _ in buffers:
        for zz in range(low):
            w2[zz] = add(w2, w1a[zz, y], *[r2a[s, zz] for s in range(tall - 1)])
    wait(two_b)
    three = []
    for _, _, _, _, _, w1b, _, r2b, w2, r3 in buffers:
        for zz in range(deep - low):
            w2[low + zz] = add(w2, w1b[zz, x], *[r2b[s, zz] for s in range(broad - 1)])
        three += [send(w2.at[(z + s) % deep], r3.at[s - 1], along_z(s)) for s in range(1, deep)]
    wait(gathers)
    all_ref[place] = gy[...]
    gathers = [send(gy, all_ref.at[place], sibling)]
    wait(three)
    for sum_ref, buffer in zip(sum_refs, buffers):
        w2, r3 = buffer[8:]
        sum_ref[...] = add(sum_ref, w2[z], *[r3[s] for s in range(deep - 1)])
    wait(gathers)


def reduce_gather(own, other, sent):
    deep, tall, broad = grid = chip_grid(own[0].shape[0])
    low = deep // 2
    shapes = [array.shape[1:] for array in own]
    copies = len(own) * (2 + 2 * (broad - 1 + tall - 1) + (deep - 1)) + (deep - 1) + (broad - 1) + (tall - 1) + 1

    def buffers(unit):
        def slots(count, *shape):
            return pltpu.VMEM((max(count, 1), *shape, *unit), BF16)

        return [
            pltpu.VMEM((*grid, *unit), BF16), pltpu.VMEM((*grid, *unit), BF16),
            slots(broad - 1, low, tall), slots(tall - 1, deep - low, broad),
            pltpu.VMEM((low, tall, *unit), BF16), pltpu.VMEM((deep - low, broad, *unit), BF16),
            slots(tall - 1, low), slots(broad - 1, deep - low),
            pltpu.VMEM((deep, *unit), BF16), slots(deep - 1),
        ]

    row = sent.shape
    space = pl.BlockSpec(memory_space=pltpu.VMEM)
    result = pl.pallas_call(
        functools.partial(reduce_gather_kernel, grid, len(own)),
        out_shape=(
            *[jax.ShapeDtypeStruct(unit, F32) for unit in shapes],
            jax.ShapeDtypeStruct((2, tall, broad, deep, *row), BF16),
        ),
        in_specs=[space] * (2 * len(own) + 1),
        out_specs=(space,) * (len(own) + 1),
        scratch_shapes=[
            *[buffer for unit in shapes for buffer in buffers(unit)],
            pltpu.VMEM((deep, *row), BF16), pltpu.VMEM((broad, deep, *row), BF16),
            pltpu.VMEM((tall, broad, deep, *row), BF16),
            pltpu.SemaphoreType.DMA((copies,)), pltpu.SemaphoreType.DMA((copies,)),
        ],
        compiler_params=pltpu.CompilerParams(
            collective_id=1, has_side_effects=True, vmem_limit_bytes=VMEM_BYTES
        ),
        name="reduce_gather",
    )(*[array.reshape(*grid, *array.shape[1:]) for array in (*own, *other)], sent)
    return result[:-1], result[-1].reshape(-1, *row)


def square_sum_kernel(grid, *refs):
    count = len(refs) - 6
    grads = refs[:count]
    out_ref, mine, near, far, sends, recvs = refs[count:]
    deep, tall, broad = grid
    wide = lax.axis_index("wide")
    place = lax.axis_index("narrow")
    z, across = wide // (tall * broad), wide % (tall * broad)
    line = z * 2 + place

    def near_device(step):
        other = (line + step) % (2 * deep)
        return {"wide": (other // 2) * (tall * broad) + across, "narrow": other % 2}

    def far_device(step):
        return {"wide": z * (tall * broad) + (across + step) % (tall * broad), "narrow": place}

    nears = [near_device(step) for step in range(1, 2 * deep)]
    fars = [far_device(step) for step in range(1, tall * broad)]
    barrier = pltpu.get_barrier_semaphore()
    for partner in nears + fars:
        pl.semaphore_signal(barrier, inc=1, device_id=partner, device_id_type=MESH)

    total = jnp.zeros((), F32)
    for grad in grads:
        value = grad[...].astype(F32)
        total = total + jnp.sum(value * value)
    mine[...] = jnp.full((8, 128), total, F32)
    pl.semaphore_wait(barrier, len(nears + fars))

    def exchange(slots, partners, first):
        copies = []
        for step, partner in enumerate(partners):
            copy = pltpu.make_async_remote_copy(
                src_ref=mine, dst_ref=slots.at[step], send_sem=sends.at[first + step],
                recv_sem=recvs.at[first + step], device_id=partner, device_id_type=MESH,
            )
            copy.start()
            copies.append(copy)
        for copy in copies:
            copy.wait()
        value = mine[...]
        for step in range(len(partners)):
            value = value + slots[step]
        return value

    mine[...] = exchange(near, nears, 0)
    out_ref[...] = exchange(far, fars, len(nears))


def square_sum(wide_count, grads):
    deep, tall, broad = grid = chip_grid(wide_count)
    near, far = 2 * deep - 1, tall * broad - 1
    return pl.pallas_call(
        functools.partial(square_sum_kernel, grid),
        out_shape=jax.ShapeDtypeStruct((8, 128), F32),
        in_specs=[pl.BlockSpec(memory_space=pltpu.VMEM)] * len(grads),
        out_specs=pl.BlockSpec(memory_space=pltpu.VMEM),
        scratch_shapes=[
            pltpu.VMEM((8, 128), F32), pltpu.VMEM((near, 8, 128), F32), pltpu.VMEM((max(far, 1), 8, 128), F32),
            pltpu.SemaphoreType.DMA((near + far,)), pltpu.SemaphoreType.DMA((near + far,)),
        ],
        compiler_params=pltpu.CompilerParams(
            collective_id=2, has_side_effects=True, vmem_limit_bytes=VMEM_BYTES
        ),
        name="square_sum",
    )(*grads)


def shared_rows(shared_ref, rows):
    half = FF // 2 * rows // D
    shared = shared_ref[...].astype(F32)
    up = [shared[at : at + rows] for at in (0, rows)]
    down = shared[2 * rows : 2 * rows + half]
    out = shared[2 * rows + half : 2 * rows + half + rows // 2]
    return [[out], up, [down]]


def adamw_kernel(rates, square_ref, shared_ref, *refs):
    clip_limit = PARAMS**0.5
    norm = jnp.sqrt(square_ref[0:1, 0:1])
    factor = clip_limit / jnp.maximum(norm, clip_limit)
    plain = (len(refs) - 3 * 7) // 8
    count = plain + 3
    grads = [[ref[...]] for ref in refs[:plain]]
    states, outs = refs[plain : plain + 3 * count], refs[plain + 3 * count :]
    grads += shared_rows(shared_ref, states[3 * (plain + 1)].shape[0])
    for index, rate in enumerate(rates):
        master_ref, first_ref, second_ref = states[3 * index : 3 * index + 3]
        first_out, second_out, master_out, copy_out = outs[4 * index : 4 * index + 4]
        start = 0
        for grad in grads[index]:
            at = (slice(None), slice(start, start + grad.shape[1]))
            start += grad.shape[1]
            scaled = grad * factor
            first_new = BETA_ONE * first_ref[at] + (1.0 - BETA_ONE) * scaled
            second_new = BETA_TWO * second_ref[at] + (1.0 - BETA_TWO) * scaled * scaled
            ratio = (first_new * (1.0 / (1.0 - BETA_ONE**STEP))) / (
                jnp.sqrt(second_new * (1.0 / (1.0 - BETA_TWO**STEP))) + ADAM_EPS
            )
            master = master_ref[at]
            master_new = master - rate * (ratio + WEIGHT_DECAY * master)
            first_out[at] = first_new
            second_out[at] = second_new
            master_out[at] = master_new
            copy_out[at] = master_new.astype(BF16)


def adamw(square, shared, grads, states, rates):
    arrays = [array for state in states for array in state]
    shapes = [
        jax.ShapeDtypeStruct(state[0].shape, dtype) for state in states for dtype in (F32, F32, F32, BF16)
    ]
    space = pl.BlockSpec(memory_space=pltpu.VMEM)
    return pl.pallas_call(
        functools.partial(adamw_kernel, rates),
        out_shape=shapes,
        in_specs=[space] * (2 + len(grads) + len(arrays)),
        out_specs=[space] * len(shapes),
        compiler_params=params(),
        name="adamw",
    )(square, shared, *grads, *arrays)


def timestep_code(stamps, channels):
    half_dim = channels // 2
    scales = jnp.exp(-jnp.log(10000.0) * jnp.arange(half_dim, dtype=F32) / half_dim)
    angles = stamps.astype(F32)[:, None] * scales[None, :]
    return jnp.concatenate([jnp.cos(angles), jnp.sin(angles)], axis=1)


def one_hot_rows(source, columns, valid=None):
    hit = source[:, None] == jnp.arange(columns, dtype=jnp.int32)[None, :]
    if valid is not None:
        hit = jnp.logical_and(hit, valid[:, None])
    return hit.astype(BF16)


def permutation(long_latent):
    row = jnp.arange(256, dtype=jnp.int32)
    p, q, s = row // 128, (row // 64) % 2, row % 64
    big = (2 * (s // 32) + p) * 64 + 2 * (s % 32) + q
    small = (2 * (s // 16) + p) * 32 + 2 * (s % 16) + q
    return one_hot_rows(jnp.where(long_latent, big, small), 256)


def edge_permutation():
    row = jnp.arange(128, dtype=jnp.int32)
    return one_hot_rows((row // 64) * 64 + 2 * (row % 32) + (row // 32) % 2, 128)


def pair_order():
    row = jnp.arange(6 * HS, dtype=jnp.int32)
    return one_hot_rows((row % 192) // HS * 128 + row // 192 * HS + row % HS, 6 * HS)


def tap_rows(kernel):
    return jnp.pad(kernel.T, ((0, 7), (0, 0)))


def per_device(tokens, cotangent, size_tags, timesteps, labels, *weights_and_states):
    modulator, class_table, mix_kernel, heads_in, heads_out, up_weight, hidden_kernel, down_weight = weights_and_states[:8]
    states = [weights_and_states[8 + 3 * i : 11 + 3 * i] for i in range(8)]
    wide_count = lax.axis_size("wide")
    wide = lax.axis_index("wide")
    place = lax.axis_index("narrow")
    cell = wide * 2 + place
    cells = wide_count * 2

    def swap(value):
        return lax.ppermute(value, "narrow", [(0, 1), (1, 0)])

    def boundary(body):
        return jnp.where(place == 0, body[:, BODY - EDGE :], body[:, :EDGE])

    edge = swap(jnp.where(place == 0, tokens[-4 * EDGE :], tokens[: 4 * EDGE]))
    hin_other = swap(heads_in)
    hout_other = swap(heads_out)
    up_other = swap(up_weight)
    down_other = swap(down_weight)
    taps_own = tap_rows(hidden_kernel)
    taps_other = swap(taps_own)
    mix_taps = tap_rows(mix_kernel)

    long_latent = size_tags[0] > SIDE * SIDE
    width = jnp.where(long_latent, SIDE, SIDE // 2)
    gap = jnp.where(long_latent, 0, 16)
    scal = jnp.stack([width, gap, long_latent.astype(jnp.int32), place]).astype(jnp.int32)
    perm = permutation(long_latent)
    perm_back = perm.T
    order = pair_order()
    embedded = timestep_code(timesteps, D) + class_table[:, labels].astype(F32).T
    cond_low = jax.nn.silu(embedded).astype(BF16)
    modulation = jnp.dot(cond_low, modulator, preferred_element_type=F32).reshape(-1, 6, D)
    mod = jnp.pad(modulation, ((0, 0), (0, 2), (0, 0)))

    x, mixed, base, shifted, q, kv = front(
        scal, tokens, edge, perm, edge_permutation(), mod, mix_taps, order, heads_in
    )
    kv_far_other = swap(kv)
    q_other, kv_other = project(mixed, order, hin_other)
    kv_far = swap(kv_other)
    attended_other, logs_other = attention(scal, q_other, kv_other, kv_far_other)
    attended, logs = attention(scal, q, kv, kv_far)
    attn, norm, cot, grad_ffn = middle(x, attended, attended_other, cotangent, perm, mod, heads_out, hout_other)
    norm_edge, grad_edge = swap((boundary(norm), boundary(grad_ffn)))
    ffn, back_norm, up_grad, up_grad_other, down_grad, down_grad_other, taps_grad = feed_forward(
        scal, taps_own, taps_other, norm, norm_edge, grad_ffn, grad_edge, up_weight, up_other, down_weight, down_other
    )

    output, grad_residual, grad_attended, grad_attended_other, sums_two, hout_grad, hout_grad_other = turn(
        x, attn, ffn, cot, back_norm, attended, attended_other, perm_back, mod, heads_out, hout_other
    )
    rows = D // wide_count
    half = FF // 2
    up_sum = up_grad.astype(F32) + swap(up_grad_other).astype(F32)
    down_sum = down_grad.astype(F32) + swap(down_grad_other).astype(F32)
    hout_sum = hout_grad.astype(F32) + swap(hout_grad_other).astype(F32)
    tap_half = taps_grad.shape[0] // 2
    taps_sum = taps_grad[:tap_half, :9] + swap(taps_grad[tap_half:, :9])
    tap_part = taps_sum.transpose(0, 2, 1).reshape(wide_count, -1)
    tap_part = jnp.pad(tap_part, ((0, 0), (0, -tap_part.shape[1] % D)))
    grads = jnp.concatenate(
        [
            up_sum.reshape(2, wide_count, rows, D).transpose(1, 0, 2, 3).reshape(wide_count, 2 * rows, D),
            down_sum.reshape(wide_count, -1, D),
            hout_sum.reshape(wide_count, -1, D),
            tap_part.reshape(wide_count, -1, D),
        ],
        axis=1,
    )
    pad = -grads.shape[1] % 16
    grads = jnp.pad(grads, ((0, 0), (0, pad), (0, 0))).astype(BF16)
    grads, grad_attended_other = lax.optimization_barrier((grads, grad_attended_other))
    mine = lax.psum_scatter(grads, "wide", scatter_dimension=0, tiled=False)

    gq_other, gkv_other, gkv_far_other = attention_back(
        scal, q_other, kv_other, kv_far_other, attended_other, grad_attended_other, logs_other
    )
    gkv_add = swap(gkv_far_other)
    gq, gkv, gkv_far = attention_back(scal, q, kv, kv_far, attended, grad_attended, logs)
    gkv_add_other = swap(gkv_far)
    gmixed, hin_grad, hin_grad_other = project_back(
        (gq, gkv, gkv_add), (gq_other, gkv_other, gkv_add_other), mixed, order, heads_in, hin_other
    )
    gmixed_edge = swap(boundary(gmixed))
    input_grad, sums_one, mix_grad = back(
        scal, x, gmixed, gmixed_edge, base, shifted, grad_residual, perm_back, mod, mix_taps
    )

    modulation_two_grad = sums_two[:, 1:3].reshape(-1, 2 * D)
    own = D // cells
    mix_parts = mix_grad[:9].T.reshape(wide_count, 2, 1, own * 9).transpose(1, 0, 2, 3).astype(BF16)
    mix_parts = jnp.pad(mix_parts, ((0, 0), (0, 0), (0, 15), (0, -own * 9 % 128)))
    mix_own = jnp.where(place == 0, mix_parts[0], mix_parts[1])
    mix_other = jnp.where(place == 0, mix_parts[1], mix_parts[0])

    def by_chip(grad):
        split = grad.reshape(wide_count, rows, -1)
        return jnp.pad(split, ((0, 0), (0, -rows % 16), (0, 0)))

    slope = jax.vjp(jax.nn.silu, embedded)[1](jnp.ones_like(embedded))[0]
    blocks = jnp.concatenate([sums_one[:, 0:2], sums_two[:, 0:4]], axis=1).transpose(1, 0, 2).reshape(12, D)
    digits = jnp.stack([labels // 32, labels % 32], axis=1).astype(F32)
    digits = jnp.pad(digits, ((0, 14), (0, 126)))
    sent = jnp.concatenate([jnp.concatenate([blocks, cond_low.astype(F32), slope], axis=0), digits], axis=1)
    (hin_mine, mix_mine), everyone = reduce_gather(
        [by_chip(hin_grad), mix_own], [by_chip(hin_grad_other), mix_other], sent.astype(BF16)
    )
    row = jnp.arange(16, dtype=jnp.int32)
    block_row = 2 * jnp.arange(6, dtype=jnp.int32)[:, None] + jnp.arange(2, dtype=jnp.int32)
    picks = (block_row[:, :, None] == row).astype(F32)
    columns = lax.dynamic_slice_in_dim(everyone[:, 12:], cell * own, own, 2).astype(F32)
    all_cond, all_slope = columns[:, :2], columns[:, 2:]
    flat = everyone.reshape(cells * 16, -1)
    left = jnp.einsum("cfd,kfr->kdcr", all_cond, picks).astype(BF16).reshape(6 * own, cells * 16)
    modulator_mine = jnp.dot(left, flat, preferred_element_type=F32)[:, :D]
    modulator_mine = modulator_mine.reshape(6, own, D).transpose(1, 0, 2).reshape(own, 6 * D)
    modulator_rows = lax.dynamic_slice_in_dim(modulator, cell * own, own, 0).reshape(own, 6, D)
    modulator_rows = modulator_rows.transpose(1, 0, 2).reshape(6 * own, D)
    products = lax.dot_general(
        flat[:, :D], modulator_rows, (((1,), (1,)), ((), ())), preferred_element_type=F32
    ).reshape(cells, 16, 6, own)
    all_embedded = all_slope * jnp.stack(
        [sum(products[:, 2 * block + frame, block] for block in range(6)) for frame in range(2)], axis=1
    )
    all_digits = everyone[:, :2, D : D + 2].astype(jnp.int32)
    all_labels = (all_digits[..., 0] * 32 + all_digits[..., 1])[..., None]
    chosen = (all_labels == jnp.arange(class_table.shape[1], dtype=jnp.int32)).astype(F32)
    class_mine = jnp.dot(
        all_embedded.reshape(cells * 2, own).T, chosen.reshape(cells * 2, -1),
        precision=lax.Precision.HIGHEST, preferred_element_type=F32,
    )
    mix_mine = mix_mine[0, : own * 9].reshape(own, 9).T
    hin_mine = hin_mine[:rows]

    shared = 2 * rows + half // wide_count + rows // 2
    hidden = half // wide_count
    taps_mine = mine[shared:].reshape(-1)[: hidden * 9].reshape(hidden, 9).T.astype(F32)
    shards = (modulator_mine, class_mine, mix_mine, hin_mine, taps_mine)
    square = square_sum(wide_count, (*shards[:4], mine))
    grad_norm = jnp.sqrt(square[0, 0])
    order = (0, 1, 2, 3, 6, 4, 5, 7)
    step_rates = (
        D ** (-0.5), 1.0, 1.0 / 3.0, D ** (-0.5), 1.0 / 3.0, (D // 32) ** (-0.5), D ** (-0.5), FF ** (-0.5),
    )
    turned = (2, 6)
    given = [tuple(array.T for array in states[i]) if i in turned else states[i] for i in order]
    updated = adamw(square, mine, shards, given, step_rates)
    flat = [None] * 32
    for at, i in enumerate(order):
        for j in range(4):
            array = updated[4 * at + j]
            flat[4 * i + j] = array.T if i in turned else array
    return (output, input_grad, grad_norm, *flat, modulation_two_grad)


def solution(mesh):
    both = P(("wide", "narrow"), None)
    turned = P(("narrow", "wide"), None)
    grid = P("wide", "narrow")
    places = (both, both, both, grid, turned, grid, turned, turned)
    in_specs = (
        both, both, P("wide"), P(("wide", "narrow")), P(("wide", "narrow")),
        P(), P(), P(), P(None, "narrow"), P("narrow", None), P(None, "narrow"), P("narrow", None), P("narrow", None),
        *[place for place in places for _ in range(3)],
    )
    out_specs = (both, both, P(), *[place for place in places for _ in range(4)], both)
    return jax.shard_map(per_device, mesh=mesh, in_specs=in_specs, out_specs=out_specs, check_vma=False)
```

```python
import functools

import jax
import jax.numpy as jnp
from jax import lax
from jax.experimental import pallas as pl
from jax.experimental.pallas import tpu as pltpu
from jax.sharding import PartitionSpec as P

D = 768
HS = 64
FF = 3072
SIDE = 32
STEP = 10
PARAMS = 11419392

NORM_EPS = 1e-06
BETA_ONE = 0.5
BETA_TWO = 0.5
ADAM_EPS = 1e-08
WEIGHT_DECAY = 0.01

F32 = jnp.float32
BF16 = jnp.bfloat16

BODY = 512
HALF = 256
EDGE = 32
PLANE = 592
CHUNK = 256
VMEM_BYTES = 60 * 1024 * 1024


def params(*semantics):
    return pltpu.CompilerParams(
        dimension_semantics=semantics or None, vmem_limit_bytes=VMEM_BYTES
    )


def nn(left, right):
    return lax.dot_general(left, right, (((1,), (0,)), ((), ())), preferred_element_type=F32)


def nt(left, right):
    return lax.dot_general(left, right, (((1,), (1,)), ((), ())), preferred_element_type=F32)


def tn(left, right):
    return lax.dot_general(left, right, (((0,), (0,)), ((), ())), preferred_element_type=F32)


def whole(shape):
    return pl.BlockSpec(shape, lambda *_: (0,) * len(shape), pipeline_mode=pl.Buffered(1))


def scalars():
    return pl.BlockSpec(memory_space=pltpu.SMEM)


def geometry(scal_ref):
    return scal_ref[0], scal_ref[1], scal_ref[2] == 1, scal_ref[3]


def body_offset(half, gap):
    return pl.multiple_of(EDGE + half * (HALF + gap), 16)


def edge_offset(place):
    return pl.multiple_of(jnp.where(place == 0, EDGE + BODY, 0), 16)


def normalize(fields):
    center = fields - jnp.mean(fields, -1, keepdims=True)
    inverse = lax.rsqrt(jnp.mean(center * center, -1, keepdims=True) + NORM_EPS)
    return center * inverse, inverse


def norm_back(grad_hat, normed, inverse):
    return inverse * (
        grad_hat
        - jnp.mean(grad_hat, -1, keepdims=True)
        - normed * jnp.mean(grad_hat * normed, -1, keepdims=True)
    )


def variants(base, shifted, offset, width, rows, lanes, kind=F32):
    up = pl.multiple_of(offset - width, 16)
    down = pl.multiple_of(offset + width, 16)
    found = {}
    for part, shift, where in ((0, 0, offset), (0, 1, down), (1, 0, offset), (1, -1, up)):
        for column in (0, 1):
            at = (2 * part + column, pl.ds(where, rows), lanes)
            found[part, shift, column, 0] = base[at].astype(kind)
            found[part, shift, column, 1] = shifted[at].astype(kind)
    return found


def tap(found, p, q, a, b):
    part, shift = ((1, -1), (0, 0), (1, 0))[a + 1] if p == 0 else ((0, 0), (1, 0), (0, 1))[a + 1]
    column, moved = ((1, 1), (0, 0), (1, 0))[b + 1] if q == 0 else ((0, 0), (1, 0), (0, 1))[b + 1]
    return found[part, shift, column, moved]


def conv_at(found, kernel, p, q, flip=False):
    total = None
    for a in (-1, 0, 1):
        for b in (-1, 0, 1):
            index = 3 * (a + 1) + (b + 1)
            term = tap(found, p, q, a, b) * kernel[8 - index if flip else index]
            total = term if total is None else total + term
    return total


def kernel_rows(kernel_ref, lanes, rows, kind=F32):
    return [
        jnp.broadcast_to(kernel_ref[index : index + 1, lanes].astype(kind), (rows, lanes.size)) for index in range(9)
    ]


def clear_borders(plane, wide_gap=True):
    zeros = jnp.zeros((4, EDGE, plane.shape[2]), plane.dtype)
    plane[:, 0:EDGE, :] = zeros
    plane[:, EDGE + HALF : EDGE + HALF + EDGE, :] = zeros
    plane[:, EDGE + BODY : EDGE + BODY + EDGE, :] = zeros
    plane[:, PLANE - EDGE : PLANE, :] = zeros


def column_masks(rows, width):
    column = lax.broadcasted_iota(jnp.int32, (rows, 128), 0) & (width - 1)
    return column != width - 1, column != 0


def moved_rows(value, column, masks):
    rows, lanes = value.shape
    moved = pltpu.roll(value, rows - 1 if column == 0 else 1, 0)
    parts = [jnp.where(masks[column], moved[:, at : at + 128], 0.0) for at in range(0, lanes, 128)]
    return parts[0] if len(parts) == 1 else jnp.concatenate(parts, axis=1)


def own_half(half):
    return lambda i: jnp.minimum(i, half - 1)


def other_half(half):
    return lambda i: jnp.maximum(i - half, 0)


def front_kernel(
    scal_ref, x_ref, edge_ref, perm_ref, edge_perm_ref, mod_ref, taps_ref, order_ref, weight_ref,
    x_out, mixed_out, base_out, shifted_out, q_out, kv_out,
):
    width, gap, long_latent, place = geometry(scal_ref)
    @pl.when(pl.program_id(0) == 0)
    def _():
        clear_borders(base_out)
        clear_borders(shifted_out)
        masks = column_masks(64, width)
        edge_masks = column_masks(EDGE, width)

        @pl.loop(0, 8, unroll=2)
        def _(block):
            half = block // 4
            rows = x_ref[pl.ds(pl.multiple_of(block * 256, 256), 256), :]
            shift = mod_ref[half, 0:1, :]
            scale = mod_ref[half, 1:2, :]
            place_in = pl.ds(pl.multiple_of(block * 64, 64), 64)
            place_out = pl.ds(pl.multiple_of(body_offset(half, gap) + (block % 4) * 64, 16), 64)
            for group in range(4):
                picked = nn(perm_ref[64 * group : 64 * group + 64, :], rows)
                x_out[group, place_in, :] = picked.astype(BF16)
                normed = normalize(picked)[0]
                value = normed * (1.0 + scale) + shift
                base_out[group, place_out, :] = value.astype(BF16)
                shifted_out[group, place_out, :] = moved_rows(value, group % 2, masks).astype(BF16)

        @pl.when(long_latent)
        def _():
            at = pl.ds(edge_offset(place), EDGE)
            for group in range(4):
                picked = nn(edge_perm_ref[32 * group : 32 * group + 32, :], edge_ref[...])
                normed = normalize(picked)[0]
                value = normed * (1.0 + mod_ref[0, 1:2, :]) + mod_ref[0, 0:1, :]
                base_out[group, at, :] = value.astype(BF16)
                shifted_out[group, at, :] = moved_rows(value, group % 2, edge_masks).astype(BF16)

        for lane in range(D // 128):
            lanes = pl.ds(lane * 128, 128)
            kernel = kernel_rows(taps_ref, lanes, 16)

            @pl.loop(0, 32, unroll=4)
            def _(tile, lanes=lanes, kernel=kernel):
                offset = body_offset(tile // 16, gap) + (tile % 16) * 16
                found = variants(base_out, shifted_out, pl.multiple_of(offset, 16), width, 16, lanes)
                for p in (0, 1):
                    for q in (0, 1):
                        at = (2 * p + q, pl.ds(pl.multiple_of(tile * 16, 16), 16), lanes)
                        mixed_out[at] = conv_at(found, kernel, p, q).astype(BF16)

    project_kernel(mixed_out, order_ref, weight_ref, q_out, kv_out)


def project_kernel(mixed_ref, order_ref, weight_ref, q_out, kv_out):
    weight = nn(weight_ref[...], order_ref[...]).astype(BF16)
    for group in range(4):
        triple = nn(mixed_ref[group], weight)
        q_out[0, group] = (triple[:, 0:128] * (HS**-0.5)).astype(BF16)
        kv_out[0, 0, group] = triple[:, 128:256].astype(BF16)
        kv_out[0, 1, group] = triple[:, 256:384].astype(BF16)


def project_specs(pairs):
    shapes = (
        jax.ShapeDtypeStruct((pairs, 4, BODY, 128), BF16),
        jax.ShapeDtypeStruct((pairs, 2, 4, BODY, 128), BF16),
    )
    blocks = (
        pl.BlockSpec((1, 4, BODY, 128), lambda i: (i, 0, 0, 0)),
        pl.BlockSpec((1, 2, 4, BODY, 128), lambda i: (i, 0, 0, 0, 0)),
    )
    return shapes, blocks, pl.BlockSpec((D, 384), lambda i: (0, i))


def front(scal, x, edge, perm, edge_perm, mod, taps, order, weight):
    pairs = weight.shape[1] // 384
    shapes, blocks, weight_block = project_specs(pairs)
    plane = jax.ShapeDtypeStruct((4, PLANE, D), BF16)
    body = jax.ShapeDtypeStruct((4, BODY, D), BF16)
    return pl.pallas_call(
        front_kernel,
        grid=(pairs,),
        out_shape=(body, body, plane, plane, *shapes),
        in_specs=[
            scalars(), whole(x.shape), whole(edge.shape), whole(perm.shape), whole(edge_perm.shape),
            whole(mod.shape), whole(taps.shape), whole(order.shape), weight_block,
        ],
        out_specs=(whole(body.shape), whole(body.shape), whole(plane.shape), whole(plane.shape), *blocks),
        compiler_params=params("arbitrary"),
        name="front",
    )(scal, x, edge, perm, edge_perm, mod, taps, order, weight)


def project(mixed, order, weight):
    pairs = weight.shape[1] // 384
    shapes, blocks, weight_block = project_specs(pairs)
    return pl.pallas_call(
        project_kernel,
        grid=(pairs,),
        out_shape=shapes,
        in_specs=[whole(mixed.shape), whole(order.shape), weight_block],
        out_specs=blocks,
        compiler_params=params("arbitrary"),
        name="project",
    )(mixed, order, weight)


def head_mask(rows, head):
    lane = lax.broadcasted_iota(jnp.int32, (rows, 128), 1)
    return (lane < HS) if head == 0 else (lane >= HS)


def pieces(first, second, rows):
    lane = lax.broadcasted_iota(jnp.int32, (rows, 128), 1)
    value = jnp.where(lane < HS, first, second)
    one = value.astype(BF16).astype(F32)
    two = (value - one).astype(BF16).astype(F32)
    three = value - one - two
    turn = lane % HS
    picked = jnp.where(turn == 0, one, jnp.where(turn == 1, two, jnp.where(turn == 2, three, 0.0)))
    return picked.astype(BF16)


def unit_pieces(rows):
    lane = lax.broadcasted_iota(jnp.int32, (rows, 128), 1)
    return jnp.where(lane % HS < 3, 1.0, 0.0).astype(BF16)


def attend_kernel(scal_ref, q_ref, own_ref, other_ref, out_ref, log_ref):
    long_latent = scal_ref[2] == 1

    def products(query, keys):
        found = []
        for head in (0, 1):
            masked = jnp.where(head_mask(query.shape[0], head), query, jnp.zeros_like(query))
            found.append([nt(masked, key) for key in keys])
        return found

    def attend(head_scores, values, rows):
        mixes, logs = [], []
        for scores in head_scores:
            highest = jnp.max(scores[0], -1, keepdims=True)
            for other in scores[1:]:
                highest = jnp.maximum(highest, jnp.max(other, -1, keepdims=True))
            mix = None
            for score, value in zip(scores, values):
                share = jnp.exp(score - highest).astype(BF16)
                part = nn(share, value)
                mix = part if mix is None else mix + part
            total = mix[:, 128:256]
            mixes.append(mix[:, 0:128] / total)
            logs.append(highest + jnp.log(total))
        mix = jnp.where(head_mask(rows, 0), mixes[0], mixes[1])
        return mix.astype(BF16), pieces(-logs[0], -logs[1], rows)

    def with_ones(value):
        return jnp.concatenate([value, jnp.ones_like(value)], axis=1)

    @pl.when(long_latent)
    def _():
        keys = [own_ref[0, 0, 0], other_ref[0, 0, 0]]
        values = [with_ones(own_ref[0, 1, 0]), with_ones(other_ref[0, 1, 0])]
        tiles = [pl.ds(tile * 128, 128) for tile in range(4)]
        scores = [products(q_ref[0, 0, at, :], keys) for at in tiles]
        for at, score in zip(tiles, scores):
            out_ref[0, at, :], log_ref[0, 0, at, :] = attend(score, values, 128)

    @pl.when(jnp.logical_not(long_latent))
    def _():
        tiles = [pl.ds(tile * 256, 256) for tile in range(2)]
        scores = [products(q_ref[0, 0, at, :], [own_ref[0, 0, 0, at, :]]) for at in tiles]
        for at, score in zip(tiles, scores):
            out_ref[0, at, :], log_ref[0, 0, at, :] = attend(score, [with_ones(own_ref[0, 1, 0, at, :])], 256)


def attention(scal, q, own, other):
    pairs = q.shape[0]
    pair_spec = pl.BlockSpec((1, 1, BODY, 128), lambda p, g: (p, g, 0, 0))
    kv_spec = pl.BlockSpec((1, 2, 1, BODY, 128), lambda p, g: (p, 0, g, 0, 0))
    return pl.pallas_call(
        attend_kernel,
        grid=(pairs, 4),
        out_shape=(
            jax.ShapeDtypeStruct((4, BODY, 128 * pairs), BF16),
            jax.ShapeDtypeStruct((pairs, 4, BODY, 128), BF16),
        ),
        in_specs=[scalars(), pair_spec, kv_spec, kv_spec],
        out_specs=(pl.BlockSpec((1, BODY, 128), lambda p, g: (g, 0, p)), pair_spec),
        compiler_params=params("arbitrary", "arbitrary"),
        name="attention",
    )(scal, q, own, other)


def attend_back_kernel(
    scal_ref, q_ref, own_ref, other_ref, mix_ref, grad_ref, log_ref, gq_ref, gown_ref, gother_ref
):
    long_latent = scal_ref[2] == 1

    def side(query, mix, grad, log):
        rows = query.shape[0]
        product = mix.astype(F32) * grad.astype(F32)
        deltas = [
            jnp.sum(jnp.where(head_mask(rows, head), product, 0.0), -1, keepdims=True) for head in (0, 1)
        ]
        delta = pieces(-deltas[0], -deltas[1], rows)
        result = []
        for head in (0, 1):
            mask = head_mask(rows, head)
            zero = jnp.zeros_like(query)
            q_head = jnp.where(mask, query, zero)
            g_head = jnp.where(mask, grad, zero)
            q_more = jnp.concatenate([q_head, jnp.where(mask, log, zero)], axis=1)
            g_more = jnp.concatenate([g_head, jnp.where(mask, delta, zero)], axis=1)
            result.append((q_head, g_head, q_more, g_more))
        return result

    def keys_ahead(heads, key, value):
        ones = unit_pieces(key.shape[0])
        key_more = jnp.concatenate([key, ones], axis=1)
        value_more = jnp.concatenate([value, ones], axis=1)
        return [(nt(key_more, q_more), nt(value_more, g_more)) for _, _, q_more, g_more in heads]

    def keys_part(heads, key, ahead):
        key_turned = key.astype(F32).T.astype(BF16)
        gk = gv = None
        turned = []
        for (q_head, g_head, _, _), (score, slope) in zip(heads, ahead):
            share = jnp.exp(score)
            slope = (share * slope).astype(BF16)
            share = share.astype(BF16)
            gv_part = nn(share, g_head)
            gk_part = nn(slope, q_head)
            gv = gv_part if gv is None else gv + gv_part
            gk = gk_part if gk is None else gk + gk_part
            turned.append(nn(key_turned, slope))
        return gk, gv, turned

    def query_grad(turned):
        row = lax.broadcasted_iota(jnp.int32, turned[0].shape, 0)
        both = jnp.where(row < HS, turned[0], turned[1]) * (HS**-0.5)
        return both.T.astype(BF16)

    @pl.when(long_latent)
    def _():
        heads = side(q_ref[0, 0], mix_ref[0], grad_ref[0], log_ref[0, 0])
        totals = None
        ahead = [keys_ahead(heads, source[0, 0, 0], source[0, 1, 0]) for source in (own_ref, other_ref)]
        for source, target, products in ((own_ref, gown_ref, ahead[0]), (other_ref, gother_ref, ahead[1])):
            gk, gv, turned = keys_part(heads, source[0, 0, 0], products)
            target[0, 0, 0] = gk.astype(BF16)
            target[0, 1, 0] = gv.astype(BF16)
            totals = turned if totals is None else [a + b for a, b in zip(totals, turned)]
        gq_ref[0, 0] = query_grad(totals)

    @pl.when(jnp.logical_not(long_latent))
    def _():
        for tile in range(2):
            at = pl.ds(tile * 256, 256)
            heads = side(q_ref[0, 0, at, :], mix_ref[0, at, :], grad_ref[0, at, :], log_ref[0, 0, at, :])
            key = own_ref[0, 0, 0, at, :]
            gk, gv, turned = keys_part(heads, key, keys_ahead(heads, key, own_ref[0, 1, 0, at, :]))
            gown_ref[0, 0, 0, at, :] = gk.astype(BF16)
            gown_ref[0, 1, 0, at, :] = gv.astype(BF16)
            gq_ref[0, 0, at, :] = query_grad(turned)
        gother_ref[...] = jnp.zeros_like(gother_ref)


def attention_back(scal, q, own, other, mix, grad, log):
    pairs = q.shape[0]
    pair_spec = pl.BlockSpec((1, 1, BODY, 128), lambda p, g: (p, g, 0, 0))
    kv_spec = pl.BlockSpec((1, 2, 1, BODY, 128), lambda p, g: (p, 0, g, 0, 0))
    lane_spec = pl.BlockSpec((1, BODY, 128), lambda p, g: (g, 0, p))
    return pl.pallas_call(
        attend_back_kernel,
        grid=(pairs, 4),
        out_shape=(
            jax.ShapeDtypeStruct(q.shape, BF16),
            jax.ShapeDtypeStruct(own.shape, BF16),
            jax.ShapeDtypeStruct(own.shape, BF16),
        ),
        in_specs=[scalars(), pair_spec, kv_spec, kv_spec, lane_spec, lane_spec, pair_spec],
        out_specs=(pair_spec, kv_spec, kv_spec),
        compiler_params=params("arbitrary", "arbitrary"),
        name="attention_back",
    )(scal, q, own, other, mix, grad, log)


def middle_kernel(
    x_ref, mix_own, mix_other, cot_ref, perm_ref, mod_ref, own_ref, other_ref, attn_out, norm_out, cot_out, grad_out
):
    gate_one = mod_ref[0, 2:3, :]
    shift = mod_ref[0, 3:4, :]
    scale = mod_ref[0, 4:5, :]
    gate_two = mod_ref[0, 5:6, :]
    for group in range(4):
        attn = nn(mix_own[group], own_ref[...]) + nn(mix_other[group], other_ref[...])
        attn_low = attn.astype(BF16)
        attn_out[group] = attn_low
        residual = x_ref[group].astype(F32) + gate_one * attn_low.astype(F32)
        norm_out[group] = (normalize(residual)[0] * (1.0 + scale) + shift).astype(BF16)
        cot = nn(perm_ref[64 * group : 64 * group + 64, :], cot_ref[...])
        cot_out[group] = cot.astype(BF16)
        grad_out[group] = (cot * gate_two).astype(BF16)


def middle(x, mix, mix_other, cot, perm, mod, weight, weight_other):
    part = pl.BlockSpec((4, 64, D // 2), lambda i: (0, i, 0))
    block = pl.BlockSpec((4, 64, D), lambda i: (0, i, 0))
    body = jax.ShapeDtypeStruct((4, BODY, D), BF16)
    return pl.pallas_call(
        middle_kernel,
        grid=(8,),
        out_shape=(body,) * 4,
        in_specs=[
            block, part, part, pl.BlockSpec((256, D), lambda i: (i, 0)), whole(perm.shape),
            pl.BlockSpec((1, 8, D), lambda i: (i // 4, 0, 0)), whole(weight.shape), whole(weight.shape),
        ],
        out_specs=(block,) * 4,
        compiler_params=params("arbitrary"),
        name="middle",
    )(x, mix, mix_other, cot, perm, mod, weight, weight_other)


def gelu_both(value):
    root = 0.7978845608028654
    square = value * value
    angle = value * (root + (root * 0.044715) * square)
    bent = jnp.tanh(angle)
    half = 0.5 + 0.5 * bent
    inner = (0.5 * root) + (1.5 * root * 0.044715) * square
    return value * half, half + value * (1.0 - bent * bent) * inner


def ffn_kernel(
    scal_ref, taps_own, taps_other, norm_ref, norm_edge, grad_ref, grad_edge,
    up_own, up_other, down_own, down_other,
    ffn_out, back_out, up_grad_own, up_grad_other, down_grad_own, down_grad_other, taps_grad,
    hid, hid_moved, gc, gc_moved, act, gh, da, da_edge, ffn_sum, back_sum, up, down, taps, norm_turned, grad_turned, tap_sums,
):
    width, gap, long_latent, place = geometry(scal_ref)
    step = pl.program_id(0)
    steps = pl.num_programs(0)

    @pl.when(step < steps // 2)
    def _():
        up[...] = up_own[...]
        down[...] = down_own[...]
        taps[...] = taps_own[...]

    @pl.when(step >= steps // 2)
    def _():
        up[...] = up_other[...]
        down[...] = down_other[...]
        taps[...] = taps_other[...]

    @pl.when(step == 0)
    def _():
        for plane in (hid, hid_moved, gc, gc_moved):
            clear_borders(plane)

        @pl.loop(0, 8)
        def _(tile):
            rows = pl.ds(pl.multiple_of((tile % 2) * HALF, HALF), HALF)
            cols = pl.ds(pl.multiple_of(tile * HALF, HALF), HALF)
            norm_turned[:, cols] = norm_ref[tile // 2, rows, :].T
            grad_turned[:, cols] = grad_ref[tile // 2, rows, :].T
            ffn_sum[tile // 2, rows, :] = jnp.zeros((HALF, D), F32)
            back_sum[tile // 2, rows, :] = jnp.zeros((HALF, D), F32)

    masks = column_masks(BODY, width)
    edge_masks = column_masks(EDGE, width)

    for group in range(4):
        value = nn(norm_ref[group], up[...])
        moved = moved_rows(value, group % 2, masks)
        for half in (0, 1):
            at = (group, pl.ds(body_offset(half, gap), HALF), slice(None))
            hid[at] = value[half * HALF : (half + 1) * HALF].astype(BF16)
            hid_moved[at] = moved[half * HALF : (half + 1) * HALF].astype(BF16)
        da[group] = nt(grad_ref[group], down[...]).astype(BF16)

    @pl.when(long_latent)
    def _():
        for group in range(4):
            at = (group, pl.ds(edge_offset(place), EDGE), slice(None))
            value = nn(norm_edge[group], up[...])
            hid[at] = value.astype(BF16)
            hid_moved[at] = moved_rows(value, group % 2, edge_masks).astype(BF16)
            da_edge[group] = nt(grad_edge[group], down[...]).astype(BF16)

    def rows_of(block):
        return slice(64 * block, 64 * block + 64)

    def plane_rows(block, tile):
        return pl.multiple_of(body_offset(block // 4, gap) + (block % 4) * 64 + tile * 32, 16)

    def accumulate(total, left, right, block):
        rows = rows_of(block)
        part = nn(left[:, rows, :].reshape(256, CHUNK), right)
        total[:, rows, :] += part.reshape(4, 64, D)

    down_now = down[...]
    up_turned = up[...].T

    for block in range(8):
        for lane in range(CHUNK // 128):
            lanes = pl.ds(lane * 128, 128)
            kernel = kernel_rows(taps, lanes, 32, BF16)
            for tile in range(2):
                offset = plane_rows(block, tile)
                found = variants(hid, hid_moved, offset, width, 32, lanes, BF16)
                rows = pl.ds(block * 64 + tile * 32, 32)
                for p in (0, 1):
                    for q in (0, 1):
                        group = 2 * p + q
                        value, slope = gelu_both(conv_at(found, kernel, p, q).astype(F32))
                        act[group, rows, lanes] = value.astype(BF16)
                        grad = slope * da[group, rows, lanes].astype(F32)
                        gc[group, pl.ds(offset, 32), lanes] = grad.astype(BF16)
                        gc_moved[group, pl.ds(offset, 32), lanes] = moved_rows(grad, q, edge_masks).astype(BF16)
        if block > 0:
            accumulate(ffn_sum, act, down_now, block - 1)
    accumulate(ffn_sum, act, down_now, 7)

    for side in (0, 1):

        @pl.when(jnp.logical_and(long_latent, place == side))
        def _(side=side):
            for lane in range(CHUNK // 128):
                lanes = pl.ds(lane * 128, 128)
                kernel = kernel_rows(taps, lanes, 32, BF16)
                offset = EDGE + BODY if side == 0 else 0
                found = {}
                for part, shift, where in ((0, 0, offset), (0, 1, offset + EDGE), (1, 0, offset), (1, -1, offset - EDGE)):
                    if where < 0 or where + 32 > PLANE:
                        continue
                    for column in (0, 1):
                        at = (2 * part + column, slice(where, where + 32), lanes)
                        found[part, shift, column, 0] = hid[at]
                        found[part, shift, column, 1] = hid_moved[at]
                for q in (0, 1):
                    group = 2 * side + q
                    slope = gelu_both(conv_at(found, kernel, side, q).astype(F32))[1]
                    grad = slope * da_edge[group, :, lanes].astype(F32)
                    gc[group, offset : offset + 32, lanes] = grad.astype(BF16)
                    gc_moved[group, offset : offset + 32, lanes] = moved_rows(grad, q, edge_masks).astype(BF16)

    for lane in range(CHUNK // 128):
        tap_sums[lane] = jnp.zeros((9, 8, 128), F32)
    for block in range(8):
        for lane in range(CHUNK // 128):
            lanes = pl.ds(lane * 128, 128)
            kernel = kernel_rows(taps, lanes, 32, BF16)
            for tile in range(2):
                offset = plane_rows(block, tile)
                rows = pl.ds(block * 64 + tile * 32, 32)
                found = variants(gc, gc_moved, offset, width, 32, lanes, BF16)
                for p in (0, 1):
                    for q in (0, 1):
                        gh[2 * p + q, rows, lanes] = conv_at(found, kernel, p, q, flip=True)
                fields = variants(hid, hid_moved, offset, width, 32, lanes, BF16)
                for index, total in enumerate(taps_at(found, fields)):
                    tap_sums[lane, index] += total
        if block > 0:
            accumulate(back_sum, gh, up_turned, block - 1)
    accumulate(back_sum, gh, up_turned, 7)
    for lane in range(CHUNK // 128):
        for index in range(9):
            taps_grad[0, index : index + 1, lane * 128 : (lane + 1) * 128] = jnp.sum(tap_sums[lane, index], 0, keepdims=True)

    def weight_grads(up_grad, down_grad):
        down_grad[...] = nn(grad_turned[...], act[...].reshape(4 * BODY, CHUNK)).T.astype(BF16)
        up_grad[0] = nn(norm_turned[...], gh[...].reshape(4 * BODY, CHUNK)).astype(BF16)

    @pl.when(step < steps // 2)
    def _():
        weight_grads(up_grad_own, down_grad_own)

    @pl.when(step >= steps // 2)
    def _():
        weight_grads(up_grad_other, down_grad_other)

    @pl.when(step == steps - 1)
    def _():
        ffn_out[...] = ffn_sum[...].astype(BF16)
        back_out[...] = back_sum[...].astype(BF16)


def taps_at(grads, fields):
    sums = []
    for a in (-1, 0, 1):
        for b in (-1, 0, 1):
            total = None
            for p in (0, 1):
                for q in (0, 1):
                    term = grads[p, 0, q, 0] * tap(fields, p, q, a, b)
                    total = term if total is None else total + term
            total = sum(total[at : at + 16] for at in range(0, total.shape[0], 16)).astype(F32)
            sums.append(total[0:8] + total[8:16])
    return sums


def feed_forward(scal, taps_own, taps_other, norm, norm_edge, grad, grad_edge, up_own, up_other, down_own, down_other):
    half = up_own.shape[1] // CHUNK
    steps = 2 * half
    body = jax.ShapeDtypeStruct((4, BODY, D), BF16)

    own, other = own_half(half), other_half(half)
    per = D // CHUNK
    plane = pltpu.VMEM((4, PLANE, CHUNK), BF16)
    small = pltpu.VMEM((4, BODY, CHUNK), BF16)
    return pl.pallas_call(
        ffn_kernel,
        grid=(steps,),
        out_shape=(
            body, body,
            *[jax.ShapeDtypeStruct((half // per, D, D), BF16)] * 2,
            *[jax.ShapeDtypeStruct((half * CHUNK, D), BF16)] * 2,
            jax.ShapeDtypeStruct((steps, 16, CHUNK), F32),
        ),
        in_specs=[
            scalars(),
            pl.BlockSpec((16, CHUNK), lambda i: (0, own(i))),
            pl.BlockSpec((16, CHUNK), lambda i: (0, other(i))),
            whole(norm.shape), whole(norm_edge.shape), whole(grad.shape), whole(grad_edge.shape),
            pl.BlockSpec((D, CHUNK), lambda i: (0, own(i))),
            pl.BlockSpec((D, CHUNK), lambda i: (0, other(i))),
            pl.BlockSpec((CHUNK, D), lambda i: (own(i), 0)),
            pl.BlockSpec((CHUNK, D), lambda i: (other(i), 0)),
        ],
        out_specs=(
            whole(body.shape), whole(body.shape),
            pl.BlockSpec((1, D, CHUNK), lambda i: (own(i) // per, 0, own(i) % per)),
            pl.BlockSpec((1, D, CHUNK), lambda i: (other(i) // per, 0, other(i) % per)),
            pl.BlockSpec((CHUNK, D), lambda i: (own(i), 0)),
            pl.BlockSpec((CHUNK, D), lambda i: (other(i), 0)),
            pl.BlockSpec((1, 16, CHUNK), lambda i: (i, 0, 0)),
        ),
        scratch_shapes=[
            plane, plane, plane, plane, small, small, small, pltpu.VMEM((4, EDGE, CHUNK), BF16),
            pltpu.VMEM((4, BODY, D), F32), pltpu.VMEM((4, BODY, D), F32),
            pltpu.VMEM((D, CHUNK), BF16), pltpu.VMEM((CHUNK, D), BF16), pltpu.VMEM((16, CHUNK), BF16),
            pltpu.VMEM((D, 4 * BODY), BF16), pltpu.VMEM((D, 4 * BODY), BF16),
            pltpu.VMEM((CHUNK // 128, 9, 8, 128), F32),
        ],
        compiler_params=params("arbitrary"),
        name="feed_forward",
    )(scal, taps_own, taps_other, norm, norm_edge, grad, grad_edge, up_own, up_other, down_own, down_other)


def turn_kernel(
    x_ref, attn_ref, ffn_ref, cot_ref, back_ref, mix_own, mix_other, perm_ref, mod_ref, own_ref, other_ref,
    out_ref, grad_ref, gmix_own, gmix_other, sums_ref, wgrad_own, wgrad_other,
    wsum,
):
    step = pl.program_id(0)
    gate_one = mod_ref[0, 2:3, :]
    scale = mod_ref[0, 4:5, :]
    gate_two = mod_ref[0, 5:6, :]

    @pl.when(step % 4 == 0)
    def _():
        sums_ref[...] = jnp.zeros_like(sums_ref)

    @pl.when(step == 0)
    def _():
        wsum[...] = jnp.zeros_like(wsum)

    result = None
    gattns = []
    for group in range(4):
        attn = attn_ref[group].astype(F32)
        ffn = ffn_ref[group].astype(F32)
        cot = cot_ref[group].astype(F32)
        back = back_ref[group].astype(F32)
        residual = x_ref[group].astype(F32) + gate_one * attn
        low = (residual + gate_two * ffn).astype(BF16)
        part = nn(perm_ref[:, 64 * group : 64 * group + 64], low)
        result = part if result is None else result + part
        normed, inverse = normalize(residual)
        grad = cot + norm_back(back * (1.0 + scale), normed, inverse)
        grad_ref[group] = grad.astype(BF16)
        for row, value in ((0, grad * attn), (1, back), (2, back * normed), (3, cot * ffn)):
            sums_ref[0, row : row + 1, :] += jnp.sum(value, 0, keepdims=True)
        gattn = (grad * gate_one).astype(BF16)
        gattns.append(gattn)
    gattn = jnp.concatenate(gattns, axis=0)
    for index, (mix, weight, gmix) in enumerate(((mix_own, own_ref, gmix_own), (mix_other, other_ref, gmix_other))):
        gmix[...] = nt(gattn, weight[...]).astype(BF16).reshape(4, 64, D // 2)
        wsum[index] += tn(mix[...].reshape(256, D // 2), gattn)
    out_ref[...] = result.astype(BF16)

    @pl.when(step == 7)
    def _():
        wgrad_own[...] = wsum[0].astype(BF16)
        wgrad_other[...] = wsum[1].astype(BF16)


def turn(x, attn, ffn, cot, back, mix, mix_other, perm, mod, weight, weight_other):
    block = pl.BlockSpec((4, 64, D), lambda i: (0, i, 0))
    part = pl.BlockSpec((4, 64, D // 2), lambda i: (0, i, 0))
    body = jax.ShapeDtypeStruct((4, BODY, D), BF16)
    half_body = jax.ShapeDtypeStruct((4, BODY, D // 2), BF16)
    half_weight = jax.ShapeDtypeStruct((D // 2, D), BF16)
    return pl.pallas_call(
        turn_kernel,
        grid=(8,),
        out_shape=(
            jax.ShapeDtypeStruct((2048, D), BF16), body, half_body, half_body,
            jax.ShapeDtypeStruct((2, 8, D), F32), half_weight, half_weight,
        ),
        in_specs=[block] * 5 + [part] * 2 + [
            whole(perm.shape), pl.BlockSpec((1, 8, D), lambda i: (i // 4, 0, 0)), whole(weight.shape), whole(weight.shape),
        ],
        out_specs=(
            pl.BlockSpec((256, D), lambda i: (i, 0)), block, part, part,
            pl.BlockSpec((1, 8, D), lambda i: (i // 4, 0, 0)), whole(weight.shape), whole(weight.shape),
        ),
        scratch_shapes=[pltpu.VMEM((2, D // 2, D), F32)],
        compiler_params=params("arbitrary"),
        name="turn",
    )(x, attn, ffn, cot, back, mix, mix_other, perm, mod, weight, weight_other)


def project_back_kernel(
    gq_own, gkv_own, add_own, gq_other, gkv_other, add_other, mixed_ref, order_ref, own_ref, other_ref,
    gmixed_ref, wgrad_own, wgrad_other,
    gsum, turned, triples, weights,
):
    step = pl.program_id(0)
    half_steps = pl.num_programs(0) // 2

    @pl.when(step == 0)
    def _():
        for tile in range(8):
            rows = slice((tile % 2) * HALF, (tile % 2 + 1) * HALF)
            turned[:, tile * HALF : (tile + 1) * HALF] = mixed_ref[tile // 2, rows, :].T

    def gather(gq_ref, gkv_ref, add_ref, weight_ref, pair):
        at = 384 * pair
        weights[:, at : at + 384] = nn(weight_ref[...], order_ref[...]).astype(BF16)
        for group in range(4):
            triples[group, :, at : at + 128] = gq_ref[0, group]
            for part in (0, 1):
                total = gkv_ref[0, part, group].astype(F32) + add_ref[0, part, group].astype(F32)
                triples[group, :, at + 128 * (part + 1) : at + 128 * (part + 2)] = total.astype(BF16)

    def finish(wgrad_ref, last):
        width = weights.shape[1]
        for group in range(4):
            part = nt(triples[group], weights[...])
            if last:
                gmixed_ref[group] = (gsum[group] + part).astype(BF16)
            else:
                gsum[group] = part
        wgrad = nn(turned[...], triples[...].reshape(4 * BODY, width)).astype(BF16)
        for at in range(0, width, 384):
            wgrad_ref[:, at : at + 384] = nt(wgrad[:, at : at + 384], order_ref[...]).astype(BF16)

    for half, refs in enumerate(((gq_own, gkv_own, add_own, own_ref), (gq_other, gkv_other, add_other, other_ref))):
        for pair in range(weights.shape[1] // 384):

            @pl.when(step == half * half_steps + pair)
            def _(refs=refs, pair=pair):
                gather(*refs, pair)

    @pl.when(step == half_steps - 1)
    def _():
        finish(wgrad_own, False)

    @pl.when(step == 2 * half_steps - 1)
    def _():
        finish(wgrad_other, True)


def project_back(own_grads, other_grads, mixed, order, weight, weight_other):
    half = own_grads[0].shape[0]
    own, other = own_half(half), other_half(half)

    def specs(at):
        kv_spec = pl.BlockSpec((1, 2, 4, BODY, 128), lambda i: (at(i), 0, 0, 0, 0))
        return [pl.BlockSpec((1, 4, BODY, 128), lambda i: (at(i), 0, 0, 0)), kv_spec, kv_spec]

    weight_specs = [pl.BlockSpec((D, 384), lambda i: (0, own(i))), pl.BlockSpec((D, 384), lambda i: (0, other(i)))]
    weight_shape = jax.ShapeDtypeStruct(weight.shape, BF16)
    return pl.pallas_call(
        project_back_kernel,
        grid=(2 * half,),
        out_shape=(jax.ShapeDtypeStruct((4, BODY, D), BF16), weight_shape, weight_shape),
        in_specs=[*specs(own), *specs(other), whole(mixed.shape), whole(order.shape), *weight_specs],
        out_specs=(whole((4, BODY, D)), whole(weight.shape), whole(weight.shape)),
        scratch_shapes=[
            pltpu.VMEM((4, BODY, D), F32), pltpu.VMEM((D, 4 * BODY), BF16),
            pltpu.VMEM((4, BODY, weight.shape[1]), BF16), pltpu.VMEM(weight.shape, BF16),
        ],
        compiler_params=params("arbitrary"),
        name="project_back",
    )(*own_grads, *other_grads, mixed, order, weight, weight_other)


def back_kernel(
    scal_ref, x_ref, gmixed_ref, gedge_ref, base_ref, shifted_ref, gres_ref, perm_ref, mod_ref, taps_ref,
    out_ref, sums_ref, taps_grad,
    gm, gm_moved, gnorm,
):
    width, gap, long_latent, place = geometry(scal_ref)
    clear_borders(gm)
    clear_borders(gm_moved)
    masks = column_masks(64, width)
    edge_masks = column_masks(EDGE, width)

    @pl.loop(0, 8)
    def _(block):
        place_in = pl.ds(pl.multiple_of(block * 64, 64), 64)
        place_out = pl.ds(pl.multiple_of(body_offset(block // 4, gap) + (block % 4) * 64, 16), 64)
        for group in range(4):
            value = gmixed_ref[group, place_in, :].astype(F32)
            gm[group, place_out, :] = value
            gm_moved[group, place_out, :] = moved_rows(value, group % 2, masks)

    @pl.when(long_latent)
    def _():
        at = pl.ds(edge_offset(place), EDGE)
        for group in range(4):
            value = gedge_ref[group].astype(F32)
            gm[group, at, :] = value
            gm_moved[group, at, :] = moved_rows(value, group % 2, edge_masks)

    for lane in range(D // 128):
        lanes = pl.ds(lane * 128, 128)
        kernel = kernel_rows(taps_ref, lanes, 16)

        def back_tile(tile, sums, lanes=lanes, kernel=kernel):
            offset = pl.multiple_of(body_offset(tile // 16, gap) + (tile % 16) * 16, 16)
            rows = pl.ds(pl.multiple_of(tile * 16, 16), 16)
            found = variants(gm, gm_moved, offset, width, 16, lanes)
            for p in (0, 1):
                for q in (0, 1):
                    gnorm[2 * p + q, rows, lanes] = conv_at(found, kernel, p, q, flip=True).astype(BF16)
            totals = taps_at(found, variants(base_ref, shifted_ref, offset, width, 16, lanes))
            return tuple(total + more for total, more in zip(sums, totals))

        sums = lax.fori_loop(0, 32, back_tile, (jnp.zeros((8, 128), F32),) * 9, unroll=2)
        for index in range(9):
            taps_grad[index : index + 1, lanes] = jnp.sum(sums[index], 0, keepdims=True)

    sums_ref[...] = jnp.zeros_like(sums_ref)

    @pl.loop(0, 8, unroll=2)
    def _(block):
        half = block // 4
        scale = mod_ref[half, 1:2, :]
        rows = pl.ds(pl.multiple_of(block * 64, 64), 64)
        result = None
        for group in range(4):
            normed, inverse = normalize(x_ref[group, rows, :].astype(F32))
            back = gnorm[group, rows, :].astype(F32)
            grad = gres_ref[group, rows, :].astype(F32) + norm_back(back * (1.0 + scale), normed, inverse)
            sums_ref[half, 0:1, :] += jnp.sum(back, 0, keepdims=True)
            sums_ref[half, 1:2, :] += jnp.sum(back * normed, 0, keepdims=True)
            part = nn(perm_ref[:, 64 * group : 64 * group + 64], grad.astype(BF16))
            result = part if result is None else result + part
        out_ref[pl.ds(pl.multiple_of(block * 256, 256), 256), :] = result.astype(BF16)


def back(scal, x, gmixed, gedge, base, shifted, gres, perm, mod, taps):
    arrays = (x, gmixed, gedge, base, shifted, gres, perm, mod, taps)
    plane = pltpu.VMEM((4, PLANE, D), F32)
    return pl.pallas_call(
        back_kernel,
        out_shape=(
            jax.ShapeDtypeStruct((2048, D), BF16),
            jax.ShapeDtypeStruct((2, 8, D), F32),
            jax.ShapeDtypeStruct((16, D), F32),
        ),
        in_specs=[scalars()] + [pl.BlockSpec(memory_space=pltpu.VMEM)] * len(arrays),
        out_specs=(pl.BlockSpec(memory_space=pltpu.VMEM),) * 3,
        scratch_shapes=[plane, plane, pltpu.VMEM((4, BODY, D), BF16)],
        compiler_params=params(),
        name="back",
    )(scal, *arrays)


MESH = pl.DeviceIdType.MESH


def chip_grid(count):
    return {16: (4, 2, 2), 64: (4, 4, 4)}.get(count, (count, 1, 1))


def reduce_gather_kernel(grid, units, *refs):
    own_refs, other_refs, sent_ref = refs[:units], refs[units : 2 * units], refs[2 * units]
    sum_refs, all_ref = refs[2 * units + 1 : 3 * units + 1], refs[3 * units + 1]
    scratch = refs[3 * units + 2 :]
    buffers = [scratch[10 * unit : 10 * unit + 10] for unit in range(units)]
    gz, gx, gy, sends, recvs = scratch[10 * units :]
    deep, tall, broad = grid
    low = deep // 2
    wide = lax.axis_index("wide")
    place = lax.axis_index("narrow")
    z, y, x = wide // (tall * broad), (wide // broad) % tall, wide % broad

    def chip(zz, yy, xx):
        return {"wide": (zz * tall + yy) * broad + xx, "narrow": place}

    def along_x(step):
        return chip(z, y, (x + step) % broad)

    def along_y(step):
        return chip(z, (y + step) % tall, x)

    def along_z(step):
        return chip((z + step) % deep, y, x)

    sibling = {"wide": wide, "narrow": 1 - place}
    partners = (
        [sibling]
        + [along_x(step) for step in range(1, broad)]
        + [along_y(step) for step in range(1, tall)]
        + [along_z(step) for step in range(1, deep)]
    )
    barrier = pltpu.get_barrier_semaphore()
    for partner in partners:
        pl.semaphore_signal(barrier, inc=1, device_id=partner, device_id_type=MESH)
    pl.semaphore_wait(barrier, len(partners))

    count = [0]

    def send(source, target, partner):
        copy = pltpu.make_async_remote_copy(
            src_ref=source, dst_ref=target, send_sem=sends.at[count[0]], recv_sem=recvs.at[count[0]],
            device_id=partner, device_id_type=MESH,
        )
        count[0] += 1
        copy.start()
        return copy

    def wait(copies):
        for copy in copies:
            copy.wait()

    def add(target, *sources):
        total = sources[0].astype(F32)
        for source in sources[1:]:
            total = total + source.astype(F32)
        return total.astype(target.dtype)

    gz[z] = sent_ref[...]
    halves = ((0, low), (low, deep))
    swaps = [
        [send(other.at[start:stop], buffer[0].at[start:stop], sibling) for other, buffer in zip(other_refs, buffers)]
        for start, stop in halves
    ]
    gathers = [send(sent_ref, gz.at[z], along_z(step)) for step in range(1, deep)]

    def add_first(start, stop):
        for own, (first, work, *_) in zip(own_refs, buffers):
            for zz in range(start, stop):

                @pl.loop(0, tall * broad)
                def _(at, zz=zz, own=own, first=first, work=work):
                    yy, xx = at // broad, at % broad
                    work[zz, yy, xx] = add(work, own[zz, yy, xx], first[zz, yy, xx])

    wait(swaps[0])
    add_first(0, low)
    one_a = [
        send(work.at[0:low, :, (x + s) % broad], r1a.at[s - 1], along_x(s))
        for _, work, r1a, *_ in buffers
        for s in range(1, broad)
    ]
    wait(swaps[1])
    add_first(low, deep)
    one_b = [
        send(work.at[low:deep, (y + s) % tall], r1b.at[s - 1], along_y(s))
        for _, work, _, r1b, *_ in buffers
        for s in range(1, tall)
    ]
    wait(gathers)
    gx[x] = gz[...]
    gathers = [send(gz, gx.at[x], along_x(step)) for step in range(1, broad)]

    wait(one_a)
    two_a = []
    for _, work, r1a, _, w1a, _, r2a, *_ in buffers:
        for zz in range(low):
            for yy in range(tall):
                w1a[zz, yy] = add(w1a, work[zz, yy, x], *[r1a[s, zz, yy] for s in range(broad - 1)])
        two_a += [send(w1a.at[:, (y + s) % tall], r2a.at[s - 1], along_y(s)) for s in range(1, tall)]
    wait(one_b)
    two_b = []
    for _, work, _, r1b, _, w1b, _, r2b, *_ in buffers:
        for zz in range(deep - low):
            for xx in range(broad):
                w1b[zz, xx] = add(w1b, work[low + zz, y, xx], *[r1b[s, zz, xx] for s in range(tall - 1)])
        two_b += [send(w1b.at[:, (x + s) % broad], r2b.at[s - 1], along_x(s)) for s in range(1, broad)]
    wait(gathers)
    gy[y] = gx[...]
    gathers = [send(gx, gy.at[y], along_y(step)) for step in range(1, tall)]

    wait(two_a)
    for _, _, _, _, w1a, _, r2a, _, w2, _ in buffers:
        for zz in range(low):
            w2[zz] = add(w2, w1a[zz, y], *[r2a[s, zz] for s in range(tall - 1)])
    wait(two_b)
    three = []
    for _, _, _, _, _, w1b, _, r2b, w2, r3 in buffers:
        for zz in range(deep - low):
            w2[low + zz] = add(w2, w1b[zz, x], *[r2b[s, zz] for s in range(broad - 1)])
        three += [send(w2.at[(z + s) % deep], r3.at[s - 1], along_z(s)) for s in range(1, deep)]
    wait(gathers)
    all_ref[place] = gy[...]
    gathers = [send(gy, all_ref.at[place], sibling)]
    wait(three)
    for sum_ref, buffer in zip(sum_refs, buffers):
        w2, r3 = buffer[8:]
        sum_ref[...] = add(sum_ref, w2[z], *[r3[s] for s in range(deep - 1)])
    wait(gathers)


def reduce_gather(own, other, sent):
    deep, tall, broad = grid = chip_grid(own[0].shape[0])
    low = deep // 2
    shapes = [array.shape[1:] for array in own]
    copies = len(own) * (2 + 2 * (broad - 1 + tall - 1) + (deep - 1)) + (deep - 1) + (broad - 1) + (tall - 1) + 1

    def buffers(unit):
        def slots(count, *shape):
            return pltpu.VMEM((max(count, 1), *shape, *unit), BF16)

        return [
            pltpu.VMEM((*grid, *unit), BF16), pltpu.VMEM((*grid, *unit), BF16),
            slots(broad - 1, low, tall), slots(tall - 1, deep - low, broad),
            pltpu.VMEM((low, tall, *unit), BF16), pltpu.VMEM((deep - low, broad, *unit), BF16),
            slots(tall - 1, low), slots(broad - 1, deep - low),
            pltpu.VMEM((deep, *unit), BF16), slots(deep - 1),
        ]

    row = sent.shape
    space = pl.BlockSpec(memory_space=pltpu.VMEM)
    result = pl.pallas_call(
        functools.partial(reduce_gather_kernel, grid, len(own)),
        out_shape=(
            *[jax.ShapeDtypeStruct(unit, F32) for unit in shapes],
            jax.ShapeDtypeStruct((2, tall, broad, deep, *row), BF16),
        ),
        in_specs=[space] * (2 * len(own) + 1),
        out_specs=(space,) * (len(own) + 1),
        scratch_shapes=[
            *[buffer for unit in shapes for buffer in buffers(unit)],
            pltpu.VMEM((deep, *row), BF16), pltpu.VMEM((broad, deep, *row), BF16),
            pltpu.VMEM((tall, broad, deep, *row), BF16),
            pltpu.SemaphoreType.DMA((copies,)), pltpu.SemaphoreType.DMA((copies,)),
        ],
        compiler_params=pltpu.CompilerParams(
            collective_id=1, has_side_effects=True, vmem_limit_bytes=VMEM_BYTES
        ),
        name="reduce_gather",
    )(*[array.reshape(*grid, *array.shape[1:]) for array in (*own, *other)], sent)
    return result[:-1], result[-1].reshape(-1, *row)


def square_sum_kernel(grid, *refs):
    count = len(refs) - 6
    grads = refs[:count]
    out_ref, mine, near, far, sends, recvs = refs[count:]
    deep, tall, broad = grid
    wide = lax.axis_index("wide")
    place = lax.axis_index("narrow")
    z, across = wide // (tall * broad), wide % (tall * broad)
    line = z * 2 + place

    def near_device(step):
        other = (line + step) % (2 * deep)
        return {"wide": (other // 2) * (tall * broad) + across, "narrow": other % 2}

    def far_device(step):
        return {"wide": z * (tall * broad) + (across + step) % (tall * broad), "narrow": place}

    nears = [near_device(step) for step in range(1, 2 * deep)]
    fars = [far_device(step) for step in range(1, tall * broad)]
    barrier = pltpu.get_barrier_semaphore()
    for partner in nears + fars:
        pl.semaphore_signal(barrier, inc=1, device_id=partner, device_id_type=MESH)

    total = jnp.zeros((), F32)
    for grad in grads:
        value = grad[...].astype(F32)
        total = total + jnp.sum(value * value)
    mine[...] = jnp.full((8, 128), total, F32)
    pl.semaphore_wait(barrier, len(nears + fars))

    def exchange(slots, partners, first):
        copies = []
        for step, partner in enumerate(partners):
            copy = pltpu.make_async_remote_copy(
                src_ref=mine, dst_ref=slots.at[step], send_sem=sends.at[first + step],
                recv_sem=recvs.at[first + step], device_id=partner, device_id_type=MESH,
            )
            copy.start()
            copies.append(copy)
        for copy in copies:
            copy.wait()
        value = mine[...]
        for step in range(len(partners)):
            value = value + slots[step]
        return value

    mine[...] = exchange(near, nears, 0)
    out_ref[...] = exchange(far, fars, len(nears))


def square_sum(wide_count, grads):
    deep, tall, broad = grid = chip_grid(wide_count)
    near, far = 2 * deep - 1, tall * broad - 1
    return pl.pallas_call(
        functools.partial(square_sum_kernel, grid),
        out_shape=jax.ShapeDtypeStruct((8, 128), F32),
        in_specs=[pl.BlockSpec(memory_space=pltpu.VMEM)] * len(grads),
        out_specs=pl.BlockSpec(memory_space=pltpu.VMEM),
        scratch_shapes=[
            pltpu.VMEM((8, 128), F32), pltpu.VMEM((near, 8, 128), F32), pltpu.VMEM((max(far, 1), 8, 128), F32),
            pltpu.SemaphoreType.DMA((near + far,)), pltpu.SemaphoreType.DMA((near + far,)),
        ],
        compiler_params=pltpu.CompilerParams(
            collective_id=2, has_side_effects=True, vmem_limit_bytes=VMEM_BYTES
        ),
        name="square_sum",
    )(*grads)


def shared_rows(shared_ref, rows):
    half = FF // 2 * rows // D
    shared = shared_ref[...].astype(F32)
    up = [shared[at : at + rows] for at in (0, rows)]
    down = shared[2 * rows : 2 * rows + half]
    out = shared[2 * rows + half : 2 * rows + half + rows // 2]
    return [[out], up, [down]]


def adamw_kernel(rates, square_ref, shared_ref, *refs):
    clip_limit = PARAMS**0.5
    norm = jnp.sqrt(square_ref[0:1, 0:1])
    factor = clip_limit / jnp.maximum(norm, clip_limit)
    plain = (len(refs) - 3 * 7) // 8
    count = plain + 3
    grads = [[ref[...]] for ref in refs[:plain]]
    states, outs = refs[plain : plain + 3 * count], refs[plain + 3 * count :]
    grads += shared_rows(shared_ref, states[3 * (plain + 1)].shape[0])
    for index, rate in enumerate(rates):
        master_ref, first_ref, second_ref = states[3 * index : 3 * index + 3]
        first_out, second_out, master_out, copy_out = outs[4 * index : 4 * index + 4]
        start = 0
        for grad in grads[index]:
            at = (slice(None), slice(start, start + grad.shape[1]))
            start += grad.shape[1]
            scaled = grad * factor
            first_new = BETA_ONE * first_ref[at] + (1.0 - BETA_ONE) * scaled
            second_new = BETA_TWO * second_ref[at] + (1.0 - BETA_TWO) * scaled * scaled
            ratio = (first_new * (1.0 / (1.0 - BETA_ONE**STEP))) / (
                jnp.sqrt(second_new * (1.0 / (1.0 - BETA_TWO**STEP))) + ADAM_EPS
            )
            master = master_ref[at]
            master_new = master - rate * (ratio + WEIGHT_DECAY * master)
            first_out[at] = first_new
            second_out[at] = second_new
            master_out[at] = master_new
            copy_out[at] = master_new.astype(BF16)


def adamw(square, shared, grads, states, rates):
    arrays = [array for state in states for array in state]
    shapes = [
        jax.ShapeDtypeStruct(state[0].shape, dtype) for state in states for dtype in (F32, F32, F32, BF16)
    ]
    space = pl.BlockSpec(memory_space=pltpu.VMEM)
    return pl.pallas_call(
        functools.partial(adamw_kernel, rates),
        out_shape=shapes,
        in_specs=[space] * (2 + len(grads) + len(arrays)),
        out_specs=[space] * len(shapes),
        compiler_params=params(),
        name="adamw",
    )(square, shared, *grads, *arrays)


def timestep_code(stamps, channels):
    half_dim = channels // 2
    scales = jnp.exp(-jnp.log(10000.0) * jnp.arange(half_dim, dtype=F32) / half_dim)
    angles = stamps.astype(F32)[:, None] * scales[None, :]
    return jnp.concatenate([jnp.cos(angles), jnp.sin(angles)], axis=1)


def one_hot_rows(source, columns, valid=None):
    hit = source[:, None] == jnp.arange(columns, dtype=jnp.int32)[None, :]
    if valid is not None:
        hit = jnp.logical_and(hit, valid[:, None])
    return hit.astype(BF16)


def permutation(long_latent):
    row = jnp.arange(256, dtype=jnp.int32)
    p, q, s = row // 128, (row // 64) % 2, row % 64
    big = (2 * (s // 32) + p) * 64 + 2 * (s % 32) + q
    small = (2 * (s // 16) + p) * 32 + 2 * (s % 16) + q
    return one_hot_rows(jnp.where(long_latent, big, small), 256)


def edge_permutation():
    row = jnp.arange(128, dtype=jnp.int32)
    return one_hot_rows((row // 64) * 64 + 2 * (row % 32) + (row // 32) % 2, 128)


def pair_order():
    row = jnp.arange(6 * HS, dtype=jnp.int32)
    return one_hot_rows((row % 192) // HS * 128 + row // 192 * HS + row % HS, 6 * HS)


def tap_rows(kernel):
    return jnp.pad(kernel.T, ((0, 7), (0, 0)))


def per_device(tokens, cotangent, size_tags, timesteps, labels, *weights_and_states):
    modulator, class_table, mix_kernel, heads_in, heads_out, up_weight, hidden_kernel, down_weight = weights_and_states[:8]
    states = [weights_and_states[8 + 3 * i : 11 + 3 * i] for i in range(8)]
    wide_count = lax.axis_size("wide")
    wide = lax.axis_index("wide")
    place = lax.axis_index("narrow")
    cell = wide * 2 + place
    cells = wide_count * 2

    def swap(value):
        return lax.ppermute(value, "narrow", [(0, 1), (1, 0)])

    def boundary(body):
        return jnp.where(place == 0, body[:, BODY - EDGE :], body[:, :EDGE])

    edge = swap(jnp.where(place == 0, tokens[-4 * EDGE :], tokens[: 4 * EDGE]))
    hin_other = swap(heads_in)
    hout_other = swap(heads_out)
    up_other = swap(up_weight)
    down_other = swap(down_weight)
    taps_own = tap_rows(hidden_kernel)
    taps_other = swap(taps_own)
    mix_taps = tap_rows(mix_kernel)

    long_latent = size_tags[0] > SIDE * SIDE
    width = jnp.where(long_latent, SIDE, SIDE // 2)
    gap = jnp.where(long_latent, 0, 16)
    scal = jnp.stack([width, gap, long_latent.astype(jnp.int32), place]).astype(jnp.int32)
    perm = permutation(long_latent)
    perm_back = perm.T
    order = pair_order()
    embedded = timestep_code(timesteps, D) + class_table[:, labels].astype(F32).T
    cond_low = jax.nn.silu(embedded).astype(BF16)
    modulation = jnp.dot(cond_low, modulator, preferred_element_type=F32).reshape(-1, 6, D)
    mod = jnp.pad(modulation, ((0, 0), (0, 2), (0, 0)))

    x, mixed, base, shifted, q, kv = front(
        scal, tokens, edge, perm, edge_permutation(), mod, mix_taps, order, heads_in
    )
    kv_far_other = swap(kv)
    q_other, kv_other = project(mixed, order, hin_other)
    kv_far = swap(kv_other)
    attended_other, logs_other = attention(scal, q_other, kv_other, kv_far_other)
    attended, logs = attention(scal, q, kv, kv_far)
    attn, norm, cot, grad_ffn = middle(x, attended, attended_other, cotangent, perm, mod, heads_out, hout_other)
    norm_edge, grad_edge = swap((boundary(norm), boundary(grad_ffn)))
    ffn, back_norm, up_grad, up_grad_other, down_grad, down_grad_other, taps_grad = feed_forward(
        scal, taps_own, taps_other, norm, norm_edge, grad_ffn, grad_edge, up_weight, up_other, down_weight, down_other
    )

    output, grad_residual, grad_attended, grad_attended_other, sums_two, hout_grad, hout_grad_other = turn(
        x, attn, ffn, cot, back_norm, attended, attended_other, perm_back, mod, heads_out, hout_other
    )
    rows = D // wide_count
    half = FF // 2
    up_sum = up_grad.astype(F32) + swap(up_grad_other).astype(F32)
    down_sum = down_grad.astype(F32) + swap(down_grad_other).astype(F32)
    hout_sum = hout_grad.astype(F32) + swap(hout_grad_other).astype(F32)
    tap_half = taps_grad.shape[0] // 2
    taps_sum = taps_grad[:tap_half, :9] + swap(taps_grad[tap_half:, :9])
    tap_part = taps_sum.transpose(0, 2, 1).reshape(wide_count, -1)
    tap_part = jnp.pad(tap_part, ((0, 0), (0, -tap_part.shape[1] % D)))
    grads = jnp.concatenate(
        [
            up_sum.reshape(2, wide_count, rows, D).transpose(1, 0, 2, 3).reshape(wide_count, 2 * rows, D),
            down_sum.reshape(wide_count, -1, D),
            hout_sum.reshape(wide_count, -1, D),
            tap_part.reshape(wide_count, -1, D),
        ],
        axis=1,
    )
    pad = -grads.shape[1] % 16
    grads = jnp.pad(grads, ((0, 0), (0, pad), (0, 0))).astype(BF16)
    grads, grad_attended_other = lax.optimization_barrier((grads, grad_attended_other))
    mine = lax.psum_scatter(grads, "wide", scatter_dimension=0, tiled=False)

    gq_other, gkv_other, gkv_far_other = attention_back(
        scal, q_other, kv_other, kv_far_other, attended_other, grad_attended_other, logs_other
    )
    gkv_add = swap(gkv_far_other)
    gq, gkv, gkv_far = attention_back(scal, q, kv, kv_far, attended, grad_attended, logs)
    gkv_add_other = swap(gkv_far)
    gmixed, hin_grad, hin_grad_other = project_back(
        (gq, gkv, gkv_add), (gq_other, gkv_other, gkv_add_other), mixed, order, heads_in, hin_other
    )
    gmixed_edge = swap(boundary(gmixed))
    input_grad, sums_one, mix_grad = back(
        scal, x, gmixed, gmixed_edge, base, shifted, grad_residual, perm_back, mod, mix_taps
    )

    modulation_two_grad = sums_two[:, 1:3].reshape(-1, 2 * D)
    own = D // cells
    mix_parts = mix_grad[:9].T.reshape(wide_count, 2, 1, own * 9).transpose(1, 0, 2, 3).astype(BF16)
    mix_parts = jnp.pad(mix_parts, ((0, 0), (0, 0), (0, 15), (0, -own * 9 % 128)))
    mix_own = jnp.where(place == 0, mix_parts[0], mix_parts[1])
    mix_other = jnp.where(place == 0, mix_parts[1], mix_parts[0])

    def by_chip(grad):
        split = grad.reshape(wide_count, rows, -1)
        return jnp.pad(split, ((0, 0), (0, -rows % 16), (0, 0)))

    slope = jax.vjp(jax.nn.silu, embedded)[1](jnp.ones_like(embedded))[0]
    blocks = jnp.concatenate([sums_one[:, 0:2], sums_two[:, 0:4]], axis=1).transpose(1, 0, 2).reshape(12, D)
    digits = jnp.stack([labels // 32, labels % 32], axis=1).astype(F32)
    digits = jnp.pad(digits, ((0, 14), (0, 126)))
    sent = jnp.concatenate([jnp.concatenate([blocks, cond_low.astype(F32), slope], axis=0), digits], axis=1)
    (hin_mine, mix_mine), everyone = reduce_gather(
        [by_chip(hin_grad), mix_own], [by_chip(hin_grad_other), mix_other], sent.astype(BF16)
    )
    row = jnp.arange(16, dtype=jnp.int32)
    block_row = 2 * jnp.arange(6, dtype=jnp.int32)[:, None] + jnp.arange(2, dtype=jnp.int32)
    picks = (block_row[:, :, None] == row).astype(F32)
    columns = lax.dynamic_slice_in_dim(everyone[:, 12:], cell * own, own, 2).astype(F32)
    all_cond, all_slope = columns[:, :2], columns[:, 2:]
    flat = everyone.reshape(cells * 16, -1)
    left = jnp.einsum("cfd,kfr->kdcr", all_cond, picks).astype(BF16).reshape(6 * own, cells * 16)
    modulator_mine = jnp.dot(left, flat, preferred_element_type=F32)[:, :D]
    modulator_mine = modulator_mine.reshape(6, own, D).transpose(1, 0, 2).reshape(own, 6 * D)
    modulator_rows = lax.dynamic_slice_in_dim(modulator, cell * own, own, 0).reshape(own, 6, D)
    modulator_rows = modulator_rows.transpose(1, 0, 2).reshape(6 * own, D)
    products = lax.dot_general(
        flat[:, :D], modulator_rows, (((1,), (1,)), ((), ())), preferred_element_type=F32
    ).reshape(cells, 16, 6, own)
    all_embedded = all_slope * jnp.stack(
        [sum(products[:, 2 * block + frame, block] for block in range(6)) for frame in range(2)], axis=1
    )
    all_digits = everyone[:, :2, D : D + 2].astype(jnp.int32)
    all_labels = (all_digits[..., 0] * 32 + all_digits[..., 1])[..., None]
    chosen = (all_labels == jnp.arange(class_table.shape[1], dtype=jnp.int32)).astype(F32)
    class_mine = jnp.dot(
        all_embedded.reshape(cells * 2, own).T, chosen.reshape(cells * 2, -1),
        precision=lax.Precision.HIGHEST, preferred_element_type=F32,
    )
    mix_mine = mix_mine[0, : own * 9].reshape(own, 9).T
    hin_mine = hin_mine[:rows]

    shared = 2 * rows + half // wide_count + rows // 2
    hidden = half // wide_count
    taps_mine = mine[shared:].reshape(-1)[: hidden * 9].reshape(hidden, 9).T.astype(F32)
    shards = (modulator_mine, class_mine, mix_mine, hin_mine, taps_mine)
    square = square_sum(wide_count, (*shards[:4], mine))
    grad_norm = jnp.sqrt(square[0, 0])
    order = (0, 1, 2, 3, 6, 4, 5, 7)
    step_rates = (
        D ** (-0.5), 1.0, 1.0 / 3.0, D ** (-0.5), 1.0 / 3.0, (D // 32) ** (-0.5), D ** (-0.5), FF ** (-0.5),
    )
    turned = (2, 6)
    given = [tuple(array.T for array in states[i]) if i in turned else states[i] for i in order]
    updated = adamw(square, mine, shards, given, step_rates)
    flat = [None] * 32
    for at, i in enumerate(order):
        for j in range(4):
            array = updated[4 * at + j]
            flat[4 * i + j] = array.T if i in turned else array
    return (output, input_grad, grad_norm, *flat, modulation_two_grad)


def solution(mesh):
    both = P(("wide", "narrow"), None)
    turned = P(("narrow", "wide"), None)
    grid = P("wide", "narrow")
    places = (both, both, both, grid, turned, grid, turned, turned)
    in_specs = (
        both, both, P("wide"), P(("wide", "narrow")), P(("wide", "narrow")),
        P(), P(), P(), P(None, "narrow"), P("narrow", None), P(None, "narrow"), P("narrow", None), P("narrow", None),
        *[place for place in places for _ in range(3)],
    )
    out_specs = (both, both, P(), *[place for place in places for _ in range(4)], both)
    return jax.shard_map(per_device, mesh=mesh, in_specs=in_specs, out_specs=out_specs, check_vma=False)
```

```python
import functools

import jax
import jax.numpy as jnp
from jax import lax
from jax.experimental import pallas as pl
from jax.experimental.pallas import tpu as pltpu
from jax.sharding import PartitionSpec as P

D = 768
HS = 64
FF = 3072
SIDE = 32
STEP = 10
PARAMS = 11419392

NORM_EPS = 1e-06
BETA_ONE = 0.5
BETA_TWO = 0.5
ADAM_EPS = 1e-08
WEIGHT_DECAY = 0.01

F32 = jnp.float32
BF16 = jnp.bfloat16

BODY = 512
HALF = 256
EDGE = 32
PLANE = 592
CHUNK = 256
VMEM_BYTES = 60 * 1024 * 1024


def params(*semantics):
    return pltpu.CompilerParams(
        dimension_semantics=semantics or None, vmem_limit_bytes=VMEM_BYTES
    )


def nn(left, right):
    return lax.dot_general(left, right, (((1,), (0,)), ((), ())), preferred_element_type=F32)


def nt(left, right):
    return lax.dot_general(left, right, (((1,), (1,)), ((), ())), preferred_element_type=F32)


def tn(left, right):
    return lax.dot_general(left, right, (((0,), (0,)), ((), ())), preferred_element_type=F32)


def whole(shape):
    return pl.BlockSpec(shape, lambda *_: (0,) * len(shape), pipeline_mode=pl.Buffered(1))


def scalars():
    return pl.BlockSpec(memory_space=pltpu.SMEM)


def geometry(scal_ref):
    return scal_ref[0], scal_ref[1], scal_ref[2] == 1, scal_ref[3]


def body_offset(half, gap):
    return pl.multiple_of(EDGE + half * (HALF + gap), 16)


def edge_offset(place):
    return pl.multiple_of(jnp.where(place == 0, EDGE + BODY, 0), 16)


def normalize(fields):
    center = fields - jnp.mean(fields, -1, keepdims=True)
    inverse = lax.rsqrt(jnp.mean(center * center, -1, keepdims=True) + NORM_EPS)
    return center * inverse, inverse


def norm_back(grad_hat, normed, inverse):
    return inverse * (
        grad_hat
        - jnp.mean(grad_hat, -1, keepdims=True)
        - normed * jnp.mean(grad_hat * normed, -1, keepdims=True)
    )


def variants(base, shifted, offset, width, rows, lanes, kind=F32):
    up = pl.multiple_of(offset - width, 16)
    down = pl.multiple_of(offset + width, 16)
    found = {}
    for part, shift, where in ((0, 0, offset), (0, 1, down), (1, 0, offset), (1, -1, up)):
        for column in (0, 1):
            at = (2 * part + column, pl.ds(where, rows), lanes)
            found[part, shift, column, 0] = base[at].astype(kind)
            found[part, shift, column, 1] = shifted[at].astype(kind)
    return found


def tap(found, p, q, a, b):
    part, shift = ((1, -1), (0, 0), (1, 0))[a + 1] if p == 0 else ((0, 0), (1, 0), (0, 1))[a + 1]
    column, moved = ((1, 1), (0, 0), (1, 0))[b + 1] if q == 0 else ((0, 0), (1, 0), (0, 1))[b + 1]
    return found[part, shift, column, moved]


def conv_at(found, kernel, p, q, flip=False):
    total = None
    for a in (-1, 0, 1):
        for b in (-1, 0, 1):
            index = 3 * (a + 1) + (b + 1)
            term = tap(found, p, q, a, b) * kernel[8 - index if flip else index]
            total = term if total is None else total + term
    return total


def kernel_rows(kernel_ref, lanes, rows, kind=F32):
    return [
        jnp.broadcast_to(kernel_ref[index : index + 1, lanes].astype(kind), (rows, lanes.size)) for index in range(9)
    ]


def clear_borders(plane, wide_gap=True):
    zeros = jnp.zeros((4, EDGE, plane.shape[2]), plane.dtype)
    plane[:, 0:EDGE, :] = zeros
    plane[:, EDGE + HALF : EDGE + HALF + EDGE, :] = zeros
    plane[:, EDGE + BODY : EDGE + BODY + EDGE, :] = zeros
    plane[:, PLANE - EDGE : PLANE, :] = zeros


def column_masks(rows, width):
    column = lax.broadcasted_iota(jnp.int32, (rows, 128), 0) & (width - 1)
    return column != width - 1, column != 0


def moved_rows(value, column, masks):
    rows, lanes = value.shape
    moved = pltpu.roll(value, rows - 1 if column == 0 else 1, 0)
    parts = [jnp.where(masks[column], moved[:, at : at + 128], 0.0) for at in range(0, lanes, 128)]
    return parts[0] if len(parts) == 1 else jnp.concatenate(parts, axis=1)


def own_half(half):
    return lambda i: jnp.minimum(i, half - 1)


def other_half(half):
    return lambda i: jnp.maximum(i - half, 0)


def front_kernel(
    scal_ref, x_ref, edge_ref, perm_ref, edge_perm_ref, mod_ref, taps_ref, order_ref, weight_ref,
    x_out, mixed_out, base_out, shifted_out, q_out, kv_out,
):
    width, gap, long_latent, place = geometry(scal_ref)
    @pl.when(pl.program_id(0) == 0)
    def _():
        clear_borders(base_out)
        clear_borders(shifted_out)
        masks = column_masks(64, width)
        edge_masks = column_masks(EDGE, width)

        @pl.loop(0, 8, unroll=2)
        def _(block):
            half = block // 4
            rows = x_ref[pl.ds(pl.multiple_of(block * 256, 256), 256), :]
            shift = mod_ref[half, 0:1, :]
            scale = mod_ref[half, 1:2, :]
            place_in = pl.ds(pl.multiple_of(block * 64, 64), 64)
            place_out = pl.ds(pl.multiple_of(body_offset(half, gap) + (block % 4) * 64, 16), 64)
            groups = [nn(perm_ref[64 * group : 64 * group + 64, :], rows) for group in range(4)]
            for group, picked in enumerate(groups):
                x_out[group, place_in, :] = picked.astype(BF16)
                normed = normalize(picked)[0]
                value = normed * (1.0 + scale) + shift
                base_out[group, place_out, :] = value.astype(BF16)
                shifted_out[group, place_out, :] = moved_rows(value, group % 2, masks).astype(BF16)

        @pl.when(long_latent)
        def _():
            at = pl.ds(edge_offset(place), EDGE)
            for group in range(4):
                picked = nn(edge_perm_ref[32 * group : 32 * group + 32, :], edge_ref[...])
                normed = normalize(picked)[0]
                value = normed * (1.0 + mod_ref[0, 1:2, :]) + mod_ref[0, 0:1, :]
                base_out[group, at, :] = value.astype(BF16)
                shifted_out[group, at, :] = moved_rows(value, group % 2, edge_masks).astype(BF16)

        for lane in range(D // 128):
            lanes = pl.ds(lane * 128, 128)
            kernel = kernel_rows(taps_ref, lanes, 16)

            @pl.loop(0, 32, unroll=4)
            def _(tile, lanes=lanes, kernel=kernel):
                offset = body_offset(tile // 16, gap) + (tile % 16) * 16
                found = variants(base_out, shifted_out, pl.multiple_of(offset, 16), width, 16, lanes)
                for p in (0, 1):
                    for q in (0, 1):
                        at = (2 * p + q, pl.ds(pl.multiple_of(tile * 16, 16), 16), lanes)
                        mixed_out[at] = conv_at(found, kernel, p, q).astype(BF16)

    project_kernel(mixed_out, order_ref, weight_ref, q_out, kv_out)


def project_kernel(mixed_ref, order_ref, weight_ref, q_out, kv_out):
    weight = nn(weight_ref[...], order_ref[...]).astype(BF16)
    for group in range(4):
        triple = nn(mixed_ref[group], weight)
        q_out[0, group] = (triple[:, 0:128] * (HS**-0.5)).astype(BF16)
        kv_out[0, 0, group] = triple[:, 128:256].astype(BF16)
        kv_out[0, 1, group] = triple[:, 256:384].astype(BF16)


def project_specs(pairs):
    shapes = (
        jax.ShapeDtypeStruct((pairs, 4, BODY, 128), BF16),
        jax.ShapeDtypeStruct((pairs, 2, 4, BODY, 128), BF16),
    )
    blocks = (
        pl.BlockSpec((1, 4, BODY, 128), lambda i: (i, 0, 0, 0)),
        pl.BlockSpec((1, 2, 4, BODY, 128), lambda i: (i, 0, 0, 0, 0)),
    )
    return shapes, blocks, pl.BlockSpec((D, 384), lambda i: (0, i))


def front(scal, x, edge, perm, edge_perm, mod, taps, order, weight):
    pairs = weight.shape[1] // 384
    shapes, blocks, weight_block = project_specs(pairs)
    plane = jax.ShapeDtypeStruct((4, PLANE, D), BF16)
    body = jax.ShapeDtypeStruct((4, BODY, D), BF16)
    return pl.pallas_call(
        front_kernel,
        grid=(pairs,),
        out_shape=(body, body, plane, plane, *shapes),
        in_specs=[
            scalars(), whole(x.shape), whole(edge.shape), whole(perm.shape), whole(edge_perm.shape),
            whole(mod.shape), whole(taps.shape), whole(order.shape), weight_block,
        ],
        out_specs=(whole(body.shape), whole(body.shape), whole(plane.shape), whole(plane.shape), *blocks),
        compiler_params=params("arbitrary"),
        name="front",
    )(scal, x, edge, perm, edge_perm, mod, taps, order, weight)


def project(mixed, order, weight):
    pairs = weight.shape[1] // 384
    shapes, blocks, weight_block = project_specs(pairs)
    return pl.pallas_call(
        project_kernel,
        grid=(pairs,),
        out_shape=shapes,
        in_specs=[whole(mixed.shape), whole(order.shape), weight_block],
        out_specs=blocks,
        compiler_params=params("arbitrary"),
        name="project",
    )(mixed, order, weight)


def head_mask(rows, head):
    lane = lax.broadcasted_iota(jnp.int32, (rows, 128), 1)
    return (lane < HS) if head == 0 else (lane >= HS)


def pieces(first, second, rows):
    lane = lax.broadcasted_iota(jnp.int32, (rows, 128), 1)
    value = jnp.where(lane < HS, first, second)
    one = value.astype(BF16).astype(F32)
    two = (value - one).astype(BF16).astype(F32)
    three = value - one - two
    turn = lane % HS
    picked = jnp.where(turn == 0, one, jnp.where(turn == 1, two, jnp.where(turn == 2, three, 0.0)))
    return picked.astype(BF16)


def unit_pieces(rows):
    lane = lax.broadcasted_iota(jnp.int32, (rows, 128), 1)
    return jnp.where(lane % HS < 3, 1.0, 0.0).astype(BF16)


def attend_kernel(scal_ref, q_ref, own_ref, other_ref, out_ref, log_ref):
    long_latent = scal_ref[2] == 1

    def products(query, keys):
        found = []
        for head in (0, 1):
            masked = jnp.where(head_mask(query.shape[0], head), query, jnp.zeros_like(query))
            found.append([nt(masked, key) for key in keys])
        return found

    def attend(head_scores, values, rows):
        mixes, logs = [], []
        for scores in head_scores:
            highest = jnp.max(scores[0], -1, keepdims=True)
            for other in scores[1:]:
                highest = jnp.maximum(highest, jnp.max(other, -1, keepdims=True))
            mix = None
            for score, value in zip(scores, values):
                share = jnp.exp(score - highest).astype(BF16)
                part = nn(share, value)
                mix = part if mix is None else mix + part
            total = mix[:, 128:256]
            mixes.append(mix[:, 0:128] / total)
            logs.append(highest + jnp.log(total))
        mix = jnp.where(head_mask(rows, 0), mixes[0], mixes[1])
        return mix.astype(BF16), pieces(-logs[0], -logs[1], rows)

    def with_ones(value):
        return jnp.concatenate([value, jnp.ones_like(value)], axis=1)

    @pl.when(long_latent)
    def _():
        keys = [own_ref[0, 0, 0], other_ref[0, 0, 0]]
        values = [with_ones(own_ref[0, 1, 0]), with_ones(other_ref[0, 1, 0])]
        tiles = [pl.ds(tile * 128, 128) for tile in range(4)]
        scores = [products(q_ref[0, 0, at, :], keys) for at in tiles]
        for at, score in zip(tiles, scores):
            out_ref[0, at, :], log_ref[0, 0, at, :] = attend(score, values, 128)

    @pl.when(jnp.logical_not(long_latent))
    def _():
        tiles = [pl.ds(tile * 256, 256) for tile in range(2)]
        scores = [products(q_ref[0, 0, at, :], [own_ref[0, 0, 0, at, :]]) for at in tiles]
        for at, score in zip(tiles, scores):
            out_ref[0, at, :], log_ref[0, 0, at, :] = attend(score, [with_ones(own_ref[0, 1, 0, at, :])], 256)


def attention(scal, q, own, other):
    pairs = q.shape[0]
    pair_spec = pl.BlockSpec((1, 1, BODY, 128), lambda p, g: (p, g, 0, 0))
    kv_spec = pl.BlockSpec((1, 2, 1, BODY, 128), lambda p, g: (p, 0, g, 0, 0))
    return pl.pallas_call(
        attend_kernel,
        grid=(pairs, 4),
        out_shape=(
            jax.ShapeDtypeStruct((4, BODY, 128 * pairs), BF16),
            jax.ShapeDtypeStruct((pairs, 4, BODY, 128), BF16),
        ),
        in_specs=[scalars(), pair_spec, kv_spec, kv_spec],
        out_specs=(pl.BlockSpec((1, BODY, 128), lambda p, g: (g, 0, p)), pair_spec),
        compiler_params=params("arbitrary", "arbitrary"),
        name="attention",
    )(scal, q, own, other)


def attend_back_kernel(
    scal_ref, q_ref, own_ref, other_ref, mix_ref, grad_ref, log_ref, gq_ref, gown_ref, gother_ref
):
    long_latent = scal_ref[2] == 1

    def side(query, mix, grad, log):
        rows = query.shape[0]
        product = mix.astype(F32) * grad.astype(F32)
        deltas = [
            jnp.sum(jnp.where(head_mask(rows, head), product, 0.0), -1, keepdims=True) for head in (0, 1)
        ]
        delta = pieces(-deltas[0], -deltas[1], rows)
        result = []
        for head in (0, 1):
            mask = head_mask(rows, head)
            zero = jnp.zeros_like(query)
            q_head = jnp.where(mask, query, zero)
            g_head = jnp.where(mask, grad, zero)
            q_more = jnp.concatenate([q_head, jnp.where(mask, log, zero)], axis=1)
            g_more = jnp.concatenate([g_head, jnp.where(mask, delta, zero)], axis=1)
            result.append((q_head, g_head, q_more, g_more))
        return result

    def keys_ahead(heads, key, value):
        ones = unit_pieces(key.shape[0])
        key_more = jnp.concatenate([key, ones], axis=1)
        value_more = jnp.concatenate([value, ones], axis=1)
        return [(nt(key_more, q_more), nt(value_more, g_more)) for _, _, q_more, g_more in heads]

    def keys_part(heads, key, ahead):
        key_turned = key.astype(F32).T.astype(BF16)
        gk = gv = None
        turned = []
        for (q_head, g_head, _, _), (score, slope) in zip(heads, ahead):
            share = jnp.exp(score)
            slope = (share * slope).astype(BF16)
            share = share.astype(BF16)
            gv_part = nn(share, g_head)
            gk_part = nn(slope, q_head)
            gv = gv_part if gv is None else gv + gv_part
            gk = gk_part if gk is None else gk + gk_part
            turned.append(nn(key_turned, slope))
        return gk, gv, turned

    def query_grad(turned):
        row = lax.broadcasted_iota(jnp.int32, turned[0].shape, 0)
        both = jnp.where(row < HS, turned[0], turned[1]) * (HS**-0.5)
        return both.T.astype(BF16)

    @pl.when(long_latent)
    def _():
        heads = side(q_ref[0, 0], mix_ref[0], grad_ref[0], log_ref[0, 0])
        totals = None
        ahead = [keys_ahead(heads, source[0, 0, 0], source[0, 1, 0]) for source in (own_ref, other_ref)]
        for source, target, products in ((own_ref, gown_ref, ahead[0]), (other_ref, gother_ref, ahead[1])):
            gk, gv, turned = keys_part(heads, source[0, 0, 0], products)
            target[0, 0, 0] = gk.astype(BF16)
            target[0, 1, 0] = gv.astype(BF16)
            totals = turned if totals is None else [a + b for a, b in zip(totals, turned)]
        gq_ref[0, 0] = query_grad(totals)

    @pl.when(jnp.logical_not(long_latent))
    def _():
        for tile in range(2):
            at = pl.ds(tile * 256, 256)
            heads = side(q_ref[0, 0, at, :], mix_ref[0, at, :], grad_ref[0, at, :], log_ref[0, 0, at, :])
            key = own_ref[0, 0, 0, at, :]
            gk, gv, turned = keys_part(heads, key, keys_ahead(heads, key, own_ref[0, 1, 0, at, :]))
            gown_ref[0, 0, 0, at, :] = gk.astype(BF16)
            gown_ref[0, 1, 0, at, :] = gv.astype(BF16)
            gq_ref[0, 0, at, :] = query_grad(turned)
        gother_ref[...] = jnp.zeros_like(gother_ref)


def attention_back(scal, q, own, other, mix, grad, log):
    pairs = q.shape[0]
    pair_spec = pl.BlockSpec((1, 1, BODY, 128), lambda p, g: (p, g, 0, 0))
    kv_spec = pl.BlockSpec((1, 2, 1, BODY, 128), lambda p, g: (p, 0, g, 0, 0))
    lane_spec = pl.BlockSpec((1, BODY, 128), lambda p, g: (g, 0, p))
    return pl.pallas_call(
        attend_back_kernel,
        grid=(pairs, 4),
        out_shape=(
            jax.ShapeDtypeStruct(q.shape, BF16),
            jax.ShapeDtypeStruct(own.shape, BF16),
            jax.ShapeDtypeStruct(own.shape, BF16),
        ),
        in_specs=[scalars(), pair_spec, kv_spec, kv_spec, lane_spec, lane_spec, pair_spec],
        out_specs=(pair_spec, kv_spec, kv_spec),
        compiler_params=params("arbitrary", "arbitrary"),
        name="attention_back",
    )(scal, q, own, other, mix, grad, log)


def middle_kernel(
    x_ref, mix_own, mix_other, cot_ref, perm_ref, mod_ref, own_ref, other_ref, attn_out, norm_out, cot_out, grad_out
):
    gate_one = mod_ref[0, 2:3, :]
    shift = mod_ref[0, 3:4, :]
    scale = mod_ref[0, 4:5, :]
    gate_two = mod_ref[0, 5:6, :]
    own = nn(mix_own[...].reshape(256, D // 2), own_ref[...])
    attns = own + nn(mix_other[...].reshape(256, D // 2), other_ref[...])
    cots = nn(perm_ref[...], cot_ref[...])
    for group in range(4):
        attn_low = attns[64 * group : 64 * group + 64].astype(BF16)
        attn_out[group] = attn_low
        residual = x_ref[group].astype(F32) + gate_one * attn_low.astype(F32)
        norm_out[group] = (normalize(residual)[0] * (1.0 + scale) + shift).astype(BF16)
        cot = cots[64 * group : 64 * group + 64]
        cot_out[group] = cot.astype(BF16)
        grad_out[group] = (cot * gate_two).astype(BF16)


def middle(x, mix, mix_other, cot, perm, mod, weight, weight_other):
    part = pl.BlockSpec((4, 64, D // 2), lambda i: (0, i, 0))
    block = pl.BlockSpec((4, 64, D), lambda i: (0, i, 0))
    body = jax.ShapeDtypeStruct((4, BODY, D), BF16)
    return pl.pallas_call(
        middle_kernel,
        grid=(8,),
        out_shape=(body,) * 4,
        in_specs=[
            block, part, part, pl.BlockSpec((256, D), lambda i: (i, 0)), whole(perm.shape),
            pl.BlockSpec((1, 8, D), lambda i: (i // 4, 0, 0)), whole(weight.shape), whole(weight.shape),
        ],
        out_specs=(block,) * 4,
        compiler_params=params("arbitrary"),
        name="middle",
    )(x, mix, mix_other, cot, perm, mod, weight, weight_other)


def gelu_both(value):
    root = 0.7978845608028654
    square = value * value
    angle = value * (root + (root * 0.044715) * square)
    bent = jnp.tanh(angle)
    half = 0.5 + 0.5 * bent
    inner = (0.5 * root) + (1.5 * root * 0.044715) * square
    return value * half, half + value * (1.0 - bent * bent) * inner


def ffn_kernel(
    scal_ref, taps_own, taps_other, norm_ref, norm_edge, grad_ref, grad_edge,
    up_own, up_other, down_own, down_other,
    ffn_out, back_out, up_grad_own, up_grad_other, down_grad_own, down_grad_other, taps_grad,
    hid, hid_moved, gc, gc_moved, act, gh, da, da_edge, ffn_sum, back_sum, up, down, taps, norm_turned, grad_turned, tap_sums,
):
    width, gap, long_latent, place = geometry(scal_ref)
    step = pl.program_id(0)
    steps = pl.num_programs(0)

    @pl.when(step < steps // 2)
    def _():
        up[...] = up_own[...]
        down[...] = down_own[...]
        taps[...] = taps_own[...]

    @pl.when(step >= steps // 2)
    def _():
        up[...] = up_other[...]
        down[...] = down_other[...]
        taps[...] = taps_other[...]

    @pl.when(step == 0)
    def _():
        for plane in (hid, hid_moved, gc, gc_moved):
            clear_borders(plane)

        @pl.loop(0, 8)
        def _(tile):
            rows = pl.ds(pl.multiple_of((tile % 2) * HALF, HALF), HALF)
            cols = pl.ds(pl.multiple_of(tile * HALF, HALF), HALF)
            norm_turned[:, cols] = norm_ref[tile // 2, rows, :].T
            grad_turned[:, cols] = grad_ref[tile // 2, rows, :].T
            ffn_sum[tile // 2, rows, :] = jnp.zeros((HALF, D), F32)
            back_sum[tile // 2, rows, :] = jnp.zeros((HALF, D), F32)

    masks = column_masks(BODY, width)
    edge_masks = column_masks(EDGE, width)

    for group in range(4):
        value = nn(norm_ref[group], up[...])
        moved = moved_rows(value, group % 2, masks)
        for half in (0, 1):
            at = (group, pl.ds(body_offset(half, gap), HALF), slice(None))
            hid[at] = value[half * HALF : (half + 1) * HALF].astype(BF16)
            hid_moved[at] = moved[half * HALF : (half + 1) * HALF].astype(BF16)
        da[group] = nt(grad_ref[group], down[...]).astype(BF16)

    @pl.when(long_latent)
    def _():
        for group in range(4):
            at = (group, pl.ds(edge_offset(place), EDGE), slice(None))
            value = nn(norm_edge[group], up[...])
            hid[at] = value.astype(BF16)
            hid_moved[at] = moved_rows(value, group % 2, edge_masks).astype(BF16)
            da_edge[group] = nt(grad_edge[group], down[...]).astype(BF16)

    def rows_of(block):
        return slice(64 * block, 64 * block + 64)

    def plane_rows(block, tile):
        return pl.multiple_of(body_offset(block // 4, gap) + (block % 4) * 64 + tile * 32, 16)

    def accumulate(total, left, right, block):
        rows = rows_of(block)
        part = nn(left[:, rows, :].reshape(256, CHUNK), right)
        total[:, rows, :] += part.reshape(4, 64, D)

    down_now = down[...]
    up_turned = up[...].T

    for block in range(8):
        for lane in range(CHUNK // 128):
            lanes = pl.ds(lane * 128, 128)
            kernel = kernel_rows(taps, lanes, 32, BF16)
            for tile in range(2):
                offset = plane_rows(block, tile)
                found = variants(hid, hid_moved, offset, width, 32, lanes, BF16)
                rows = pl.ds(block * 64 + tile * 32, 32)
                for p in (0, 1):
                    for q in (0, 1):
                        group = 2 * p + q
                        value, slope = gelu_both(conv_at(found, kernel, p, q).astype(F32))
                        act[group, rows, lanes] = value.astype(BF16)
                        grad = slope * da[group, rows, lanes].astype(F32)
                        gc[group, pl.ds(offset, 32), lanes] = grad.astype(BF16)
                        gc_moved[group, pl.ds(offset, 32), lanes] = moved_rows(grad, q, edge_masks).astype(BF16)
        if block > 0:
            accumulate(ffn_sum, act, down_now, block - 1)
    accumulate(ffn_sum, act, down_now, 7)

    for side in (0, 1):

        @pl.when(jnp.logical_and(long_latent, place == side))
        def _(side=side):
            for lane in range(CHUNK // 128):
                lanes = pl.ds(lane * 128, 128)
                kernel = kernel_rows(taps, lanes, 32, BF16)
                offset = EDGE + BODY if side == 0 else 0
                found = {}
                for part, shift, where in ((0, 0, offset), (0, 1, offset + EDGE), (1, 0, offset), (1, -1, offset - EDGE)):
                    if where < 0 or where + 32 > PLANE:
                        continue
                    for column in (0, 1):
                        at = (2 * part + column, slice(where, where + 32), lanes)
                        found[part, shift, column, 0] = hid[at]
                        found[part, shift, column, 1] = hid_moved[at]
                for q in (0, 1):
                    group = 2 * side + q
                    slope = gelu_both(conv_at(found, kernel, side, q).astype(F32))[1]
                    grad = slope * da_edge[group, :, lanes].astype(F32)
                    gc[group, offset : offset + 32, lanes] = grad.astype(BF16)
                    gc_moved[group, offset : offset + 32, lanes] = moved_rows(grad, q, edge_masks).astype(BF16)

    for lane in range(CHUNK // 128):
        tap_sums[lane] = jnp.zeros((9, 8, 128), F32)
    for block in range(8):
        for lane in range(CHUNK // 128):
            lanes = pl.ds(lane * 128, 128)
            kernel = kernel_rows(taps, lanes, 32, BF16)
            for tile in range(2):
                offset = plane_rows(block, tile)
                rows = pl.ds(block * 64 + tile * 32, 32)
                found = variants(gc, gc_moved, offset, width, 32, lanes, BF16)
                for p in (0, 1):
                    for q in (0, 1):
                        gh[2 * p + q, rows, lanes] = conv_at(found, kernel, p, q, flip=True)
                fields = variants(hid, hid_moved, offset, width, 32, lanes, BF16)
                for index, total in enumerate(taps_at(found, fields)):
                    tap_sums[lane, index] += total
        if block > 0:
            accumulate(back_sum, gh, up_turned, block - 1)
    accumulate(back_sum, gh, up_turned, 7)
    for lane in range(CHUNK // 128):
        for index in range(9):
            taps_grad[0, index : index + 1, lane * 128 : (lane + 1) * 128] = jnp.sum(tap_sums[lane, index], 0, keepdims=True)

    def weight_grads(up_grad, down_grad):
        down_grad[...] = nn(grad_turned[...], act[...].reshape(4 * BODY, CHUNK)).T.astype(BF16)
        up_grad[0] = nn(norm_turned[...], gh[...].reshape(4 * BODY, CHUNK)).astype(BF16)

    @pl.when(step < steps // 2)
    def _():
        weight_grads(up_grad_own, down_grad_own)

    @pl.when(step >= steps // 2)
    def _():
        weight_grads(up_grad_other, down_grad_other)

    @pl.when(step == steps - 1)
    def _():
        ffn_out[...] = ffn_sum[...].astype(BF16)
        back_out[...] = back_sum[...].astype(BF16)


def taps_at(grads, fields):
    sums = []
    for a in (-1, 0, 1):
        for b in (-1, 0, 1):
            total = None
            for p in (0, 1):
                for q in (0, 1):
                    term = grads[p, 0, q, 0] * tap(fields, p, q, a, b)
                    total = term if total is None else total + term
            total = sum(total[at : at + 16] for at in range(0, total.shape[0], 16)).astype(F32)
            sums.append(total[0:8] + total[8:16])
    return sums


def feed_forward(scal, taps_own, taps_other, norm, norm_edge, grad, grad_edge, up_own, up_other, down_own, down_other):
    half = up_own.shape[1] // CHUNK
    steps = 2 * half
    body = jax.ShapeDtypeStruct((4, BODY, D), BF16)

    own, other = own_half(half), other_half(half)
    per = D // CHUNK
    plane = pltpu.VMEM((4, PLANE, CHUNK), BF16)
    small = pltpu.VMEM((4, BODY, CHUNK), BF16)
    return pl.pallas_call(
        ffn_kernel,
        grid=(steps,),
        out_shape=(
            body, body,
            *[jax.ShapeDtypeStruct((half // per, D, D), BF16)] * 2,
            *[jax.ShapeDtypeStruct((half * CHUNK, D), BF16)] * 2,
            jax.ShapeDtypeStruct((steps, 16, CHUNK), F32),
        ),
        in_specs=[
            scalars(),
            pl.BlockSpec((16, CHUNK), lambda i: (0, own(i))),
            pl.BlockSpec((16, CHUNK), lambda i: (0, other(i))),
            whole(norm.shape), whole(norm_edge.shape), whole(grad.shape), whole(grad_edge.shape),
            pl.BlockSpec((D, CHUNK), lambda i: (0, own(i))),
            pl.BlockSpec((D, CHUNK), lambda i: (0, other(i))),
            pl.BlockSpec((CHUNK, D), lambda i: (own(i), 0)),
            pl.BlockSpec((CHUNK, D), lambda i: (other(i), 0)),
        ],
        out_specs=(
            whole(body.shape), whole(body.shape),
            pl.BlockSpec((1, D, CHUNK), lambda i: (own(i) // per, 0, own(i) % per)),
            pl.BlockSpec((1, D, CHUNK), lambda i: (other(i) // per, 0, other(i) % per)),
            pl.BlockSpec((CHUNK, D), lambda i: (own(i), 0)),
            pl.BlockSpec((CHUNK, D), lambda i: (other(i), 0)),
            pl.BlockSpec((1, 16, CHUNK), lambda i: (i, 0, 0)),
        ),
        scratch_shapes=[
            plane, plane, plane, plane, small, small, small, pltpu.VMEM((4, EDGE, CHUNK), BF16),
            pltpu.VMEM((4, BODY, D), F32), pltpu.VMEM((4, BODY, D), F32),
            pltpu.VMEM((D, CHUNK), BF16), pltpu.VMEM((CHUNK, D), BF16), pltpu.VMEM((16, CHUNK), BF16),
            pltpu.VMEM((D, 4 * BODY), BF16), pltpu.VMEM((D, 4 * BODY), BF16),
            pltpu.VMEM((CHUNK // 128, 9, 8, 128), F32),
        ],
        compiler_params=params("arbitrary"),
        name="feed_forward",
    )(scal, taps_own, taps_other, norm, norm_edge, grad, grad_edge, up_own, up_other, down_own, down_other)


def turn_kernel(
    x_ref, attn_ref, ffn_ref, cot_ref, back_ref, mix_own, mix_other, perm_ref, mod_ref, own_ref, other_ref,
    out_ref, grad_ref, gmix_own, gmix_other, sums_ref, wgrad_own, wgrad_other,
    wsum,
):
    step = pl.program_id(0)
    gate_one = mod_ref[0, 2:3, :]
    scale = mod_ref[0, 4:5, :]
    gate_two = mod_ref[0, 5:6, :]

    @pl.when(step % 4 == 0)
    def _():
        sums_ref[...] = jnp.zeros_like(sums_ref)

    @pl.when(step == 0)
    def _():
        wsum[...] = jnp.zeros_like(wsum)

    result = None
    gattns = []
    for group in range(4):
        attn = attn_ref[group].astype(F32)
        ffn = ffn_ref[group].astype(F32)
        cot = cot_ref[group].astype(F32)
        back = back_ref[group].astype(F32)
        residual = x_ref[group].astype(F32) + gate_one * attn
        low = (residual + gate_two * ffn).astype(BF16)
        part = nn(perm_ref[:, 64 * group : 64 * group + 64], low)
        result = part if result is None else result + part
        normed, inverse = normalize(residual)
        grad = cot + norm_back(back * (1.0 + scale), normed, inverse)
        grad_ref[group] = grad.astype(BF16)
        for row, value in ((0, grad * attn), (1, back), (2, back * normed), (3, cot * ffn)):
            sums_ref[0, row : row + 1, :] += jnp.sum(value, 0, keepdims=True)
        gattn = (grad * gate_one).astype(BF16)
        gattns.append(gattn)
    gattn = jnp.concatenate(gattns, axis=0)
    for index, (mix, weight, gmix) in enumerate(((mix_own, own_ref, gmix_own), (mix_other, other_ref, gmix_other))):
        gmix[...] = nt(gattn, weight[...]).astype(BF16).reshape(4, 64, D // 2)
        wsum[index] += tn(mix[...].reshape(256, D // 2), gattn)
    out_ref[...] = result.astype(BF16)

    @pl.when(step == 7)
    def _():
        wgrad_own[...] = wsum[0].astype(BF16)
        wgrad_other[...] = wsum[1].astype(BF16)


def turn(x, attn, ffn, cot, back, mix, mix_other, perm, mod, weight, weight_other):
    block = pl.BlockSpec((4, 64, D), lambda i: (0, i, 0))
    part = pl.BlockSpec((4, 64, D // 2), lambda i: (0, i, 0))
    body = jax.ShapeDtypeStruct((4, BODY, D), BF16)
    half_body = jax.ShapeDtypeStruct((4, BODY, D // 2), BF16)
    half_weight = jax.ShapeDtypeStruct((D // 2, D), BF16)
    return pl.pallas_call(
        turn_kernel,
        grid=(8,),
        out_shape=(
            jax.ShapeDtypeStruct((2048, D), BF16), body, half_body, half_body,
            jax.ShapeDtypeStruct((2, 8, D), F32), half_weight, half_weight,
        ),
        in_specs=[block] * 5 + [part] * 2 + [
            whole(perm.shape), pl.BlockSpec((1, 8, D), lambda i: (i // 4, 0, 0)), whole(weight.shape), whole(weight.shape),
        ],
        out_specs=(
            pl.BlockSpec((256, D), lambda i: (i, 0)), block, part, part,
            pl.BlockSpec((1, 8, D), lambda i: (i // 4, 0, 0)), whole(weight.shape), whole(weight.shape),
        ),
        scratch_shapes=[pltpu.VMEM((2, D // 2, D), F32)],
        compiler_params=params("arbitrary"),
        name="turn",
    )(x, attn, ffn, cot, back, mix, mix_other, perm, mod, weight, weight_other)


def project_back_kernel(
    gq_own, gkv_own, add_own, gq_other, gkv_other, add_other, mixed_ref, order_ref, own_ref, other_ref,
    gmixed_ref, wgrad_own, wgrad_other,
    gsum, turned, triples, weights,
):
    step = pl.program_id(0)
    half_steps = pl.num_programs(0) // 2

    @pl.when(step == 0)
    def _():
        for tile in range(8):
            rows = slice((tile % 2) * HALF, (tile % 2 + 1) * HALF)
            turned[:, tile * HALF : (tile + 1) * HALF] = mixed_ref[tile // 2, rows, :].T

    def gather(gq_ref, gkv_ref, add_ref, weight_ref, pair):
        at = 384 * pair
        weights[:, at : at + 384] = nn(weight_ref[...], order_ref[...]).astype(BF16)
        for group in range(4):
            triples[group, :, at : at + 128] = gq_ref[0, group]
            for part in (0, 1):
                total = gkv_ref[0, part, group].astype(F32) + add_ref[0, part, group].astype(F32)
                triples[group, :, at + 128 * (part + 1) : at + 128 * (part + 2)] = total.astype(BF16)

    def finish(wgrad_ref, last):
        width = weights.shape[1]
        for group in range(4):
            part = nt(triples[group], weights[...])
            if last:
                gmixed_ref[group] = (gsum[group] + part).astype(BF16)
            else:
                gsum[group] = part
        wgrad = nn(turned[...], triples[...].reshape(4 * BODY, width)).astype(BF16)
        for at in range(0, width, 384):
            wgrad_ref[:, at : at + 384] = nt(wgrad[:, at : at + 384], order_ref[...]).astype(BF16)

    for half, refs in enumerate(((gq_own, gkv_own, add_own, own_ref), (gq_other, gkv_other, add_other, other_ref))):
        for pair in range(weights.shape[1] // 384):

            @pl.when(step == half * half_steps + pair)
            def _(refs=refs, pair=pair):
                gather(*refs, pair)

    @pl.when(step == half_steps - 1)
    def _():
        finish(wgrad_own, False)

    @pl.when(step == 2 * half_steps - 1)
    def _():
        finish(wgrad_other, True)


def project_back(own_grads, other_grads, mixed, order, weight, weight_other):
    half = own_grads[0].shape[0]
    own, other = own_half(half), other_half(half)

    def specs(at):
        kv_spec = pl.BlockSpec((1, 2, 4, BODY, 128), lambda i: (at(i), 0, 0, 0, 0))
        return [pl.BlockSpec((1, 4, BODY, 128), lambda i: (at(i), 0, 0, 0)), kv_spec, kv_spec]

    weight_specs = [pl.BlockSpec((D, 384), lambda i: (0, own(i))), pl.BlockSpec((D, 384), lambda i: (0, other(i)))]
    weight_shape = jax.ShapeDtypeStruct(weight.shape, BF16)
    return pl.pallas_call(
        project_back_kernel,
        grid=(2 * half,),
        out_shape=(jax.ShapeDtypeStruct((4, BODY, D), BF16), weight_shape, weight_shape),
        in_specs=[*specs(own), *specs(other), whole(mixed.shape), whole(order.shape), *weight_specs],
        out_specs=(whole((4, BODY, D)), whole(weight.shape), whole(weight.shape)),
        scratch_shapes=[
            pltpu.VMEM((4, BODY, D), F32), pltpu.VMEM((D, 4 * BODY), BF16),
            pltpu.VMEM((4, BODY, weight.shape[1]), BF16), pltpu.VMEM(weight.shape, BF16),
        ],
        compiler_params=params("arbitrary"),
        name="project_back",
    )(*own_grads, *other_grads, mixed, order, weight, weight_other)


def back_kernel(
    scal_ref, x_ref, gmixed_ref, gedge_ref, base_ref, shifted_ref, gres_ref, perm_ref, mod_ref, taps_ref,
    out_ref, sums_ref, taps_grad,
    gm, gm_moved, gnorm,
):
    width, gap, long_latent, place = geometry(scal_ref)
    clear_borders(gm)
    clear_borders(gm_moved)
    masks = column_masks(64, width)
    edge_masks = column_masks(EDGE, width)

    @pl.loop(0, 8)
    def _(block):
        place_in = pl.ds(pl.multiple_of(block * 64, 64), 64)
        place_out = pl.ds(pl.multiple_of(body_offset(block // 4, gap) + (block % 4) * 64, 16), 64)
        for group in range(4):
            value = gmixed_ref[group, place_in, :].astype(F32)
            gm[group, place_out, :] = value
            gm_moved[group, place_out, :] = moved_rows(value, group % 2, masks)

    @pl.when(long_latent)
    def _():
        at = pl.ds(edge_offset(place), EDGE)
        for group in range(4):
            value = gedge_ref[group].astype(F32)
            gm[group, at, :] = value
            gm_moved[group, at, :] = moved_rows(value, group % 2, edge_masks)

    for lane in range(D // 128):
        lanes = pl.ds(lane * 128, 128)
        kernel = kernel_rows(taps_ref, lanes, 16)

        def back_tile(tile, sums, lanes=lanes, kernel=kernel):
            offset = pl.multiple_of(body_offset(tile // 16, gap) + (tile % 16) * 16, 16)
            rows = pl.ds(pl.multiple_of(tile * 16, 16), 16)
            found = variants(gm, gm_moved, offset, width, 16, lanes)
            for p in (0, 1):
                for q in (0, 1):
                    gnorm[2 * p + q, rows, lanes] = conv_at(found, kernel, p, q, flip=True).astype(BF16)
            totals = taps_at(found, variants(base_ref, shifted_ref, offset, width, 16, lanes))
            return tuple(total + more for total, more in zip(sums, totals))

        sums = lax.fori_loop(0, 32, back_tile, (jnp.zeros((8, 128), F32),) * 9, unroll=2)
        for index in range(9):
            taps_grad[index : index + 1, lanes] = jnp.sum(sums[index], 0, keepdims=True)

    sums_ref[...] = jnp.zeros_like(sums_ref)

    @pl.loop(0, 8, unroll=2)
    def _(block):
        half = block // 4
        scale = mod_ref[half, 1:2, :]
        rows = pl.ds(pl.multiple_of(block * 64, 64), 64)
        result = None
        for group in range(4):
            normed, inverse = normalize(x_ref[group, rows, :].astype(F32))
            back = gnorm[group, rows, :].astype(F32)
            grad = gres_ref[group, rows, :].astype(F32) + norm_back(back * (1.0 + scale), normed, inverse)
            sums_ref[half, 0:1, :] += jnp.sum(back, 0, keepdims=True)
            sums_ref[half, 1:2, :] += jnp.sum(back * normed, 0, keepdims=True)
            part = nn(perm_ref[:, 64 * group : 64 * group + 64], grad.astype(BF16))
            result = part if result is None else result + part
        out_ref[pl.ds(pl.multiple_of(block * 256, 256), 256), :] = result.astype(BF16)


def back(scal, x, gmixed, gedge, base, shifted, gres, perm, mod, taps):
    arrays = (x, gmixed, gedge, base, shifted, gres, perm, mod, taps)
    plane = pltpu.VMEM((4, PLANE, D), F32)
    return pl.pallas_call(
        back_kernel,
        out_shape=(
            jax.ShapeDtypeStruct((2048, D), BF16),
            jax.ShapeDtypeStruct((2, 8, D), F32),
            jax.ShapeDtypeStruct((16, D), F32),
        ),
        in_specs=[scalars()] + [pl.BlockSpec(memory_space=pltpu.VMEM)] * len(arrays),
        out_specs=(pl.BlockSpec(memory_space=pltpu.VMEM),) * 3,
        scratch_shapes=[plane, plane, pltpu.VMEM((4, BODY, D), BF16)],
        compiler_params=params(),
        name="back",
    )(scal, *arrays)


MESH = pl.DeviceIdType.MESH


def chip_grid(count):
    return {16: (4, 2, 2), 64: (4, 4, 4)}.get(count, (count, 1, 1))


def reduce_gather_kernel(grid, units, *refs):
    own_refs, other_refs, sent_ref = refs[:units], refs[units : 2 * units], refs[2 * units]
    sum_refs, all_ref = refs[2 * units + 1 : 3 * units + 1], refs[3 * units + 1]
    scratch = refs[3 * units + 2 :]
    buffers = [scratch[10 * unit : 10 * unit + 10] for unit in range(units)]
    gz, gx, gy, sends, recvs = scratch[10 * units :]
    deep, tall, broad = grid
    low = deep // 2
    wide = lax.axis_index("wide")
    place = lax.axis_index("narrow")
    z, y, x = wide // (tall * broad), (wide // broad) % tall, wide % broad

    def chip(zz, yy, xx):
        return {"wide": (zz * tall + yy) * broad + xx, "narrow": place}

    def along_x(step):
        return chip(z, y, (x + step) % broad)

    def along_y(step):
        return chip(z, (y + step) % tall, x)

    def along_z(step):
        return chip((z + step) % deep, y, x)

    sibling = {"wide": wide, "narrow": 1 - place}
    partners = (
        [sibling]
        + [along_x(step) for step in range(1, broad)]
        + [along_y(step) for step in range(1, tall)]
        + [along_z(step) for step in range(1, deep)]
    )
    barrier = pltpu.get_barrier_semaphore()
    for partner in partners:
        pl.semaphore_signal(barrier, inc=1, device_id=partner, device_id_type=MESH)
    pl.semaphore_wait(barrier, len(partners))

    count = [0]

    def send(source, target, partner):
        copy = pltpu.make_async_remote_copy(
            src_ref=source, dst_ref=target, send_sem=sends.at[count[0]], recv_sem=recvs.at[count[0]],
            device_id=partner, device_id_type=MESH,
        )
        count[0] += 1
        copy.start()
        return copy

    def wait(copies):
        for copy in copies:
            copy.wait()

    def add(target, *sources):
        total = sources[0].astype(F32)
        for source in sources[1:]:
            total = total + source.astype(F32)
        return total.astype(target.dtype)

    gz[z] = sent_ref[...]
    halves = ((0, low), (low, deep))
    swaps = [
        [send(other.at[start:stop], buffer[0].at[start:stop], sibling) for other, buffer in zip(other_refs, buffers)]
        for start, stop in halves
    ]
    gathers = [send(sent_ref, gz.at[z], along_z(step)) for step in range(1, deep)]

    def add_first(start, stop):
        for own, (first, work, *_) in zip(own_refs, buffers):
            for zz in range(start, stop):

                @pl.loop(0, tall * broad)
                def _(at, zz=zz, own=own, first=first, work=work):
                    yy, xx = at // broad, at % broad
                    work[zz, yy, xx] = add(work, own[zz, yy, xx], first[zz, yy, xx])

    wait(swaps[0])
    add_first(0, low)
    one_a = [
        send(work.at[0:low, :, (x + s) % broad], r1a.at[s - 1], along_x(s))
        for _, work, r1a, *_ in buffers
        for s in range(1, broad)
    ]
    wait(swaps[1])
    add_first(low, deep)
    one_b = [
        send(work.at[low:deep, (y + s) % tall], r1b.at[s - 1], along_y(s))
        for _, work, _, r1b, *_ in buffers
        for s in range(1, tall)
    ]
    wait(gathers)
    gx[x] = gz[...]
    gathers = [send(gz, gx.at[x], along_x(step)) for step in range(1, broad)]

    wait(one_a)
    two_a = []
    for _, work, r1a, _, w1a, _, r2a, *_ in buffers:
        for zz in range(low):
            for yy in range(tall):
                w1a[zz, yy] = add(w1a, work[zz, yy, x], *[r1a[s, zz, yy] for s in range(broad - 1)])
        two_a += [send(w1a.at[:, (y + s) % tall], r2a.at[s - 1], along_y(s)) for s in range(1, tall)]
    wait(one_b)
    two_b = []
    for _, work, _, r1b, _, w1b, _, r2b, *_ in buffers:
        for zz in range(deep - low):
            for xx in range(broad):
                w1b[zz, xx] = add(w1b, work[low + zz, y, xx], *[r1b[s, zz, xx] for s in range(tall - 1)])
        two_b += [send(w1b.at[:, (x + s) % broad], r2b.at[s - 1], along_x(s)) for s in range(1, broad)]
    wait(gathers)
    gy[y] = gx[...]
    gathers = [send(gx, gy.at[y], along_y(step)) for step in range(1, tall)]

    wait(two_a)
    for _, _, _, _, w1a, _, r2a, _, w2, _ in buffers:
        for zz in range(low):
            w2[zz] = add(w2, w1a[zz, y], *[r2a[s, zz] for s in range(tall - 1)])
    wait(two_b)
    three = []
    for _, _, _, _, _, w1b, _, r2b, w2, r3 in buffers:
        for zz in range(deep - low):
            w2[low + zz] = add(w2, w1b[zz, x], *[r2b[s, zz] for s in range(broad - 1)])
        three += [send(w2.at[(z + s) % deep], r3.at[s - 1], along_z(s)) for s in range(1, deep)]
    wait(gathers)
    all_ref[place] = gy[...]
    gathers = [send(gy, all_ref.at[place], sibling)]
    wait(three)
    for sum_ref, buffer in zip(sum_refs, buffers):
        w2, r3 = buffer[8:]
        sum_ref[...] = add(sum_ref, w2[z], *[r3[s] for s in range(deep - 1)])
    wait(gathers)


def reduce_gather(own, other, sent):
    deep, tall, broad = grid = chip_grid(own[0].shape[0])
    low = deep // 2
    shapes = [array.shape[1:] for array in own]
    copies = len(own) * (2 + 2 * (broad - 1 + tall - 1) + (deep - 1)) + (deep - 1) + (broad - 1) + (tall - 1) + 1

    def buffers(unit):
        def slots(count, *shape):
            return pltpu.VMEM((max(count, 1), *shape, *unit), BF16)

        return [
            pltpu.VMEM((*grid, *unit), BF16), pltpu.VMEM((*grid, *unit), BF16),
            slots(broad - 1, low, tall), slots(tall - 1, deep - low, broad),
            pltpu.VMEM((low, tall, *unit), BF16), pltpu.VMEM((deep - low, broad, *unit), BF16),
            slots(tall - 1, low), slots(broad - 1, deep - low),
            pltpu.VMEM((deep, *unit), BF16), slots(deep - 1),
        ]

    row = sent.shape
    space = pl.BlockSpec(memory_space=pltpu.VMEM)
    result = pl.pallas_call(
        functools.partial(reduce_gather_kernel, grid, len(own)),
        out_shape=(
            *[jax.ShapeDtypeStruct(unit, F32) for unit in shapes],
            jax.ShapeDtypeStruct((2, tall, broad, deep, *row), BF16),
        ),
        in_specs=[space] * (2 * len(own) + 1),
        out_specs=(space,) * (len(own) + 1),
        scratch_shapes=[
            *[buffer for unit in shapes for buffer in buffers(unit)],
            pltpu.VMEM((deep, *row), BF16), pltpu.VMEM((broad, deep, *row), BF16),
            pltpu.VMEM((tall, broad, deep, *row), BF16),
            pltpu.SemaphoreType.DMA((copies,)), pltpu.SemaphoreType.DMA((copies,)),
        ],
        compiler_params=pltpu.CompilerParams(
            collective_id=1, has_side_effects=True, vmem_limit_bytes=VMEM_BYTES
        ),
        name="reduce_gather",
    )(*[array.reshape(*grid, *array.shape[1:]) for array in (*own, *other)], sent)
    return result[:-1], result[-1].reshape(-1, *row)


def square_sum_kernel(grid, *refs):
    count = len(refs) - 6
    grads = refs[:count]
    out_ref, mine, near, far, sends, recvs = refs[count:]
    deep, tall, broad = grid
    wide = lax.axis_index("wide")
    place = lax.axis_index("narrow")
    z, across = wide // (tall * broad), wide % (tall * broad)
    line = z * 2 + place

    def near_device(step):
        other = (line + step) % (2 * deep)
        return {"wide": (other // 2) * (tall * broad) + across, "narrow": other % 2}

    def far_device(step):
        return {"wide": z * (tall * broad) + (across + step) % (tall * broad), "narrow": place}

    nears = [near_device(step) for step in range(1, 2 * deep)]
    fars = [far_device(step) for step in range(1, tall * broad)]
    barrier = pltpu.get_barrier_semaphore()
    for partner in nears + fars:
        pl.semaphore_signal(barrier, inc=1, device_id=partner, device_id_type=MESH)

    total = jnp.zeros((), F32)
    for grad in grads:
        value = grad[...].astype(F32)
        total = total + jnp.sum(value * value)
    mine[...] = jnp.full((8, 128), total, F32)
    pl.semaphore_wait(barrier, len(nears + fars))

    def exchange(slots, partners, first):
        copies = []
        for step, partner in enumerate(partners):
            copy = pltpu.make_async_remote_copy(
                src_ref=mine, dst_ref=slots.at[step], send_sem=sends.at[first + step],
                recv_sem=recvs.at[first + step], device_id=partner, device_id_type=MESH,
            )
            copy.start()
            copies.append(copy)
        for copy in copies:
            copy.wait()
        value = mine[...]
        for step in range(len(partners)):
            value = value + slots[step]
        return value

    mine[...] = exchange(near, nears, 0)
    out_ref[...] = exchange(far, fars, len(nears))


def square_sum(wide_count, grads):
    deep, tall, broad = grid = chip_grid(wide_count)
    near, far = 2 * deep - 1, tall * broad - 1
    return pl.pallas_call(
        functools.partial(square_sum_kernel, grid),
        out_shape=jax.ShapeDtypeStruct((8, 128), F32),
        in_specs=[pl.BlockSpec(memory_space=pltpu.VMEM)] * len(grads),
        out_specs=pl.BlockSpec(memory_space=pltpu.VMEM),
        scratch_shapes=[
            pltpu.VMEM((8, 128), F32), pltpu.VMEM((near, 8, 128), F32), pltpu.VMEM((max(far, 1), 8, 128), F32),
            pltpu.SemaphoreType.DMA((near + far,)), pltpu.SemaphoreType.DMA((near + far,)),
        ],
        compiler_params=pltpu.CompilerParams(
            collective_id=2, has_side_effects=True, vmem_limit_bytes=VMEM_BYTES
        ),
        name="square_sum",
    )(*grads)


def shared_rows(shared_ref, rows):
    half = FF // 2 * rows // D
    shared = shared_ref[...].astype(F32)
    up = [shared[at : at + rows] for at in (0, rows)]
    down = shared[2 * rows : 2 * rows + half]
    out = shared[2 * rows + half : 2 * rows + half + rows // 2]
    return [[out], up, [down]]


def adamw_kernel(rates, square_ref, shared_ref, *refs):
    clip_limit = PARAMS**0.5
    norm = jnp.sqrt(square_ref[0:1, 0:1])
    factor = clip_limit / jnp.maximum(norm, clip_limit)
    plain = (len(refs) - 3 * 7) // 8
    count = plain + 3
    grads = [[ref[...]] for ref in refs[:plain]]
    states, outs = refs[plain : plain + 3 * count], refs[plain + 3 * count :]
    grads += shared_rows(shared_ref, states[3 * (plain + 1)].shape[0])
    for index, rate in enumerate(rates):
        master_ref, first_ref, second_ref = states[3 * index : 3 * index + 3]
        first_out, second_out, master_out, copy_out = outs[4 * index : 4 * index + 4]
        start = 0
        for grad in grads[index]:
            at = (slice(None), slice(start, start + grad.shape[1]))
            start += grad.shape[1]
            scaled = grad * factor
            first_new = BETA_ONE * first_ref[at] + (1.0 - BETA_ONE) * scaled
            second_new = BETA_TWO * second_ref[at] + (1.0 - BETA_TWO) * scaled * scaled
            ratio = (first_new * (1.0 / (1.0 - BETA_ONE**STEP))) / (
                jnp.sqrt(second_new * (1.0 / (1.0 - BETA_TWO**STEP))) + ADAM_EPS
            )
            master = master_ref[at]
            master_new = master - rate * (ratio + WEIGHT_DECAY * master)
            first_out[at] = first_new
            second_out[at] = second_new
            master_out[at] = master_new
            copy_out[at] = master_new.astype(BF16)


def adamw(square, shared, grads, states, rates):
    arrays = [array for state in states for array in state]
    shapes = [
        jax.ShapeDtypeStruct(state[0].shape, dtype) for state in states for dtype in (F32, F32, F32, BF16)
    ]
    space = pl.BlockSpec(memory_space=pltpu.VMEM)
    return pl.pallas_call(
        functools.partial(adamw_kernel, rates),
        out_shape=shapes,
        in_specs=[space] * (2 + len(grads) + len(arrays)),
        out_specs=[space] * len(shapes),
        compiler_params=params(),
        name="adamw",
    )(square, shared, *grads, *arrays)


def timestep_code(stamps, channels):
    half_dim = channels // 2
    scales = jnp.exp(-jnp.log(10000.0) * jnp.arange(half_dim, dtype=F32) / half_dim)
    angles = stamps.astype(F32)[:, None] * scales[None, :]
    return jnp.concatenate([jnp.cos(angles), jnp.sin(angles)], axis=1)


def one_hot_rows(source, columns, valid=None):
    hit = source[:, None] == jnp.arange(columns, dtype=jnp.int32)[None, :]
    if valid is not None:
        hit = jnp.logical_and(hit, valid[:, None])
    return hit.astype(BF16)


def permutation(long_latent):
    row = jnp.arange(256, dtype=jnp.int32)
    p, q, s = row // 128, (row // 64) % 2, row % 64
    big = (2 * (s // 32) + p) * 64 + 2 * (s % 32) + q
    small = (2 * (s // 16) + p) * 32 + 2 * (s % 16) + q
    return one_hot_rows(jnp.where(long_latent, big, small), 256)


def edge_permutation():
    row = jnp.arange(128, dtype=jnp.int32)
    return one_hot_rows((row // 64) * 64 + 2 * (row % 32) + (row // 32) % 2, 128)


def pair_order():
    row = jnp.arange(6 * HS, dtype=jnp.int32)
    return one_hot_rows((row % 192) // HS * 128 + row // 192 * HS + row % HS, 6 * HS)


def tap_rows(kernel):
    return jnp.pad(kernel.T, ((0, 7), (0, 0)))


def per_device(tokens, cotangent, size_tags, timesteps, labels, *weights_and_states):
    modulator, class_table, mix_kernel, heads_in, heads_out, up_weight, hidden_kernel, down_weight = weights_and_states[:8]
    states = [weights_and_states[8 + 3 * i : 11 + 3 * i] for i in range(8)]
    wide_count = lax.axis_size("wide")
    wide = lax.axis_index("wide")
    place = lax.axis_index("narrow")
    cell = wide * 2 + place
    cells = wide_count * 2

    def swap(value):
        return lax.ppermute(value, "narrow", [(0, 1), (1, 0)])

    def boundary(body):
        return jnp.where(place == 0, body[:, BODY - EDGE :], body[:, :EDGE])

    edge = swap(jnp.where(place == 0, tokens[-4 * EDGE :], tokens[: 4 * EDGE]))
    hin_other = swap(heads_in)
    hout_other = swap(heads_out)
    up_other = swap(up_weight)
    down_other = swap(down_weight)
    taps_own = tap_rows(hidden_kernel)
    taps_other = swap(taps_own)
    mix_taps = tap_rows(mix_kernel)

    long_latent = size_tags[0] > SIDE * SIDE
    width = jnp.where(long_latent, SIDE, SIDE // 2)
    gap = jnp.where(long_latent, 0, 16)
    scal = jnp.stack([width, gap, long_latent.astype(jnp.int32), place]).astype(jnp.int32)
    perm = permutation(long_latent)
    perm_back = perm.T
    order = pair_order()
    embedded = timestep_code(timesteps, D) + class_table[:, labels].astype(F32).T
    cond_low = jax.nn.silu(embedded).astype(BF16)
    modulation = jnp.dot(cond_low, modulator, preferred_element_type=F32).reshape(-1, 6, D)
    mod = jnp.pad(modulation, ((0, 0), (0, 2), (0, 0)))

    x, mixed, base, shifted, q, kv = front(
        scal, tokens, edge, perm, edge_permutation(), mod, mix_taps, order, heads_in
    )
    kv_far_other = swap(kv)
    q_other, kv_other = project(mixed, order, hin_other)
    kv_far = swap(kv_other)
    attended_other, logs_other = attention(scal, q_other, kv_other, kv_far_other)
    attended, logs = attention(scal, q, kv, kv_far)
    attn, norm, cot, grad_ffn = middle(x, attended, attended_other, cotangent, perm, mod, heads_out, hout_other)
    norm_edge, grad_edge = swap((boundary(norm), boundary(grad_ffn)))
    ffn, back_norm, up_grad, up_grad_other, down_grad, down_grad_other, taps_grad = feed_forward(
        scal, taps_own, taps_other, norm, norm_edge, grad_ffn, grad_edge, up_weight, up_other, down_weight, down_other
    )

    output, grad_residual, grad_attended, grad_attended_other, sums_two, hout_grad, hout_grad_other = turn(
        x, attn, ffn, cot, back_norm, attended, attended_other, perm_back, mod, heads_out, hout_other
    )
    rows = D // wide_count
    half = FF // 2
    up_sum = up_grad.astype(F32) + swap(up_grad_other).astype(F32)
    down_sum = down_grad.astype(F32) + swap(down_grad_other).astype(F32)
    hout_sum = hout_grad.astype(F32) + swap(hout_grad_other).astype(F32)
    tap_half = taps_grad.shape[0] // 2
    taps_sum = taps_grad[:tap_half, :9] + swap(taps_grad[tap_half:, :9])
    tap_part = taps_sum.transpose(0, 2, 1).reshape(wide_count, -1)
    tap_part = jnp.pad(tap_part, ((0, 0), (0, -tap_part.shape[1] % D)))
    grads = jnp.concatenate(
        [
            up_sum.reshape(2, wide_count, rows, D).transpose(1, 0, 2, 3).reshape(wide_count, 2 * rows, D),
            down_sum.reshape(wide_count, -1, D),
            hout_sum.reshape(wide_count, -1, D),
            tap_part.reshape(wide_count, -1, D),
        ],
        axis=1,
    )
    pad = -grads.shape[1] % 16
    grads = jnp.pad(grads, ((0, 0), (0, pad), (0, 0))).astype(BF16)
    grads, grad_attended_other = lax.optimization_barrier((grads, grad_attended_other))
    mine = lax.psum_scatter(grads, "wide", scatter_dimension=0, tiled=False)

    gq_other, gkv_other, gkv_far_other = attention_back(
        scal, q_other, kv_other, kv_far_other, attended_other, grad_attended_other, logs_other
    )
    gkv_add = swap(gkv_far_other)
    gq, gkv, gkv_far = attention_back(scal, q, kv, kv_far, attended, grad_attended, logs)
    gkv_add_other = swap(gkv_far)
    gmixed, hin_grad, hin_grad_other = project_back(
        (gq, gkv, gkv_add), (gq_other, gkv_other, gkv_add_other), mixed, order, heads_in, hin_other
    )
    gmixed_edge = swap(boundary(gmixed))
    input_grad, sums_one, mix_grad = back(
        scal, x, gmixed, gmixed_edge, base, shifted, grad_residual, perm_back, mod, mix_taps
    )

    modulation_two_grad = sums_two[:, 1:3].reshape(-1, 2 * D)
    own = D // cells
    mix_parts = mix_grad[:9].T.reshape(wide_count, 2, 1, own * 9).transpose(1, 0, 2, 3).astype(BF16)
    mix_parts = jnp.pad(mix_parts, ((0, 0), (0, 0), (0, 15), (0, -own * 9 % 128)))
    mix_own = jnp.where(place == 0, mix_parts[0], mix_parts[1])
    mix_other = jnp.where(place == 0, mix_parts[1], mix_parts[0])

    def by_chip(grad):
        split = grad.reshape(wide_count, rows, -1)
        return jnp.pad(split, ((0, 0), (0, -rows % 16), (0, 0)))

    slope = jax.vjp(jax.nn.silu, embedded)[1](jnp.ones_like(embedded))[0]
    blocks = jnp.concatenate([sums_one[:, 0:2], sums_two[:, 0:4]], axis=1).transpose(1, 0, 2).reshape(12, D)
    digits = jnp.stack([labels // 32, labels % 32], axis=1).astype(F32)
    digits = jnp.pad(digits, ((0, 14), (0, 126)))
    sent = jnp.concatenate([jnp.concatenate([blocks, cond_low.astype(F32), slope], axis=0), digits], axis=1)
    (hin_mine, mix_mine), everyone = reduce_gather(
        [by_chip(hin_grad), mix_own], [by_chip(hin_grad_other), mix_other], sent.astype(BF16)
    )
    row = jnp.arange(16, dtype=jnp.int32)
    block_row = 2 * jnp.arange(6, dtype=jnp.int32)[:, None] + jnp.arange(2, dtype=jnp.int32)
    picks = (block_row[:, :, None] == row).astype(F32)
    columns = lax.dynamic_slice_in_dim(everyone[:, 12:], cell * own, own, 2).astype(F32)
    all_cond, all_slope = columns[:, :2], columns[:, 2:]
    flat = everyone.reshape(cells * 16, -1)
    left = jnp.einsum("cfd,kfr->kdcr", all_cond, picks).astype(BF16).reshape(6 * own, cells * 16)
    modulator_mine = jnp.dot(left, flat, preferred_element_type=F32)[:, :D]
    modulator_mine = modulator_mine.reshape(6, own, D).transpose(1, 0, 2).reshape(own, 6 * D)
    modulator_rows = lax.dynamic_slice_in_dim(modulator, cell * own, own, 0).reshape(own, 6, D)
    modulator_rows = modulator_rows.transpose(1, 0, 2).reshape(6 * own, D)
    products = lax.dot_general(
        flat[:, :D], modulator_rows, (((1,), (1,)), ((), ())), preferred_element_type=F32
    ).reshape(cells, 16, 6, own)
    all_embedded = all_slope * jnp.stack(
        [sum(products[:, 2 * block + frame, block] for block in range(6)) for frame in range(2)], axis=1
    )
    all_digits = everyone[:, :2, D : D + 2].astype(jnp.int32)
    all_labels = (all_digits[..., 0] * 32 + all_digits[..., 1])[..., None]
    chosen = (all_labels == jnp.arange(class_table.shape[1], dtype=jnp.int32)).astype(F32)
    class_mine = jnp.dot(
        all_embedded.reshape(cells * 2, own).T, chosen.reshape(cells * 2, -1),
        precision=lax.Precision.HIGHEST, preferred_element_type=F32,
    )
    mix_mine = mix_mine[0, : own * 9].reshape(own, 9).T
    hin_mine = hin_mine[:rows]

    shared = 2 * rows + half // wide_count + rows // 2
    hidden = half // wide_count
    taps_mine = mine[shared:].reshape(-1)[: hidden * 9].reshape(hidden, 9).T.astype(F32)
    shards = (modulator_mine, class_mine, mix_mine, hin_mine, taps_mine)
    square = square_sum(wide_count, (*shards[:4], mine))
    grad_norm = jnp.sqrt(square[0, 0])
    order = (0, 1, 2, 3, 6, 4, 5, 7)
    step_rates = (
        D ** (-0.5), 1.0, 1.0 / 3.0, D ** (-0.5), 1.0 / 3.0, (D // 32) ** (-0.5), D ** (-0.5), FF ** (-0.5),
    )
    turned = (2, 6)
    given = [tuple(array.T for array in states[i]) if i in turned else states[i] for i in order]
    updated = adamw(square, mine, shards, given, step_rates)
    flat = [None] * 32
    for at, i in enumerate(order):
        for j in range(4):
            array = updated[4 * at + j]
            flat[4 * i + j] = array.T if i in turned else array
    return (output, input_grad, grad_norm, *flat, modulation_two_grad)


def solution(mesh):
    both = P(("wide", "narrow"), None)
    turned = P(("narrow", "wide"), None)
    grid = P("wide", "narrow")
    places = (both, both, both, grid, turned, grid, turned, turned)
    in_specs = (
        both, both, P("wide"), P(("wide", "narrow")), P(("wide", "narrow")),
        P(), P(), P(), P(None, "narrow"), P("narrow", None), P(None, "narrow"), P("narrow", None), P("narrow", None),
        *[place for place in places for _ in range(3)],
    )
    out_specs = (both, both, P(), *[place for place in places for _ in range(4)], both)
    return jax.shard_map(per_device, mesh=mesh, in_specs=in_specs, out_specs=out_specs, check_vma=False)
```
